32 devices in a mesh: dp: 4 (over y, core), ctx: 8 (over z, x).
Axes of the slice: x: 2, y: 2, z: 4, core: 2. Of those that a mesh axis runs over, the one named last changes fastest.
Arguments:
- tokens: bfloat16 [8, 1024, 768], P('dp', 'ctx'), may hold values from -6 to 6
- ln1_gain: bfloat16 [768], P(('dp', 'ctx')), may hold values from 0.5 to 1.5
- ln1_bias: bfloat16 [768], P(('dp', 'ctx')), may hold values from -1.5 to 1.5
- w_qkv: bfloat16 [768, 2304], P(('dp', 'ctx')), may hold values from -0.3125 to 0.3125
- b_qv: bfloat16 [1536], P(('dp', 'ctx')), may hold values from -1.5 to 1.5
- w_proj: bfloat16 [768, 768], P(('dp', 'ctx')), may hold values from -1.75 to 1.75
- b_proj: bfloat16 [768], P(('dp', 'ctx')), may hold values from -4 to 4
- ln2_gain: bfloat16 [768], P(('dp', 'ctx')), may hold values from 0.5 to 1.5
- ln2_bias: bfloat16 [768], P(('dp', 'ctx')), may hold values from -1.5 to 1.5
- w_fc: bfloat16 [768, 3072], P(('dp', 'ctx')), may hold values from -0.21875 to 0.21875
- b_fc: bfloat16 [3072], P(('dp', 'ctx')), may hold values from -1.5 to 1.5
- w_out: bfloat16 [3072, 768], P(('dp', 'ctx')), may hold values from -0.109375 to 0.109375
- b_out: bfloat16 [768], P(('dp', 'ctx')), may hold values from -4 to 4
- cotangent: bfloat16 [8, 1024, 768], P('dp', 'ctx'), may hold values from -6 to 6
Outputs:
- block_out: bfloat16 [8, 1024, 768], P('dp', 'ctx')
- grad_tokens: float32 [8, 1024, 768], P('dp', 'ctx')
- grad_ln1_gain: float32 [768], P(('dp', 'ctx'))
- grad_ln1_bias: float32 [768], P(('dp', 'ctx'))
- grad_w_qkv: float32 [768, 2304], P(('dp', 'ctx'))
- grad_b_qv: float32 [1536], P(('dp', 'ctx'))
- grad_w_proj: float32 [768, 768], P(('dp', 'ctx'))
- grad_b_proj: float32 [768], P(('dp', 'ctx'))
- grad_ln2_gain: float32 [768], P(('dp', 'ctx'))
- grad_ln2_bias: float32 [768], P(('dp', 'ctx'))
- grad_w_fc: float32 [768, 3072], P(('dp', 'ctx'))
- grad_b_fc: float32 [3072], P(('dp', 'ctx'))
- grad_w_out: float32 [3072, 768], P(('dp', 'ctx'))
- grad_b_out: float32 [768], P(('dp', 'ctx'))
The draws below stay inside these ranges and needn't reach their ends.
All inputs are finite; a program needn't handle non-finite values.
Results may differ from the reference program's by a relative error of at most 0.035.
Values may be sent and summed in bfloat16 or wider, within the bound.
No kernel may reach another device: no remote copies, remote signals or barrier semaphores. Data moves between devices by JAX's collectives and lax.ppermute only.
A program may use at most 192 MiB of HBM per device.

```python
import math
import jax
import jax.numpy as jnp
from jax import lax

D = 768
H = 12
HD = 64
FF = 3072
LEN = 1024
SEQS = 8


def shard_levels(key, dims, split, least, top_value):
    def one(position, parts):
        draws = jax.random.uniform(jax.random.fold_in(jax.random.fold_in(key, 6), position), (parts,), jnp.float32, least / len(split), top_value / len(split))
        return jnp.repeat(jnp.exp(draws), dims[position] // parts).reshape((-1,) + (1,) * (len(dims) - position - 1))

    loudness = one(*split[0])
    for cut in split[1:]:
        loudness = loudness * one(*cut)
    return loudness


def bell_draw(key, shape, spread, bound, pieces=(), dtype=jnp.bfloat16):
    loudness = shard_levels(key, shape, pieces, -0.22, 0.18) if pieces else 1.0
    entries = jax.random.normal(key, shape, jnp.float32) * spread * loudness
    return jnp.minimum(jnp.maximum(entries, -bound), bound).astype(dtype)


def setup_inputs(seed: int = 0) -> dict:
    streams_of = jax.random.split(jax.random.key(seed), 15)
    return {
        "tokens": bell_draw(streams_of[0], (SEQS, LEN, D), 1.0, 6.0, ((0, 4), (1, 8))),
        "ln1_gain": jnp.clip(0.5 + 1.0 * jax.random.uniform(streams_of[1], (D,), jnp.float32) ** shard_levels(streams_of[1], (D,), ((0, 32),), -0.2, 0.2), 0.5, 1.5).astype(jnp.bfloat16),
        "ln1_bias": bell_draw(streams_of[2], (D,), 0.3, 1.5, ((0, 32),)),
        "w_qkv": bell_draw(streams_of[3], (D, 3 * D), (D // 2) ** -0.5, 0.3125, ((0, 32),)),
        "b_qv": bell_draw(streams_of[4], (2 * D,), 0.3, 1.5, ((0, 32),)),
        "w_proj": bell_draw(streams_of[5], (D, D), (D // 64) ** -0.5, 1.75, ((0, 32),)),
        "b_proj": bell_draw(streams_of[6], (D,), 1.0, 4.0, ((0, 32),)),
        "ln2_gain": jnp.clip(0.5 + 1.0 * jax.random.uniform(streams_of[7], (D,), jnp.float32) ** shard_levels(streams_of[7], (D,), ((0, 32),), -0.2, 0.2), 0.5, 1.5).astype(jnp.bfloat16),
        "ln2_bias": bell_draw(streams_of[8], (D,), 0.3, 1.5, ((0, 32),)),
        "w_fc": bell_draw(streams_of[9], (D, FF), D ** -0.5, 0.21875, ((0, 32),)),
        "b_fc": bell_draw(streams_of[10], (FF,), 0.3, 1.5, ((0, 32),)),
        "w_out": bell_draw(streams_of[11], (FF, D), FF ** -0.5, 0.109375, ((0, 32),)),
        "b_out": bell_draw(streams_of[12], (D,), 1.0, 4.0, ((0, 32),)),
        "cotangent": bell_draw(streams_of[13], (SEQS, LEN, D), 1.0, 6.0, ((0, 4), (1, 8))),
    }


EPS = 1e-05
NEG = -1e+30

@jax.custom_vjp
def low(v):
    return lax.optimization_barrier(v.astype(jnp.bfloat16)).astype(jnp.float32)

@jax.custom_vjp
def low_back(v):
    return v

def low_keep(v):
    return (low(v), None)

def low_pass(kept, grad):
    return (grad,)

def back_keep(v):
    return (v, None)

def back_low(kept, grad):
    return (low(grad),)
low.defvjp(low_keep, low_pass)
low_back.defvjp(back_keep, back_low)

def layer_norm(values, gain_vec, bias_vec):
    average = lax.optimization_barrier(jnp.mean(values, axis=-1, keepdims=True))
    centered = values - average
    variance = lax.optimization_barrier(jnp.mean(centered * centered, axis=-1, keepdims=True))
    return centered * lax.rsqrt(variance + EPS) * gain_vec + bias_vec

def product(left, right):
    return jnp.dot(left, right, precision=lax.Precision.HIGHEST, preferred_element_type=jnp.float32)

def block_forward(inputs, parameters):
    ln1_gain, ln1_bias, w_qkv, b_qv, w_proj, b_proj, ln2_gain, ln2_bias, w_fc, b_fc, w_out, b_out = parameters
    length = inputs.shape[0]
    factor = 1.0 / math.sqrt(HD)
    normed = low(layer_norm(inputs, ln1_gain, ln1_bias))
    bias_all = jnp.concatenate([b_qv[:D], jnp.zeros((D,), jnp.float32), b_qv[D:]])
    projected = low(low_back(product(normed, w_qkv) + bias_all))
    queries = projected[:, :D].reshape(length, H, HD)
    key_rows = projected[:, D:2 * D].reshape(length, H, HD)
    value_rows = projected[:, 2 * D:].reshape(length, H, HD)
    scores = jnp.einsum('qhd,khd->hqk', queries, key_rows, precision=lax.Precision.HIGHEST) * factor
    scores = low_back(scores)
    positions = jnp.arange(length)
    visible = positions[None, :] <= positions[:, None]
    scores = jnp.where(visible[None], scores, NEG)
    weights_soft = low(jax.nn.softmax(scores, axis=-1))
    attended = jnp.einsum('hqk,khd->qhd', weights_soft, value_rows, precision=lax.Precision.HIGHEST)
    merged = low(low_back(attended.reshape(length, D)))
    branch = low_back(product(merged, w_proj) + b_proj)
    middle = inputs + branch
    normed_two = low(layer_norm(middle, ln2_gain, ln2_bias))
    pre_act = low_back(product(normed_two, w_fc) + b_fc)
    activated = low(jax.nn.gelu(pre_act, approximate=True))
    feed_out = low_back(product(activated, w_out) + b_out)
    return middle + feed_out

def add_up(first, second):
    return first + second

def reference(tokens, ln1_gain, ln1_bias, w_qkv, b_qv, w_proj, b_proj, ln2_gain, ln2_bias, w_fc, b_fc, w_out, b_out, cotangent):
    parameters = tuple((item.astype(jnp.float32) for item in (ln1_gain, ln1_bias, w_qkv, b_qv, w_proj, b_proj, ln2_gain, ln2_bias, w_fc, b_fc, w_out, b_out)))

    def scan_step(totals, sequence_pair):
        seq_in, seq_grad = sequence_pair
        output_seq, pullback = jax.vjp(block_forward, seq_in.astype(jnp.float32), parameters)
        grad_seq, grad_params = pullback(seq_grad.astype(jnp.float32))
        totals = jax.tree.map(add_up, totals, grad_params)
        return (totals, (output_seq.astype(jnp.bfloat16), grad_seq))
    zero_sums = jax.tree.map(jnp.zeros_like, parameters)
    totals, (outputs, grad_inputs) = lax.scan(scan_step, zero_sums, (tokens, cotangent))
    return (outputs, grad_inputs, totals[0], totals[1], totals[2], totals[3], totals[4], totals[5], totals[6], totals[7], totals[8], totals[9], totals[10], totals[11])
```

```python
import functools
import math

import jax
import jax.numpy as jnp
from jax import lax
from jax.experimental import pallas as pl
from jax.experimental.pallas import tpu as pltpu
from jax.sharding import PartitionSpec as P

H = 12
HD = 64


EPS = 1e-05
NEG = -1e30


def layer_norm(values, gain_vec, bias_vec):
    average = jnp.mean(values, axis=-1, keepdims=True)
    centered = values - average
    variance = jnp.mean(centered * centered, axis=-1, keepdims=True)
    return centered * lax.rsqrt(variance + EPS) * gain_vec + bias_vec


def gelu_tanh(values):
    return jax.nn.gelu(values, approximate=True)


def outer_sum(left, right):
    return lax.dot_general(
        left, right, (((0,), (0,)), ((), ())), preferred_element_type=jnp.float32
    )


def back_through(grad_rows, weight_mat):
    return lax.dot_general(
        grad_rows, weight_mat, (((1,), (1,)), ((), ())), preferred_element_type=jnp.float32
    )


def split_heads(flat_rows):
    return flat_rows.reshape(flat_rows.shape[0], flat_rows.shape[1], H, HD)


def attend_block(query_rows, key_rows, value_rows, query_pos, key_pos, running):
    factor = 1.0 / math.sqrt(HD)
    scores = (
        jnp.einsum("sqhd,skhd->shqk", query_rows, key_rows, preferred_element_type=jnp.float32)
        * factor
    )
    visible = key_pos[None, :] <= query_pos[:, None]
    scores = jnp.where(visible, scores, NEG)
    run_max, run_sum, run_acc = running
    new_max = jnp.maximum(run_max, jnp.max(scores, axis=-1))
    weights = jnp.where(visible, jnp.exp(scores - new_max[..., None]), 0.0)
    new_sum = jnp.sum(weights, axis=-1)
    added = jnp.einsum(
        "shqk,skhd->shqd",
        weights.astype(jnp.bfloat16),
        value_rows,
        preferred_element_type=jnp.float32,
    )
    return (new_max, new_sum, added)


def attend_grad(
    query_rows, grad_heads, log_total, delta_rows, key_rows, value_rows, query_pos, key_pos
):
    factor = 1.0 / math.sqrt(HD)
    scores = (
        jnp.einsum("sqhd,skhd->shqk", query_rows, key_rows, preferred_element_type=jnp.float32)
        * factor
    )
    visible = key_pos[None, :] <= query_pos[:, None]
    probs = jnp.where(visible, jnp.exp(scores - log_total[..., None]), 0.0)
    grad_values = jnp.einsum(
        "shqk,sqhd->skhd",
        probs.astype(jnp.bfloat16),
        grad_heads,
        preferred_element_type=jnp.float32,
    )
    grad_probs = jnp.einsum(
        "sqhd,skhd->shqk", grad_heads, value_rows, preferred_element_type=jnp.float32
    )
    grad_scores = (probs * (grad_probs - delta_rows[..., None])).astype(jnp.bfloat16)
    grad_query = (
        jnp.einsum("shqk,skhd->sqhd", grad_scores, key_rows, preferred_element_type=jnp.float32)
        * factor
    )
    grad_keys = (
        jnp.einsum("shqk,sqhd->skhd", grad_scores, query_rows, preferred_element_type=jnp.float32)
        * factor
    )
    return (grad_query, grad_keys, grad_values)


def plain_body(
    tokens,
    ln1_gain,
    ln1_bias,
    w_qkv,
    b_qv,
    w_proj,
    b_proj,
    ln2_gain,
    ln2_bias,
    w_fc,
    b_fc,
    w_out,
    b_out,
    cotangent,
):
    gathered = (
        lax.all_gather(ln1_gain, ("dp", "ctx"), axis=0, tiled=True),
        lax.all_gather(ln1_bias, ("dp", "ctx"), axis=0, tiled=True),
        lax.all_gather(w_qkv, ("dp", "ctx"), axis=0, tiled=True),
        lax.all_gather(b_qv, ("dp", "ctx"), axis=0, tiled=True),
        lax.all_gather(w_proj, ("dp", "ctx"), axis=0, tiled=True),
        lax.all_gather(b_proj, ("dp", "ctx"), axis=0, tiled=True),
        lax.all_gather(ln2_gain, ("dp", "ctx"), axis=0, tiled=True),
        lax.all_gather(ln2_bias, ("dp", "ctx"), axis=0, tiled=True),
        lax.all_gather(w_fc, ("dp", "ctx"), axis=0, tiled=True),
        lax.all_gather(b_fc, ("dp", "ctx"), axis=0, tiled=True),
        lax.all_gather(w_out, ("dp", "ctx"), axis=0, tiled=True),
        lax.all_gather(b_out, ("dp", "ctx"), axis=0, tiled=True),
    )
    (
        gain_one,
        bias_one,
        qkv_weight,
        qkv_bias,
        proj_weight,
        proj_bias,
        gain_two,
        bias_two,
        fc_weight,
        fc_bias,
        out_weight,
        out_bias,
    ) = gathered
    count_seq, group_len, model_width = tokens.shape
    rows_total = count_seq * group_len
    query_pos = lax.axis_index("ctx") * group_len + jnp.arange(group_len, dtype=jnp.int32)
    inputs = tokens.astype(jnp.float32).reshape(rows_total, model_width)
    normed_one, pull_one = jax.vjp(
        layer_norm, inputs, gain_one.astype(jnp.float32), bias_one.astype(jnp.float32)
    )
    normed_low = normed_one.astype(jnp.bfloat16)
    qkv_bias32 = qkv_bias.astype(jnp.float32)
    bias_full = jnp.concatenate(
        [qkv_bias32[:model_width], jnp.zeros((model_width,), jnp.float32), qkv_bias32[model_width:]]
    )
    qkv_low = (
        jnp.dot(normed_low, qkv_weight, preferred_element_type=jnp.float32) + bias_full
    ).astype(jnp.bfloat16)
    query_flat = qkv_low[:, :model_width].reshape(count_seq, group_len, model_width)
    query_rows = split_heads(query_flat)
    key_value = qkv_low[:, model_width:].reshape(count_seq, group_len, 2 * model_width)
    initial = (
        jnp.full((count_seq, H, group_len), NEG, jnp.float32),
        jnp.zeros((count_seq, H, group_len), jnp.float32),
        jnp.zeros((count_seq, H, group_len, HD), jnp.float32),
    )
    remote = lax.all_gather(key_value, "ctx", axis=1, tiled=True)
    rows_here = remote.shape[1]
    key_pos = jnp.arange(rows_here, dtype=jnp.int32)
    key_rows = split_heads(remote[:, :, :model_width])
    value_rows = split_heads(remote[:, :, model_width:])
    run_max, run_sum, run_acc = attend_block(
        query_rows, key_rows, value_rows, query_pos, key_pos, initial
    )
    attended = run_acc / run_sum[..., None]
    log_total = run_max + jnp.log(run_sum)
    merged_low = (
        attended.transpose(0, 2, 1, 3).reshape(rows_total, model_width).astype(jnp.bfloat16)
    )
    middle = (
        inputs
        + jnp.dot(merged_low, proj_weight, preferred_element_type=jnp.float32)
        + proj_bias.astype(jnp.float32)
    )
    normed_two, pull_two = jax.vjp(
        layer_norm, middle, gain_two.astype(jnp.float32), bias_two.astype(jnp.float32)
    )
    normed_two_low = normed_two.astype(jnp.bfloat16)
    pre_act = jnp.dot(
        normed_two_low, fc_weight, preferred_element_type=jnp.float32
    ) + fc_bias.astype(jnp.float32)
    activated, gelu_pull = jax.vjp(gelu_tanh, pre_act)
    activated_low = activated.astype(jnp.bfloat16)
    feed_out = jnp.dot(
        activated_low, out_weight, preferred_element_type=jnp.float32
    ) + out_bias.astype(jnp.float32)
    result = (middle + feed_out).astype(jnp.bfloat16).reshape(count_seq, group_len, model_width)
    regathered = (
        lax.all_gather(ln1_gain, ("dp", "ctx"), axis=0, tiled=True),
        lax.all_gather(ln1_bias, ("dp", "ctx"), axis=0, tiled=True),
        lax.all_gather(w_qkv, ("dp", "ctx"), axis=0, tiled=True),
        lax.all_gather(b_qv, ("dp", "ctx"), axis=0, tiled=True),
        lax.all_gather(w_proj, ("dp", "ctx"), axis=0, tiled=True),
        lax.all_gather(b_proj, ("dp", "ctx"), axis=0, tiled=True),
        lax.all_gather(ln2_gain, ("dp", "ctx"), axis=0, tiled=True),
        lax.all_gather(ln2_bias, ("dp", "ctx"), axis=0, tiled=True),
        lax.all_gather(w_fc, ("dp", "ctx"), axis=0, tiled=True),
        lax.all_gather(b_fc, ("dp", "ctx"), axis=0, tiled=True),
        lax.all_gather(w_out, ("dp", "ctx"), axis=0, tiled=True),
        lax.all_gather(b_out, ("dp", "ctx"), axis=0, tiled=True),
    )
    qkv_weight = regathered[2]
    proj_weight = regathered[4]
    fc_weight = regathered[8]
    out_weight = regathered[10]
    grad_top = cotangent.reshape(rows_total, model_width)
    grad_top32 = grad_top.astype(jnp.float32)
    grad_out_bias = jnp.sum(grad_top32, axis=0)
    grad_out_weight = outer_sum(activated_low, grad_top)
    grad_act = back_through(grad_top, out_weight)
    grad_pre = gelu_pull(grad_act)[0].astype(jnp.bfloat16)
    grad_fc_bias = jnp.sum(grad_pre.astype(jnp.float32), axis=0)
    grad_fc_weight = outer_sum(normed_two_low, grad_pre)
    grad_normed_two = back_through(grad_pre, fc_weight)
    grad_middle_ln, grad_gain_two, grad_bias_two = pull_two(grad_normed_two)
    grad_middle = grad_top32 + grad_middle_ln
    grad_branch = grad_middle.astype(jnp.bfloat16)
    grad_proj_bias = jnp.sum(grad_branch.astype(jnp.float32), axis=0)
    grad_proj_weight = outer_sum(merged_low, grad_branch)
    grad_merged = back_through(grad_branch, proj_weight).astype(jnp.bfloat16)
    grad_flat = grad_merged.reshape(count_seq, group_len, model_width)
    grad_heads = split_heads(grad_flat)
    delta_rows = jnp.einsum("sqhd,shqd->shq", grad_heads.astype(jnp.float32), attended)
    remote = lax.all_gather(key_value, "ctx", axis=1, tiled=True)
    rows_here = remote.shape[1]
    key_pos = jnp.arange(rows_here, dtype=jnp.int32)
    part_query, part_keys, part_values = attend_grad(
        query_rows,
        grad_heads,
        log_total,
        delta_rows,
        split_heads(remote[:, :, :model_width]),
        split_heads(remote[:, :, model_width:]),
        query_pos,
        key_pos,
    )
    joined = jnp.concatenate(
        [
            part_keys.reshape(count_seq, rows_here, model_width),
            part_values.reshape(count_seq, rows_here, model_width),
        ],
        axis=2,
    )
    grad_kv_all = joined
    grad_query, grad_kv_all = (part_query, grad_kv_all)
    grad_kv = lax.psum_scatter(
        grad_kv_all.astype(jnp.bfloat16), "ctx", scatter_dimension=1, tiled=True
    ).astype(jnp.float32)
    grad_query_flat = grad_query.reshape(count_seq, group_len, model_width)
    grad_qkv = jnp.concatenate(
        [
            grad_query_flat.reshape(rows_total, model_width),
            grad_kv.reshape(rows_total, 2 * model_width),
        ],
        axis=1,
    ).astype(jnp.bfloat16)
    column_sums = jnp.sum(grad_qkv.astype(jnp.float32), axis=0)
    grad_qkv_bias = jnp.concatenate([column_sums[:model_width], column_sums[2 * model_width :]])
    grad_qkv_weight = outer_sum(normed_low, grad_qkv)
    grad_normed_one = back_through(grad_qkv, qkv_weight)
    grad_input_ln, grad_gain_one, grad_bias_one = pull_one(grad_normed_one)
    grad_input = (grad_middle + grad_input_ln).reshape(count_seq, group_len, model_width)
    gradients = (
        lax.psum_scatter(grad_gain_one, ("dp", "ctx"), scatter_dimension=0, tiled=True),
        lax.psum_scatter(grad_bias_one, ("dp", "ctx"), scatter_dimension=0, tiled=True),
        lax.psum_scatter(grad_qkv_weight, ("dp", "ctx"), scatter_dimension=0, tiled=True),
        lax.psum_scatter(grad_qkv_bias, ("dp", "ctx"), scatter_dimension=0, tiled=True),
        lax.psum_scatter(grad_proj_weight, ("dp", "ctx"), scatter_dimension=0, tiled=True),
        lax.psum_scatter(grad_proj_bias, ("dp", "ctx"), scatter_dimension=0, tiled=True),
        lax.psum_scatter(grad_gain_two, ("dp", "ctx"), scatter_dimension=0, tiled=True),
        lax.psum_scatter(grad_bias_two, ("dp", "ctx"), scatter_dimension=0, tiled=True),
        lax.psum_scatter(grad_fc_weight, ("dp", "ctx"), scatter_dimension=0, tiled=True),
        lax.psum_scatter(grad_fc_bias, ("dp", "ctx"), scatter_dimension=0, tiled=True),
        lax.psum_scatter(grad_out_weight, ("dp", "ctx"), scatter_dimension=0, tiled=True),
        lax.psum_scatter(grad_out_bias, ("dp", "ctx"), scatter_dimension=0, tiled=True),
    )
    return (result, grad_input) + tuple(gradients)


def axis_bits(axis):
    size = lax.axis_size(axis)
    return [(axis, 1 << k) for k in reversed(range(size.bit_length() - 1))]


def swap(values, bit):
    axis, mask = bit
    return lax.ppermute(values, axis, [(i, i ^ mask) for i in range(lax.axis_size(axis))])


def bit_value(bit):
    axis, mask = bit
    return (lax.axis_index(axis) // mask) % 2


def in_order(mine, other, bit, dim):
    upper = bit_value(bit) == 1
    return jnp.stack([jnp.where(upper, other, mine), jnp.where(upper, mine, other)], axis=dim)


def gather_bit(values, bit, dim):
    return in_order(values, swap(values, bit), bit, dim)


def take(values, index, dim):
    return lax.dynamic_index_in_dim(values, index, dim, keepdims=False)


def scatter_bit(values, bit, dim):
    here = bit_value(bit)
    sent = swap(take(values, 1 - here, dim), bit)
    kept = take(values, here, dim).astype(jnp.float32)
    return (kept + sent.astype(jnp.float32)).astype(values.dtype)


def trade_bit(values, bit, dim):
    here = bit_value(bit)
    return in_order(take(values, here, dim), swap(take(values, 1 - here, dim), bit), bit, dim)


def gather_rows(shard, order, bits):
    held = []
    values = shard
    for bit in order:
        held = sorted(held + [bit], key=bits.index)
        values = gather_bit(values, bit, held.index(bit))
    return values.reshape((-1,) + shard.shape[1:])


def scatter_rows(values, order, bits):
    count = 1 << len(bits)
    values = values.reshape((2,) * len(bits) + (values.shape[0] // count,) + values.shape[1:])
    left = list(bits)
    for bit in order:
        values = scatter_bit(values, bit, left.index(bit))
        left.remove(bit)
    return values


def turned(items, steps):
    steps = steps % max(len(items), 1)
    return items[steps:] + items[:steps]


def dot_last(left, right):
    return lax.dot_general(left, right, (((1,), (1,)), ((), ())), preferred_element_type=jnp.float32)


def dot_first(left, right):
    return lax.dot_general(left, right, (((0,), (0,)), ((), ())), preferred_element_type=jnp.float32)


def seen_scores(keys, queries, start):
    scores = dot_last(keys, queries)
    key_pos = lax.broadcasted_iota(jnp.int32, scores.shape, 0)
    query_pos = lax.broadcasted_iota(jnp.int32, scores.shape, 1) + start
    return jnp.where(key_pos <= query_pos, scores, NEG)


def attend_kernel(heads, block, qkv_ref, out_ref):
    wide = heads * HD
    for head in range(heads):
        at = head * HD
        for low in range(0, qkv_ref.shape[0], block):
            high = low + block
            queries = qkv_ref[low:high, at : at + HD] * (1.0 / math.sqrt(HD))
            keys = qkv_ref[:high, wide + at : wide + at + HD]
            values = qkv_ref[:high, 2 * wide + at : 2 * wide + at + HD]
            scores = seen_scores(keys, queries, low)
            weights = jnp.exp(scores - jnp.max(scores, axis=0, keepdims=True))
            total = jnp.sum(weights, axis=0, keepdims=True)
            mixed = dot_first(values, weights.astype(jnp.bfloat16)) / total
            out_ref[low:high, at : at + HD] = mixed.T.astype(jnp.bfloat16)


def attend_grad_kernel(heads, block, qkv_ref, grad_ref, out_ref, keys_acc, values_acc):
    wide = heads * HD
    factor = 1.0 / math.sqrt(HD)
    for head in range(heads):
        at = head * HD
        keys_acc[...] = jnp.zeros_like(keys_acc)
        values_acc[...] = jnp.zeros_like(values_acc)
        for low in range(0, qkv_ref.shape[0], block):
            high = low + block
            queries = qkv_ref[low:high, at : at + HD] * factor
            keys = qkv_ref[:high, wide + at : wide + at + HD]
            values = qkv_ref[:high, 2 * wide + at : 2 * wide + at + HD]
            grads = grad_ref[low:high, at : at + HD]
            scores = seen_scores(keys, queries, low)
            weights = jnp.exp(scores - jnp.max(scores, axis=0, keepdims=True))
            probs = weights / jnp.sum(weights, axis=0, keepdims=True)
            grad_probs = dot_last(values, grads)
            delta = jnp.sum(probs * grad_probs, axis=0, keepdims=True)
            grad_scores = (probs * (grad_probs - delta)).astype(jnp.bfloat16)
            values_acc[:high] += jnp.dot(
                probs.astype(jnp.bfloat16), grads, preferred_element_type=jnp.float32
            )
            keys_acc[:high] += jnp.dot(grad_scores, queries, preferred_element_type=jnp.float32)
            grad_queries = dot_first(keys, grad_scores) * factor
            out_ref[low:high, at : at + HD] = grad_queries.T.astype(jnp.bfloat16)
        out_ref[:, wide + at : wide + at + HD] = keys_acc[...].astype(jnp.bfloat16)
        out_ref[:, 2 * wide + at : 2 * wide + at + HD] = values_acc[...].astype(jnp.bfloat16)


VMEM_LIMIT = 48 * 1024 * 1024


def attend(qkv, heads):
    rows = qkv.shape[0]
    return pl.pallas_call(
        functools.partial(attend_kernel, heads, min(rows, 256)),
        out_shape=jax.ShapeDtypeStruct((rows, heads * HD), jnp.bfloat16),
        compiler_params=pltpu.CompilerParams(vmem_limit_bytes=VMEM_LIMIT),
        name="attend",
    )(qkv)


def attend_back(qkv, grads, heads):
    rows = qkv.shape[0]
    return pl.pallas_call(
        functools.partial(attend_grad_kernel, heads, min(rows, 256)),
        out_shape=jax.ShapeDtypeStruct(qkv.shape, jnp.bfloat16),
        scratch_shapes=[pltpu.VMEM((rows, HD), jnp.float32), pltpu.VMEM((rows, HD), jnp.float32)],
        compiler_params=pltpu.CompilerParams(vmem_limit_bytes=VMEM_LIMIT),
        name="attend_back",
    )(qkv, grads)


def normalize(values):
    average = jnp.mean(values, axis=-1, keepdims=True)
    centered = values - average
    variance = jnp.mean(centered * centered, axis=-1, keepdims=True)
    scale = lax.rsqrt(variance + EPS)
    return centered * scale, scale


def normalize_back(grad_normed, gain, unit, scale):
    inner = grad_normed * gain
    return scale * (
        inner
        - jnp.mean(inner, axis=-1, keepdims=True)
        - unit * jnp.mean(inner * unit, axis=-1, keepdims=True)
    )


def split_body(
    tokens,
    ln1_gain,
    ln1_bias,
    w_qkv,
    b_qv,
    w_proj,
    b_proj,
    ln2_gain,
    ln2_bias,
    w_fc,
    b_fc,
    w_out,
    b_out,
    cotangent,
):
    f32, bf16 = jnp.float32, jnp.bfloat16
    count_seq, group_len, model_width = tokens.shape
    rows_total = count_seq * group_len
    dp_bits, ctx_bits = axis_bits("dp"), axis_bits("ctx")
    bits = dp_bits + ctx_bits
    seq_bit, team_bits = ctx_bits[0], ctx_bits[1:]
    ctx_size = lax.axis_size("ctx")
    devices = ctx_size * lax.axis_size("dp")
    team = 1 << len(team_bits)
    heads = H // team
    wide = heads * HD
    sequence = bit_value(seq_bit)
    member = lax.axis_index("ctx") % team
    near, far = dp_bits[-1], seq_bit
    middle = [bit for bit in turned(team_bits, 1) + dp_bits[:-1]]

    def gather_order(turn):
        return [far] + turned(middle, turn) + [near]

    def scatter_order(turn):
        return [near] + turned(middle, turn) + [far]

    mine = take(tokens, sequence, 0)
    theirs = swap(take(tokens, 1 - sequence, 0), seq_bit)
    pair = in_order(mine, theirs, seq_bit, 0)
    half = model_width // 2
    sides = []
    for side, order in ((0, team_bits), (1, team_bits[::-1])):
        held = []
        part = pair[..., side * half : (side + 1) * half]
        for bit in order:
            held = sorted(held + [bit], key=team_bits.index)
            part = gather_bit(part, bit, 1 + held.index(bit))
        sides.append(part.reshape(ctx_size * group_len, half))
    long_tokens = jnp.concatenate(sides, axis=1)

    vectors = (ln1_gain, ln1_bias, b_qv, b_proj, ln2_gain, ln2_bias, b_fc, b_out)
    sizes = [vector.shape[0] for vector in vectors]
    starts = [sum(sizes[:k]) for k in range(len(sizes))]
    packed = jnp.concatenate(vectors)[None, :]
    all_vectors = gather_rows(packed, bits[::-1], bits).astype(f32)
    (gain_one, bias_one, qv_bias, proj_bias, gain_two, bias_two, fc_bias, out_bias) = (
        all_vectors[:, start : start + size].reshape(devices * size)
        for start, size in zip(starts, sizes)
    )
    rows_own = w_qkv.shape[0]
    columns = w_qkv.reshape(rows_own, 3, team, wide).transpose(2, 0, 1, 3)
    columns = columns.reshape((2,) * len(team_bits) + (rows_own, 3 * wide))
    for k in reversed(range(len(team_bits))):
        columns = trade_bit(columns, team_bits[k], k)
    for bit in [seq_bit] + dp_bits[::-1]:
        columns = gather_bit(columns, bit, 0)
    qkv_weight = columns.reshape(devices * rows_own, 3 * wide)

    proj_weight = gather_rows(w_proj, gather_order(0), bits)
    fc_weight = gather_rows(w_fc, gather_order(1), bits)
    out_weight = gather_rows(w_out, gather_order(2), bits)

    unit_long, _ = normalize(long_tokens.astype(f32))
    normed_long = (unit_long * gain_one + bias_one).astype(bf16)
    team_bias = take(qv_bias.reshape(2, team, wide), member, 1)
    bias_row = jnp.concatenate([team_bias[0], jnp.zeros((wide,), f32), team_bias[1]])
    qkv = (jnp.dot(normed_long, qkv_weight, preferred_element_type=f32) + bias_row).astype(bf16)
    attended = attend(qkv, heads)

    def to_rows(values):
        parts = lax.all_to_all(
            values.reshape(ctx_size, group_len, wide), "ctx", 0, 0, tiled=True
        )
        parts = parts.reshape(count_seq, team, group_len, wide).transpose(0, 2, 1, 3)
        return parts.reshape(rows_total, model_width)

    def to_heads(values):
        parts = values.reshape(count_seq, group_len, team, wide).transpose(0, 2, 1, 3)
        parts = parts.reshape(ctx_size, group_len, wide)
        return lax.all_to_all(parts, "ctx", 0, 0, tiled=True).reshape(ctx_size * group_len, wide)

    merged = to_rows(attended)

    inputs = tokens.astype(f32).reshape(rows_total, model_width)
    middle_rows = inputs + jnp.dot(merged, proj_weight, preferred_element_type=f32) + proj_bias
    unit_two, scale_two = normalize(middle_rows)
    normed_two = (unit_two * gain_two + bias_two).astype(bf16)
    pre_act = jnp.dot(normed_two, fc_weight, preferred_element_type=f32) + fc_bias
    activated32, gelu_pull = jax.vjp(gelu_tanh, pre_act)
    activated = activated32.astype(bf16)
    result = middle_rows + jnp.dot(activated, out_weight, preferred_element_type=f32) + out_bias
    result = result.astype(bf16).reshape(tokens.shape)

    grad_top = cotangent.reshape(rows_total, model_width)
    grad_top32 = grad_top.astype(f32)
    grad_out_bias = jnp.sum(grad_top32, axis=0)
    grad_out_weight = scatter_rows(outer_sum(activated, grad_top).astype(bf16), scatter_order(0), bits)
    grad_pre = gelu_pull(back_through(grad_top, out_weight))[0].astype(bf16)
    grad_fc_bias = jnp.sum(grad_pre.astype(f32), axis=0)
    grad_fc_weight = scatter_rows(outer_sum(normed_two, grad_pre).astype(bf16), scatter_order(1), bits)
    grad_normed_two = back_through(grad_pre, fc_weight)
    grad_gain_two = jnp.sum(grad_normed_two * unit_two, axis=0)
    grad_bias_two = jnp.sum(grad_normed_two, axis=0)
    grad_middle = grad_top32 + normalize_back(grad_normed_two, gain_two, unit_two, scale_two)
    grad_branch = grad_middle.astype(bf16)
    grad_proj_bias = jnp.sum(grad_branch.astype(f32), axis=0)
    grad_proj_weight = scatter_rows(outer_sum(merged, grad_branch).astype(bf16), scatter_order(2), bits)
    grad_heads = to_heads(back_through(grad_branch, proj_weight).astype(bf16))
    grad_qkv = attend_back(qkv, grad_heads, heads)

    grad_long = back_through(grad_qkv, qkv_weight)
    grad_gain_one = jnp.sum(grad_long * unit_long, axis=0)
    grad_bias_one = jnp.sum(grad_long, axis=0)
    blocks = grad_long.astype(bf16).reshape(
        (2,) * len(ctx_bits) + (group_len, model_width)
    )
    sides = []
    for side, order in ((0, team_bits), (1, team_bits[::-1])):
        left = list(team_bits)
        part = blocks[..., side * half : (side + 1) * half]
        for bit in order:
            part = scatter_bit(part, bit, 1 + left.index(bit))
            left.remove(bit)
        sides.append(part)
    part = jnp.concatenate(sides, axis=-1)
    grad_normed_one = trade_bit(part, seq_bit, 0).astype(f32)
    unit_one, scale_one = normalize(tokens.astype(f32))
    grad_input = grad_middle.reshape(tokens.shape) + normalize_back(
        grad_normed_one, gain_one, unit_one, scale_one
    )

    parts = outer_sum(normed_long, grad_qkv).astype(bf16)
    parts = parts.reshape((2,) * len(bits) + (rows_own, 3 * wide))
    left = list(bits)
    for bit in dp_bits[::-1] + [seq_bit]:
        parts = scatter_bit(parts, bit, left.index(bit))
        left.remove(bit)
    for k in range(len(team_bits)):
        parts = trade_bit(parts, team_bits[k], k)
    grad_qkv_weight = (
        parts.reshape(team, rows_own, 3, wide).transpose(1, 2, 0, 3).reshape(w_qkv.shape).astype(f32)
    )

    sums = jnp.sum(grad_qkv.astype(f32), axis=0).reshape(3, 1, wide)
    placed = lax.dynamic_update_index_in_dim(
        jnp.zeros((2, team, wide), f32), jnp.concatenate([sums[:1], sums[2:]]), member, 1
    )
    totals = (
        grad_gain_one,
        grad_bias_one,
        placed.reshape(2 * model_width),
        grad_proj_bias,
        grad_gain_two,
        grad_bias_two,
        grad_fc_bias,
        grad_out_bias,
    )
    spread = jnp.concatenate([total.reshape(devices, -1) for total in totals], axis=1)
    own = scatter_rows(spread, scatter_order(0), bits)[0]
    (g_gain_one, g_bias_one, g_qv, g_proj, g_gain_two, g_bias_two, g_fc, g_out) = (
        own[start : start + size] for start, size in zip(starts, sizes)
    )
    return (
        result,
        grad_input,
        g_gain_one,
        g_bias_one,
        grad_qkv_weight,
        g_qv,
        grad_proj_weight.astype(f32),
        g_proj,
        g_gain_two,
        g_bias_two,
        grad_fc_weight.astype(f32),
        g_fc,
        grad_out_weight.astype(f32),
        g_out,
    )


def body(tokens, *others):
    ctx_size, dp_size = lax.axis_size("ctx"), lax.axis_size("dp")
    powers = ctx_size & (ctx_size - 1) == 0 and dp_size & (dp_size - 1) == 0
    if powers and dp_size > 1 and ctx_size > 2 and tokens.shape[0] == 2 and H % (ctx_size // 2) == 0:
        return split_body(tokens, *others)
    return plain_body(tokens, *others)


def solution(mesh):
    placed = (
        P("dp", "ctx", None),
        P(("dp", "ctx")),
        P(("dp", "ctx")),
        P(("dp", "ctx"), None),
        P(("dp", "ctx")),
        P(("dp", "ctx"), None),
        P(("dp", "ctx")),
        P(("dp", "ctx")),
        P(("dp", "ctx")),
        P(("dp", "ctx"), None),
        P(("dp", "ctx")),
        P(("dp", "ctx"), None),
        P(("dp", "ctx")),
        P("dp", "ctx", None),
    )
    return jax.shard_map(
        body,
        mesh=mesh,
        in_specs=placed,
        out_specs=(
            P("dp", "ctx", None),
            P("dp", "ctx", None),
            P(("dp", "ctx")),
            P(("dp", "ctx")),
            P(("dp", "ctx"), None),
            P(("dp", "ctx")),
            P(("dp", "ctx"), None),
            P(("dp", "ctx")),
            P(("dp", "ctx")),
            P(("dp", "ctx")),
            P(("dp", "ctx"), None),
            P(("dp", "ctx")),
            P(("dp", "ctx"), None),
            P(("dp", "ctx")),
        ),
        check_vma=False,
    )
```

```python
import functools
import math

import jax
import jax.numpy as jnp
from jax import lax
from jax.experimental import pallas as pl
from jax.experimental.pallas import tpu as pltpu
from jax.sharding import PartitionSpec as P

H = 12
HD = 64


EPS = 1e-05
NEG = -1e30


def layer_norm(values, gain_vec, bias_vec):
    average = jnp.mean(values, axis=-1, keepdims=True)
    centered = values - average
    variance = jnp.mean(centered * centered, axis=-1, keepdims=True)
    return centered * lax.rsqrt(variance + EPS) * gain_vec + bias_vec


def gelu_tanh(values):
    return jax.nn.gelu(values, approximate=True)


def outer_sum(left, right):
    return lax.dot_general(
        left, right, (((0,), (0,)), ((), ())), preferred_element_type=jnp.float32
    )


def back_through(grad_rows, weight_mat):
    return lax.dot_general(
        grad_rows, weight_mat, (((1,), (1,)), ((), ())), preferred_element_type=jnp.float32
    )


def split_heads(flat_rows):
    return flat_rows.reshape(flat_rows.shape[0], flat_rows.shape[1], H, HD)


def attend_block(query_rows, key_rows, value_rows, query_pos, key_pos, running):
    factor = 1.0 / math.sqrt(HD)
    scores = (
        jnp.einsum("sqhd,skhd->shqk", query_rows, key_rows, preferred_element_type=jnp.float32)
        * factor
    )
    visible = key_pos[None, :] <= query_pos[:, None]
    scores = jnp.where(visible, scores, NEG)
    run_max, run_sum, run_acc = running
    new_max = jnp.maximum(run_max, jnp.max(scores, axis=-1))
    weights = jnp.where(visible, jnp.exp(scores - new_max[..., None]), 0.0)
    new_sum = jnp.sum(weights, axis=-1)
    added = jnp.einsum(
        "shqk,skhd->shqd",
        weights.astype(jnp.bfloat16),
        value_rows,
        preferred_element_type=jnp.float32,
    )
    return (new_max, new_sum, added)


def attend_grad(
    query_rows, grad_heads, log_total, delta_rows, key_rows, value_rows, query_pos, key_pos
):
    factor = 1.0 / math.sqrt(HD)
    scores = (
        jnp.einsum("sqhd,skhd->shqk", query_rows, key_rows, preferred_element_type=jnp.float32)
        * factor
    )
    visible = key_pos[None, :] <= query_pos[:, None]
    probs = jnp.where(visible, jnp.exp(scores - log_total[..., None]), 0.0)
    grad_values = jnp.einsum(
        "shqk,sqhd->skhd",
        probs.astype(jnp.bfloat16),
        grad_heads,
        preferred_element_type=jnp.float32,
    )
    grad_probs = jnp.einsum(
        "sqhd,skhd->shqk", grad_heads, value_rows, preferred_element_type=jnp.float32
    )
    grad_scores = (probs * (grad_probs - delta_rows[..., None])).astype(jnp.bfloat16)
    grad_query = (
        jnp.einsum("shqk,skhd->sqhd", grad_scores, key_rows, preferred_element_type=jnp.float32)
        * factor
    )
    grad_keys = (
        jnp.einsum("shqk,sqhd->skhd", grad_scores, query_rows, preferred_element_type=jnp.float32)
        * factor
    )
    return (grad_query, grad_keys, grad_values)


def plain_body(
    tokens,
    ln1_gain,
    ln1_bias,
    w_qkv,
    b_qv,
    w_proj,
    b_proj,
    ln2_gain,
    ln2_bias,
    w_fc,
    b_fc,
    w_out,
    b_out,
    cotangent,
):
    gathered = (
        lax.all_gather(ln1_gain, ("dp", "ctx"), axis=0, tiled=True),
        lax.all_gather(ln1_bias, ("dp", "ctx"), axis=0, tiled=True),
        lax.all_gather(w_qkv, ("dp", "ctx"), axis=0, tiled=True),
        lax.all_gather(b_qv, ("dp", "ctx"), axis=0, tiled=True),
        lax.all_gather(w_proj, ("dp", "ctx"), axis=0, tiled=True),
        lax.all_gather(b_proj, ("dp", "ctx"), axis=0, tiled=True),
        lax.all_gather(ln2_gain, ("dp", "ctx"), axis=0, tiled=True),
        lax.all_gather(ln2_bias, ("dp", "ctx"), axis=0, tiled=True),
        lax.all_gather(w_fc, ("dp", "ctx"), axis=0, tiled=True),
        lax.all_gather(b_fc, ("dp", "ctx"), axis=0, tiled=True),
        lax.all_gather(w_out, ("dp", "ctx"), axis=0, tiled=True),
        lax.all_gather(b_out, ("dp", "ctx"), axis=0, tiled=True),
    )
    (
        gain_one,
        bias_one,
        qkv_weight,
        qkv_bias,
        proj_weight,
        proj_bias,
        gain_two,
        bias_two,
        fc_weight,
        fc_bias,
        out_weight,
        out_bias,
    ) = gathered
    count_seq, group_len, model_width = tokens.shape
    rows_total = count_seq * group_len
    query_pos = lax.axis_index("ctx") * group_len + jnp.arange(group_len, dtype=jnp.int32)
    inputs = tokens.astype(jnp.float32).reshape(rows_total, model_width)
    normed_one, pull_one = jax.vjp(
        layer_norm, inputs, gain_one.astype(jnp.float32), bias_one.astype(jnp.float32)
    )
    normed_low = normed_one.astype(jnp.bfloat16)
    qkv_bias32 = qkv_bias.astype(jnp.float32)
    bias_full = jnp.concatenate(
        [qkv_bias32[:model_width], jnp.zeros((model_width,), jnp.float32), qkv_bias32[model_width:]]
    )
    qkv_low = (
        jnp.dot(normed_low, qkv_weight, preferred_element_type=jnp.float32) + bias_full
    ).astype(jnp.bfloat16)
    query_flat = qkv_low[:, :model_width].reshape(count_seq, group_len, model_width)
    query_rows = split_heads(query_flat)
    key_value = qkv_low[:, model_width:].reshape(count_seq, group_len, 2 * model_width)
    initial = (
        jnp.full((count_seq, H, group_len), NEG, jnp.float32),
        jnp.zeros((count_seq, H, group_len), jnp.float32),
        jnp.zeros((count_seq, H, group_len, HD), jnp.float32),
    )
    remote = lax.all_gather(key_value, "ctx", axis=1, tiled=True)
    rows_here = remote.shape[1]
    key_pos = jnp.arange(rows_here, dtype=jnp.int32)
    key_rows = split_heads(remote[:, :, :model_width])
    value_rows = split_heads(remote[:, :, model_width:])
    run_max, run_sum, run_acc = attend_block(
        query_rows, key_rows, value_rows, query_pos, key_pos, initial
    )
    attended = run_acc / run_sum[..., None]
    log_total = run_max + jnp.log(run_sum)
    merged_low = (
        attended.transpose(0, 2, 1, 3).reshape(rows_total, model_width).astype(jnp.bfloat16)
    )
    middle = (
        inputs
        + jnp.dot(merged_low, proj_weight, preferred_element_type=jnp.float32)
        + proj_bias.astype(jnp.float32)
    )
    normed_two, pull_two = jax.vjp(
        layer_norm, middle, gain_two.astype(jnp.float32), bias_two.astype(jnp.float32)
    )
    normed_two_low = normed_two.astype(jnp.bfloat16)
    pre_act = jnp.dot(
        normed_two_low, fc_weight, preferred_element_type=jnp.float32
    ) + fc_bias.astype(jnp.float32)
    activated, gelu_pull = jax.vjp(gelu_tanh, pre_act)
    activated_low = activated.astype(jnp.bfloat16)
    feed_out = jnp.dot(
        activated_low, out_weight, preferred_element_type=jnp.float32
    ) + out_bias.astype(jnp.float32)
    result = (middle + feed_out).astype(jnp.bfloat16).reshape(count_seq, group_len, model_width)
    regathered = (
        lax.all_gather(ln1_gain, ("dp", "ctx"), axis=0, tiled=True),
        lax.all_gather(ln1_bias, ("dp", "ctx"), axis=0, tiled=True),
        lax.all_gather(w_qkv, ("dp", "ctx"), axis=0, tiled=True),
        lax.all_gather(b_qv, ("dp", "ctx"), axis=0, tiled=True),
        lax.all_gather(w_proj, ("dp", "ctx"), axis=0, tiled=True),
        lax.all_gather(b_proj, ("dp", "ctx"), axis=0, tiled=True),
        lax.all_gather(ln2_gain, ("dp", "ctx"), axis=0, tiled=True),
        lax.all_gather(ln2_bias, ("dp", "ctx"), axis=0, tiled=True),
        lax.all_gather(w_fc, ("dp", "ctx"), axis=0, tiled=True),
        lax.all_gather(b_fc, ("dp", "ctx"), axis=0, tiled=True),
        lax.all_gather(w_out, ("dp", "ctx"), axis=0, tiled=True),
        lax.all_gather(b_out, ("dp", "ctx"), axis=0, tiled=True),
    )
    qkv_weight = regathered[2]
    proj_weight = regathered[4]
    fc_weight = regathered[8]
    out_weight = regathered[10]
    grad_top = cotangent.reshape(rows_total, model_width)
    grad_top32 = grad_top.astype(jnp.float32)
    grad_out_bias = jnp.sum(grad_top32, axis=0)
    grad_out_weight = outer_sum(activated_low, grad_top)
    grad_act = back_through(grad_top, out_weight)
    grad_pre = gelu_pull(grad_act)[0].astype(jnp.bfloat16)
    grad_fc_bias = jnp.sum(grad_pre.astype(jnp.float32), axis=0)
    grad_fc_weight = outer_sum(normed_two_low, grad_pre)
    grad_normed_two = back_through(grad_pre, fc_weight)
    grad_middle_ln, grad_gain_two, grad_bias_two = pull_two(grad_normed_two)
    grad_middle = grad_top32 + grad_middle_ln
    grad_branch = grad_middle.astype(jnp.bfloat16)
    grad_proj_bias = jnp.sum(grad_branch.astype(jnp.float32), axis=0)
    grad_proj_weight = outer_sum(merged_low, grad_branch)
    grad_merged = back_through(grad_branch, proj_weight).astype(jnp.bfloat16)
    grad_flat = grad_merged.reshape(count_seq, group_len, model_width)
    grad_heads = split_heads(grad_flat)
    delta_rows = jnp.einsum("sqhd,shqd->shq", grad_heads.astype(jnp.float32), attended)
    remote = lax.all_gather(key_value, "ctx", axis=1, tiled=True)
    rows_here = remote.shape[1]
    key_pos = jnp.arange(rows_here, dtype=jnp.int32)
    part_query, part_keys, part_values = attend_grad(
        query_rows,
        grad_heads,
        log_total,
        delta_rows,
        split_heads(remote[:, :, :model_width]),
        split_heads(remote[:, :, model_width:]),
        query_pos,
        key_pos,
    )
    joined = jnp.concatenate(
        [
            part_keys.reshape(count_seq, rows_here, model_width),
            part_values.reshape(count_seq, rows_here, model_width),
        ],
        axis=2,
    )
    grad_kv_all = joined
    grad_query, grad_kv_all = (part_query, grad_kv_all)
    grad_kv = lax.psum_scatter(
        grad_kv_all.astype(jnp.bfloat16), "ctx", scatter_dimension=1, tiled=True
    ).astype(jnp.float32)
    grad_query_flat = grad_query.reshape(count_seq, group_len, model_width)
    grad_qkv = jnp.concatenate(
        [
            grad_query_flat.reshape(rows_total, model_width),
            grad_kv.reshape(rows_total, 2 * model_width),
        ],
        axis=1,
    ).astype(jnp.bfloat16)
    column_sums = jnp.sum(grad_qkv.astype(jnp.float32), axis=0)
    grad_qkv_bias = jnp.concatenate([column_sums[:model_width], column_sums[2 * model_width :]])
    grad_qkv_weight = outer_sum(normed_low, grad_qkv)
    grad_normed_one = back_through(grad_qkv, qkv_weight)
    grad_input_ln, grad_gain_one, grad_bias_one = pull_one(grad_normed_one)
    grad_input = (grad_middle + grad_input_ln).reshape(count_seq, group_len, model_width)
    gradients = (
        lax.psum_scatter(grad_gain_one, ("dp", "ctx"), scatter_dimension=0, tiled=True),
        lax.psum_scatter(grad_bias_one, ("dp", "ctx"), scatter_dimension=0, tiled=True),
        lax.psum_scatter(grad_qkv_weight, ("dp", "ctx"), scatter_dimension=0, tiled=True),
        lax.psum_scatter(grad_qkv_bias, ("dp", "ctx"), scatter_dimension=0, tiled=True),
        lax.psum_scatter(grad_proj_weight, ("dp", "ctx"), scatter_dimension=0, tiled=True),
        lax.psum_scatter(grad_proj_bias, ("dp", "ctx"), scatter_dimension=0, tiled=True),
        lax.psum_scatter(grad_gain_two, ("dp", "ctx"), scatter_dimension=0, tiled=True),
        lax.psum_scatter(grad_bias_two, ("dp", "ctx"), scatter_dimension=0, tiled=True),
        lax.psum_scatter(grad_fc_weight, ("dp", "ctx"), scatter_dimension=0, tiled=True),
        lax.psum_scatter(grad_fc_bias, ("dp", "ctx"), scatter_dimension=0, tiled=True),
        lax.psum_scatter(grad_out_weight, ("dp", "ctx"), scatter_dimension=0, tiled=True),
        lax.psum_scatter(grad_out_bias, ("dp", "ctx"), scatter_dimension=0, tiled=True),
    )
    return (result, grad_input) + tuple(gradients)


def axis_bits(axis):
    size = lax.axis_size(axis)
    return [(axis, 1 << k) for k in reversed(range(size.bit_length() - 1))]


def swap(values, bit):
    axis, mask = bit
    return lax.ppermute(values, axis, [(i, i ^ mask) for i in range(lax.axis_size(axis))])


def bit_value(bit):
    axis, mask = bit
    return (lax.axis_index(axis) // mask) % 2


def in_order(mine, other, bit, dim):
    place = lax.broadcasted_iota(jnp.int32, (2,) + (1,) * (mine.ndim - dim), 0)
    own = place == bit_value(bit)
    return jnp.where(own, jnp.expand_dims(mine, dim), jnp.expand_dims(other, dim))


def gather_bit(values, bit, dim):
    return in_order(values, swap(values, bit), bit, dim)


def take(values, index, dim):
    return lax.dynamic_index_in_dim(values, index, dim, keepdims=False)


def scatter_bit(values, bit, dim):
    here = bit_value(bit)
    sent = swap(take(values, 1 - here, dim), bit)
    kept = take(values, here, dim).astype(jnp.float32)
    return (kept + sent.astype(jnp.float32)).astype(values.dtype)


def trade_bit(values, bit, dim):
    here = bit_value(bit)
    return in_order(take(values, here, dim), swap(take(values, 1 - here, dim), bit), bit, dim)


def gather_bits(values, order, bits, held):
    held = list(held)
    for bit in order:
        held = sorted(held + [bit], key=bits.index)
        values = gather_bit(values, bit, held.index(bit))
    return values


def scatter_bits(values, order, bits):
    left = list(bits)
    for bit in order:
        values = scatter_bit(values, bit, left.index(bit))
        left.remove(bit)
    return values


def stack_rows(vectors, width):
    count = len(vectors)
    rows = [
        lax.pad(
            vector.astype(jnp.float32).reshape(1, -1),
            jnp.float32(0),
            ((k, count - 1 - k, 0), (0, width - vector.shape[0], 0)),
        )
        for k, vector in enumerate(vectors)
    ]
    return functools.reduce(jnp.add, rows)


def after(values, *others):
    return lax.optimization_barrier((values,) + others)[0]


def dot_last(left, right):
    return lax.dot_general(left, right, (((1,), (1,)), ((), ())), preferred_element_type=jnp.float32)


def dot_first(left, right):
    return lax.dot_general(left, right, (((0,), (0,)), ((), ())), preferred_element_type=jnp.float32)


def seen_scores(keys, queries, start):
    scores = dot_last(keys, queries)
    key_pos = lax.broadcasted_iota(jnp.int32, scores.shape, 0)
    query_pos = lax.broadcasted_iota(jnp.int32, scores.shape, 1) + start
    return jnp.where(key_pos <= query_pos, scores, NEG)


def attend_kernel(heads, block, qkv_ref, out_ref):
    wide = heads * HD
    for head in range(heads):
        at = head * HD
        for low in range(0, qkv_ref.shape[0], block):
            high = low + block
            queries = qkv_ref[low:high, at : at + HD] * (1.0 / math.sqrt(HD))
            keys = qkv_ref[:high, wide + at : wide + at + HD]
            values = qkv_ref[:high, 2 * wide + at : 2 * wide + at + HD]
            scores = seen_scores(keys, queries, low)
            weights = jnp.exp(scores - jnp.max(scores, axis=0, keepdims=True))
            total = jnp.sum(weights, axis=0, keepdims=True)
            mixed = dot_first(values, weights.astype(jnp.bfloat16)) / total
            out_ref[low:high, at : at + HD] = mixed.T.astype(jnp.bfloat16)


def attend_grad_kernel(heads, block, qkv_ref, grad_ref, out_ref, keys_acc, values_acc):
    wide = heads * HD
    factor = 1.0 / math.sqrt(HD)
    for head in range(heads):
        at = head * HD
        keys_acc[...] = jnp.zeros_like(keys_acc)
        values_acc[...] = jnp.zeros_like(values_acc)
        for low in range(0, qkv_ref.shape[0], block):
            high = low + block
            queries = qkv_ref[low:high, at : at + HD] * factor
            keys = qkv_ref[:high, wide + at : wide + at + HD]
            values = qkv_ref[:high, 2 * wide + at : 2 * wide + at + HD]
            grads = grad_ref[low:high, at : at + HD]
            scores = seen_scores(keys, queries, low)
            weights = jnp.exp(scores - jnp.max(scores, axis=0, keepdims=True))
            probs = weights / jnp.sum(weights, axis=0, keepdims=True)
            grad_probs = dot_last(values, grads)
            delta = jnp.sum(probs * grad_probs, axis=0, keepdims=True)
            grad_scores = (probs * (grad_probs - delta)).astype(jnp.bfloat16)
            values_acc[:high] += jnp.dot(
                probs.astype(jnp.bfloat16), grads, preferred_element_type=jnp.float32
            )
            keys_acc[:high] += jnp.dot(grad_scores, queries, preferred_element_type=jnp.float32)
            grad_queries = dot_first(keys, grad_scores) * factor
            out_ref[low:high, at : at + HD] = grad_queries.T.astype(jnp.bfloat16)
        out_ref[:, wide + at : wide + at + HD] = keys_acc[...].astype(jnp.bfloat16)
        out_ref[:, 2 * wide + at : 2 * wide + at + HD] = values_acc[...].astype(jnp.bfloat16)


VMEM_LIMIT = 48 * 1024 * 1024


def attend(qkv, heads):
    rows = qkv.shape[0]
    return pl.pallas_call(
        functools.partial(attend_kernel, heads, min(rows, 256)),
        out_shape=jax.ShapeDtypeStruct((rows, heads * HD), jnp.bfloat16),
        compiler_params=pltpu.CompilerParams(vmem_limit_bytes=VMEM_LIMIT),
        name="attend",
    )(qkv)


def attend_back(qkv, grads, heads):
    rows = qkv.shape[0]
    return pl.pallas_call(
        functools.partial(attend_grad_kernel, heads, min(rows, 256)),
        out_shape=jax.ShapeDtypeStruct(qkv.shape, jnp.bfloat16),
        scratch_shapes=[pltpu.VMEM((rows, HD), jnp.float32), pltpu.VMEM((rows, HD), jnp.float32)],
        compiler_params=pltpu.CompilerParams(vmem_limit_bytes=VMEM_LIMIT),
        name="attend_back",
    )(qkv, grads)


def normalize(values):
    average = jnp.mean(values, axis=-1, keepdims=True)
    centered = values - average
    variance = jnp.mean(centered * centered, axis=-1, keepdims=True)
    scale = lax.rsqrt(variance + EPS)
    return centered * scale, scale


def normalize_back(grad_normed, gain, unit, scale):
    inner = grad_normed * gain
    return scale * (
        inner
        - jnp.mean(inner, axis=-1, keepdims=True)
        - unit * jnp.mean(inner * unit, axis=-1, keepdims=True)
    )


def split_body(
    tokens,
    ln1_gain,
    ln1_bias,
    w_qkv,
    b_qv,
    w_proj,
    b_proj,
    ln2_gain,
    ln2_bias,
    w_fc,
    b_fc,
    w_out,
    b_out,
    cotangent,
):
    f32, bf16 = jnp.float32, jnp.bfloat16
    count_seq, group_len, model_width = tokens.shape
    rows_total = count_seq * group_len
    dp_bits, ctx_bits = axis_bits("dp"), axis_bits("ctx")
    bits = dp_bits + ctx_bits
    near, high_bits = dp_bits[-1], dp_bits[:-1]
    far, team_bits = ctx_bits[0], ctx_bits[1:]
    ctx_size, dp_size = lax.axis_size("ctx"), lax.axis_size("dp")
    devices = ctx_size * dp_size
    team = 1 << len(team_bits)
    heads = H // team
    wide = heads * HD
    sequence = bit_value(far)
    member = lax.axis_index("ctx") % team
    core = bit_value(near)
    own_rows = w_qkv.shape[0]
    link_bits = high_bits + ctx_bits
    team_dims, link_dims, all_dims = (2,) * len(team_bits), (2,) * len(link_bits), (2,) * len(bits)

    mine = take(tokens, sequence, 0)
    theirs = swap(take(tokens, 1 - sequence, 0), far)
    pair = in_order(mine, theirs, far, 0)
    half = model_width // 2
    sides = [
        gather_bits(part, order, [far] + team_bits, [far]).reshape(ctx_size * group_len, half)
        for part, order in ((pair[..., :half], team_bits), (pair[..., half:], team_bits[::-1]))
    ]
    long_tokens = jnp.concatenate(sides, axis=1)

    vectors = (ln1_gain, ln1_bias, b_qv, b_proj, ln2_gain, ln2_bias, b_fc, b_out)
    sizes = [vector.shape[0] for vector in vectors]
    riders = stack_rows(vectors, 3 * wide).astype(bf16)
    columns = w_qkv.reshape(own_rows, 3, team, wide).transpose(2, 0, 1, 3)
    columns = columns.reshape(team, own_rows, 3 * wide)
    columns = jnp.concatenate(
        [columns, jnp.broadcast_to(riders, (team,) + riders.shape)], axis=1
    ).reshape(team_dims + (own_rows + len(vectors), 3 * wide))
    for k in reversed(range(len(team_bits))):
        columns = trade_bit(columns, team_bits[k], k)
    columns = gather_bits(columns, [far] + dp_bits[::-1], bits, team_bits)
    columns = columns.reshape(devices, own_rows + len(vectors), 3 * wide)
    qkv_weight = columns[:, :own_rows].reshape(devices * own_rows, 3 * wide)
    (gain_one, bias_one, qv_bias, proj_bias, gain_two, bias_two, fc_bias, out_bias) = (
        columns[:, own_rows + k, :size].reshape(devices * size).astype(f32)
        for k, size in enumerate(sizes)
    )

    hidden_part = w_fc.shape[1] // dp_size
    hidden = w_fc.shape[1] // 2
    fc_sides = w_fc.reshape(own_rows, dp_size // 2, 2, hidden_part).transpose(2, 0, 1, 3)
    fc_sides = fc_sides.reshape(2, own_rows, hidden)
    proj_both = jnp.broadcast_to(w_proj, (2,) + w_proj.shape)
    cut, proj_cut = hidden // 2, model_width // 2
    first = jnp.concatenate(
        [fc_sides[..., :cut], proj_both[..., :proj_cut], fc_sides[..., cut:], proj_both[..., proj_cut:]],
        axis=2,
    )
    first = trade_bit(first, near, 0)
    whole = cut + proj_cut

    def ordered(turn):
        links = team_bits[::-1] + high_bits
        return links[turn % len(links) :] + links[: turn % len(links)]

    def gather_weight(shard, turn, held):
        order = [far] + ordered(turn)
        early = gather_bits(shard, order[:2], bits, held)
        return gather_bits(after(early, long_tokens), order[2:], bits, held + order[:2])

    left = gather_weight(first[..., :whole], 1, [near]).reshape(devices * own_rows, whole)
    right = gather_weight(first[..., whole:], 2, [near]).reshape(devices * own_rows, whole)
    out_weight = gather_weight(w_out, 0, []).reshape(hidden, model_width)
    fc_weight = jnp.concatenate([left[:, :cut], right[:, :cut]], axis=1)
    proj_weight = jnp.concatenate([left[:, cut:], right[:, cut:]], axis=1)
    fc_bias = take(fc_bias.reshape(dp_size // 2, 2, hidden_part), core, 1).reshape(hidden)

    unit_long, _ = normalize(long_tokens.astype(f32))
    normed_long = (unit_long * gain_one + bias_one).astype(bf16)
    team_bias = take(qv_bias.reshape(2, team, wide), member, 1)
    bias_row = jnp.concatenate([team_bias[0], jnp.zeros((wide,), f32), team_bias[1]])
    qkv = (jnp.dot(normed_long, qkv_weight, preferred_element_type=f32) + bias_row).astype(bf16)
    attended = attend(qkv, heads)

    def to_rows(values):
        parts = lax.all_to_all(
            values.reshape(ctx_size, group_len, wide), "ctx", 0, 0, tiled=True
        )
        parts = parts.reshape(count_seq, team, group_len, wide).transpose(0, 2, 1, 3)
        return parts.reshape(rows_total, model_width)

    def to_heads(values):
        parts = values.reshape(count_seq, group_len, team, wide).transpose(0, 2, 1, 3)
        parts = parts.reshape(ctx_size, group_len, wide)
        return lax.all_to_all(parts, "ctx", 0, 0, tiled=True).reshape(ctx_size * group_len, wide)

    def both_rows(values):
        return gather_bit(values, near, 0).reshape(2 * rows_total, values.shape[1])

    def own_sum(values):
        return scatter_bit(values.reshape(2, rows_total, values.shape[1]), near, 0)

    merged = to_rows(attended)

    grad_top = cotangent.reshape(rows_total, model_width)
    grad_top32 = grad_top.astype(f32)
    grad_both = both_rows(grad_top)
    inputs = tokens.astype(f32).reshape(rows_total, model_width)
    middle_rows = inputs + jnp.dot(merged, proj_weight, preferred_element_type=f32) + proj_bias
    unit_two, scale_two = normalize(middle_rows)
    normed_two = both_rows((unit_two * gain_two + bias_two).astype(bf16))
    pre_act = jnp.dot(normed_two, fc_weight, preferred_element_type=f32) + fc_bias
    activated32, gelu_pull = jax.vjp(gelu_tanh, pre_act)
    activated = activated32.astype(bf16)
    fed = own_sum(jnp.dot(activated, out_weight, preferred_element_type=f32))
    result = (middle_rows + fed + out_bias).astype(bf16).reshape(tokens.shape)

    out_left, out_order = list(link_bits), ordered(0)[::-1] + [far]
    grad_out_weight = outer_sum(activated, grad_both).astype(bf16)
    grad_out_weight = grad_out_weight.reshape(link_dims + w_out.shape)
    out_one = scatter_bits(grad_out_weight, out_order[:1], link_bits)
    out_left.remove(out_order[0])

    grad_pre = gelu_pull(back_through(grad_both, out_weight))[0].astype(bf16)
    grad_fc_bias = jnp.sum(grad_pre.astype(f32), axis=0)
    grad_fc_weight = outer_sum(normed_two, grad_pre).astype(bf16)
    grad_normed_two = own_sum(back_through(grad_pre, fc_weight))
    grad_gain_two = jnp.sum(grad_normed_two * unit_two, axis=0)
    grad_bias_two = jnp.sum(grad_normed_two, axis=0)
    grad_middle = grad_top32 + normalize_back(grad_normed_two, gain_two, unit_two, scale_two)
    grad_branch = grad_middle.astype(bf16)
    grad_proj_bias = jnp.sum(grad_branch.astype(f32), axis=0)
    grad_proj_weight = outer_sum(merged, grad_branch).astype(bf16)
    halves = [
        jnp.concatenate([grad_fc_weight[:, low : low + cut], grad_proj_weight[:, at : at + proj_cut]], 1)
        for low, at in ((0, 0), (cut, proj_cut))
    ]
    halves = [part.reshape(all_dims + (own_rows, whole)) for part in halves]
    half_orders = [ordered(turn)[::-1] + [far] for turn in (1, 2)]
    half_ones = [scatter_bits(part, order[:1], bits) for part, order in zip(halves, half_orders)]

    grad_heads = to_heads(back_through(grad_branch, proj_weight).astype(bf16))
    grad_heads, out_one = lax.optimization_barrier((grad_heads, out_one))
    grad_qkv = attend_back(qkv, grad_heads, heads)
    grad_long = back_through(grad_qkv, qkv_weight)
    grad_gain_one = jnp.sum(grad_long * unit_long, axis=0)
    grad_bias_one = jnp.sum(grad_long, axis=0)
    blocks = grad_long.astype(bf16).reshape((2,) + team_dims + (group_len, model_width))
    parts = outer_sum(normed_long, grad_qkv).astype(bf16)
    parts, blocks, out_one, *half_ones = lax.optimization_barrier((parts, blocks, out_one, *half_ones))
    grad_out_weight = scatter_bits(out_one, out_order[1:], out_left)
    half_ends = []
    for part, order in zip(half_ones, half_orders):
        half_left = [bit for bit in bits if bit != order[0]]
        half_ends.append(scatter_bits(part, order[1:], half_left))
    fc_and_proj = jnp.concatenate(half_ends, axis=-1)
    kept, sent = take(fc_and_proj, core, 0), take(fc_and_proj, 1 - core, 0)
    sent = swap(sent, near)
    grad_proj_weight = (kept.astype(f32) + sent.astype(f32)).reshape(own_rows, 2, whole)[..., cut:]
    grad_proj_weight = grad_proj_weight.reshape(w_proj.shape)
    grad_fc_weight = in_order(kept, sent, near, 0).reshape(2, own_rows, 2, whole)[..., :cut]
    grad_fc_weight = grad_fc_weight.reshape(2, own_rows, dp_size // 2, hidden_part)
    grad_fc_weight = grad_fc_weight.transpose(1, 2, 0, 3).reshape(w_fc.shape).astype(f32)

    sides = [
        scatter_bits(part, order, [far] + team_bits)
        for part, order in ((blocks[..., :half], team_bits), (blocks[..., half:], team_bits[::-1]))
    ]
    part = jnp.concatenate(sides, axis=-1)
    grad_normed_one = trade_bit(part, far, 0).astype(f32)
    unit_one, scale_one = normalize(tokens.astype(f32))
    grad_input = grad_middle.reshape(tokens.shape) + normalize_back(
        grad_normed_one, gain_one, unit_one, scale_one
    )

    sums = jnp.sum(grad_qkv.astype(f32), axis=0).reshape(3, 1, wide)
    placed = lax.dynamic_update_index_in_dim(
        jnp.zeros((2, team, wide), f32), jnp.concatenate([sums[:1], sums[2:]]), member, 1
    )
    fc_bias_placed = lax.dynamic_update_index_in_dim(
        jnp.zeros((dp_size // 2, 2, hidden_part), f32),
        grad_fc_bias.reshape(dp_size // 2, 1, hidden_part),
        core,
        1,
    )
    totals = (
        grad_gain_one,
        grad_bias_one,
        placed,
        grad_proj_bias,
        grad_gain_two,
        grad_bias_two,
        fc_bias_placed,
        jnp.sum(grad_top32, axis=0),
    )
    parts = parts.reshape(all_dims + (own_rows, 3 * wide))
    parts = scatter_bits(parts, dp_bits[::-1] + [far], bits)
    for k in range(len(team_bits)):
        parts = trade_bit(parts, team_bits[k], k)
    grad_qkv_weight = parts.reshape(team, own_rows, 3, wide).transpose(1, 2, 0, 3)
    grad_qkv_weight = grad_qkv_weight.reshape(w_qkv.shape).astype(f32)
    spread = jnp.concatenate([total.reshape(devices, -1) for total in totals], axis=1)
    spread = lax.all_to_all(spread, ("dp", "ctx"), 0, 0, tiled=True)
    summed = jnp.sum(spread, axis=0)
    starts = [sum(sizes[:k]) for k in range(len(sizes))]
    (g_gain_one, g_bias_one, g_qv, g_proj, g_gain_two, g_bias_two, g_fc, g_out) = (
        summed[start : start + size] for start, size in zip(starts, sizes)
    )
    return (
        result,
        grad_input,
        g_gain_one,
        g_bias_one,
        grad_qkv_weight,
        g_qv,
        grad_proj_weight,
        g_proj,
        g_gain_two,
        g_bias_two,
        grad_fc_weight,
        g_fc,
        grad_out_weight.astype(f32),
        g_out,
    )


def body(tokens, *others):
    ctx_size, dp_size = lax.axis_size("ctx"), lax.axis_size("dp")
    powers = ctx_size & (ctx_size - 1) == 0 and dp_size & (dp_size - 1) == 0
    if powers and dp_size > 1 and ctx_size > 2 and tokens.shape[0] == 2 and H % (ctx_size // 2) == 0:
        return split_body(tokens, *others)
    return plain_body(tokens, *others)


def solution(mesh):
    placed = (
        P("dp", "ctx", None),
        P(("dp", "ctx")),
        P(("dp", "ctx")),
        P(("dp", "ctx"), None),
        P(("dp", "ctx")),
        P(("dp", "ctx"), None),
        P(("dp", "ctx")),
        P(("dp", "ctx")),
        P(("dp", "ctx")),
        P(("dp", "ctx"), None),
        P(("dp", "ctx")),
        P(("dp", "ctx"), None),
        P(("dp", "ctx")),
        P("dp", "ctx", None),
    )
    return jax.shard_map(
        body,
        mesh=mesh,
        in_specs=placed,
        out_specs=(
            P("dp", "ctx", None),
            P("dp", "ctx", None),
            P(("dp", "ctx")),
            P(("dp", "ctx")),
            P(("dp", "ctx"), None),
            P(("dp", "ctx")),
            P(("dp", "ctx"), None),
            P(("dp", "ctx")),
            P(("dp", "ctx")),
            P(("dp", "ctx")),
            P(("dp", "ctx"), None),
            P(("dp", "ctx")),
            P(("dp", "ctx"), None),
            P(("dp", "ctx")),
        ),
        check_vma=False,
    )
```

```python
import functools
import math

import jax
import jax.numpy as jnp
from jax import lax
from jax.experimental import pallas as pl
from jax.experimental.layout import Layout, with_layout_constraint
from jax.experimental.pallas import tpu as pltpu
from jax.sharding import PartitionSpec as P

H = 12
HD = 64


EPS = 1e-05
NEG = -1e30


def layer_norm(values, gain_vec, bias_vec):
    average = jnp.mean(values, axis=-1, keepdims=True)
    centered = values - average
    variance = jnp.mean(centered * centered, axis=-1, keepdims=True)
    return centered * lax.rsqrt(variance + EPS) * gain_vec + bias_vec


def gelu_tanh(values):
    return jax.nn.gelu(values, approximate=True)


def outer_sum(left, right):
    return lax.dot_general(
        left, right, (((0,), (0,)), ((), ())), preferred_element_type=jnp.float32
    )


def back_through(grad_rows, weight_mat):
    return lax.dot_general(
        grad_rows, weight_mat, (((1,), (1,)), ((), ())), preferred_element_type=jnp.float32
    )


def split_heads(flat_rows):
    return flat_rows.reshape(flat_rows.shape[0], flat_rows.shape[1], H, HD)


def attend_block(query_rows, key_rows, value_rows, query_pos, key_pos, running):
    factor = 1.0 / math.sqrt(HD)
    scores = (
        jnp.einsum("sqhd,skhd->shqk", query_rows, key_rows, preferred_element_type=jnp.float32)
        * factor
    )
    visible = key_pos[None, :] <= query_pos[:, None]
    scores = jnp.where(visible, scores, NEG)
    run_max, run_sum, run_acc = running
    new_max = jnp.maximum(run_max, jnp.max(scores, axis=-1))
    weights = jnp.where(visible, jnp.exp(scores - new_max[..., None]), 0.0)
    new_sum = jnp.sum(weights, axis=-1)
    added = jnp.einsum(
        "shqk,skhd->shqd",
        weights.astype(jnp.bfloat16),
        value_rows,
        preferred_element_type=jnp.float32,
    )
    return (new_max, new_sum, added)


def attend_grad(
    query_rows, grad_heads, log_total, delta_rows, key_rows, value_rows, query_pos, key_pos
):
    factor = 1.0 / math.sqrt(HD)
    scores = (
        jnp.einsum("sqhd,skhd->shqk", query_rows, key_rows, preferred_element_type=jnp.float32)
        * factor
    )
    visible = key_pos[None, :] <= query_pos[:, None]
    probs = jnp.where(visible, jnp.exp(scores - log_total[..., None]), 0.0)
    grad_values = jnp.einsum(
        "shqk,sqhd->skhd",
        probs.astype(jnp.bfloat16),
        grad_heads,
        preferred_element_type=jnp.float32,
    )
    grad_probs = jnp.einsum(
        "sqhd,skhd->shqk", grad_heads, value_rows, preferred_element_type=jnp.float32
    )
    grad_scores = (probs * (grad_probs - delta_rows[..., None])).astype(jnp.bfloat16)
    grad_query = (
        jnp.einsum("shqk,skhd->sqhd", grad_scores, key_rows, preferred_element_type=jnp.float32)
        * factor
    )
    grad_keys = (
        jnp.einsum("shqk,sqhd->skhd", grad_scores, query_rows, preferred_element_type=jnp.float32)
        * factor
    )
    return (grad_query, grad_keys, grad_values)


def plain_body(
    tokens,
    ln1_gain,
    ln1_bias,
    w_qkv,
    b_qv,
    w_proj,
    b_proj,
    ln2_gain,
    ln2_bias,
    w_fc,
    b_fc,
    w_out,
    b_out,
    cotangent,
):
    gathered = (
        lax.all_gather(ln1_gain, ("dp", "ctx"), axis=0, tiled=True),
        lax.all_gather(ln1_bias, ("dp", "ctx"), axis=0, tiled=True),
        lax.all_gather(w_qkv, ("dp", "ctx"), axis=0, tiled=True),
        lax.all_gather(b_qv, ("dp", "ctx"), axis=0, tiled=True),
        lax.all_gather(w_proj, ("dp", "ctx"), axis=0, tiled=True),
        lax.all_gather(b_proj, ("dp", "ctx"), axis=0, tiled=True),
        lax.all_gather(ln2_gain, ("dp", "ctx"), axis=0, tiled=True),
        lax.all_gather(ln2_bias, ("dp", "ctx"), axis=0, tiled=True),
        lax.all_gather(w_fc, ("dp", "ctx"), axis=0, tiled=True),
        lax.all_gather(b_fc, ("dp", "ctx"), axis=0, tiled=True),
        lax.all_gather(w_out, ("dp", "ctx"), axis=0, tiled=True),
        lax.all_gather(b_out, ("dp", "ctx"), axis=0, tiled=True),
    )
    (
        gain_one,
        bias_one,
        qkv_weight,
        qkv_bias,
        proj_weight,
        proj_bias,
        gain_two,
        bias_two,
        fc_weight,
        fc_bias,
        out_weight,
        out_bias,
    ) = gathered
    count_seq, group_len, model_width = tokens.shape
    rows_total = count_seq * group_len
    query_pos = lax.axis_index("ctx") * group_len + jnp.arange(group_len, dtype=jnp.int32)
    inputs = tokens.astype(jnp.float32).reshape(rows_total, model_width)
    normed_one, pull_one = jax.vjp(
        layer_norm, inputs, gain_one.astype(jnp.float32), bias_one.astype(jnp.float32)
    )
    normed_low = normed_one.astype(jnp.bfloat16)
    qkv_bias32 = qkv_bias.astype(jnp.float32)
    bias_full = jnp.concatenate(
        [qkv_bias32[:model_width], jnp.zeros((model_width,), jnp.float32), qkv_bias32[model_width:]]
    )
    qkv_low = (
        jnp.dot(normed_low, qkv_weight, preferred_element_type=jnp.float32) + bias_full
    ).astype(jnp.bfloat16)
    query_flat = qkv_low[:, :model_width].reshape(count_seq, group_len, model_width)
    query_rows = split_heads(query_flat)
    key_value = qkv_low[:, model_width:].reshape(count_seq, group_len, 2 * model_width)
    initial = (
        jnp.full((count_seq, H, group_len), NEG, jnp.float32),
        jnp.zeros((count_seq, H, group_len), jnp.float32),
        jnp.zeros((count_seq, H, group_len, HD), jnp.float32),
    )
    remote = lax.all_gather(key_value, "ctx", axis=1, tiled=True)
    rows_here = remote.shape[1]
    key_pos = jnp.arange(rows_here, dtype=jnp.int32)
    key_rows = split_heads(remote[:, :, :model_width])
    value_rows = split_heads(remote[:, :, model_width:])
    run_max, run_sum, run_acc = attend_block(
        query_rows, key_rows, value_rows, query_pos, key_pos, initial
    )
    attended = run_acc / run_sum[..., None]
    log_total = run_max + jnp.log(run_sum)
    merged_low = (
        attended.transpose(0, 2, 1, 3).reshape(rows_total, model_width).astype(jnp.bfloat16)
    )
    middle = (
        inputs
        + jnp.dot(merged_low, proj_weight, preferred_element_type=jnp.float32)
        + proj_bias.astype(jnp.float32)
    )
    normed_two, pull_two = jax.vjp(
        layer_norm, middle, gain_two.astype(jnp.float32), bias_two.astype(jnp.float32)
    )
    normed_two_low = normed_two.astype(jnp.bfloat16)
    pre_act = jnp.dot(
        normed_two_low, fc_weight, preferred_element_type=jnp.float32
    ) + fc_bias.astype(jnp.float32)
    activated, gelu_pull = jax.vjp(gelu_tanh, pre_act)
    activated_low = activated.astype(jnp.bfloat16)
    feed_out = jnp.dot(
        activated_low, out_weight, preferred_element_type=jnp.float32
    ) + out_bias.astype(jnp.float32)
    result = (middle + feed_out).astype(jnp.bfloat16).reshape(count_seq, group_len, model_width)
    regathered = (
        lax.all_gather(ln1_gain, ("dp", "ctx"), axis=0, tiled=True),
        lax.all_gather(ln1_bias, ("dp", "ctx"), axis=0, tiled=True),
        lax.all_gather(w_qkv, ("dp", "ctx"), axis=0, tiled=True),
        lax.all_gather(b_qv, ("dp", "ctx"), axis=0, tiled=True),
        lax.all_gather(w_proj, ("dp", "ctx"), axis=0, tiled=True),
        lax.all_gather(b_proj, ("dp", "ctx"), axis=0, tiled=True),
        lax.all_gather(ln2_gain, ("dp", "ctx"), axis=0, tiled=True),
        lax.all_gather(ln2_bias, ("dp", "ctx"), axis=0, tiled=True),
        lax.all_gather(w_fc, ("dp", "ctx"), axis=0, tiled=True),
        lax.all_gather(b_fc, ("dp", "ctx"), axis=0, tiled=True),
        lax.all_gather(w_out, ("dp", "ctx"), axis=0, tiled=True),
        lax.all_gather(b_out, ("dp", "ctx"), axis=0, tiled=True),
    )
    qkv_weight = regathered[2]
    proj_weight = regathered[4]
    fc_weight = regathered[8]
    out_weight = regathered[10]
    grad_top = cotangent.reshape(rows_total, model_width)
    grad_top32 = grad_top.astype(jnp.float32)
    grad_out_bias = jnp.sum(grad_top32, axis=0)
    grad_out_weight = outer_sum(activated_low, grad_top)
    grad_act = back_through(grad_top, out_weight)
    grad_pre = gelu_pull(grad_act)[0].astype(jnp.bfloat16)
    grad_fc_bias = jnp.sum(grad_pre.astype(jnp.float32), axis=0)
    grad_fc_weight = outer_sum(normed_two_low, grad_pre)
    grad_normed_two = back_through(grad_pre, fc_weight)
    grad_middle_ln, grad_gain_two, grad_bias_two = pull_two(grad_normed_two)
    grad_middle = grad_top32 + grad_middle_ln
    grad_branch = grad_middle.astype(jnp.bfloat16)
    grad_proj_bias = jnp.sum(grad_branch.astype(jnp.float32), axis=0)
    grad_proj_weight = outer_sum(merged_low, grad_branch)
    grad_merged = back_through(grad_branch, proj_weight).astype(jnp.bfloat16)
    grad_flat = grad_merged.reshape(count_seq, group_len, model_width)
    grad_heads = split_heads(grad_flat)
    delta_rows = jnp.einsum("sqhd,shqd->shq", grad_heads.astype(jnp.float32), attended)
    remote = lax.all_gather(key_value, "ctx", axis=1, tiled=True)
    rows_here = remote.shape[1]
    key_pos = jnp.arange(rows_here, dtype=jnp.int32)
    part_query, part_keys, part_values = attend_grad(
        query_rows,
        grad_heads,
        log_total,
        delta_rows,
        split_heads(remote[:, :, :model_width]),
        split_heads(remote[:, :, model_width:]),
        query_pos,
        key_pos,
    )
    joined = jnp.concatenate(
        [
            part_keys.reshape(count_seq, rows_here, model_width),
            part_values.reshape(count_seq, rows_here, model_width),
        ],
        axis=2,
    )
    grad_kv_all = joined
    grad_query, grad_kv_all = (part_query, grad_kv_all)
    grad_kv = lax.psum_scatter(
        grad_kv_all.astype(jnp.bfloat16), "ctx", scatter_dimension=1, tiled=True
    ).astype(jnp.float32)
    grad_query_flat = grad_query.reshape(count_seq, group_len, model_width)
    grad_qkv = jnp.concatenate(
        [
            grad_query_flat.reshape(rows_total, model_width),
            grad_kv.reshape(rows_total, 2 * model_width),
        ],
        axis=1,
    ).astype(jnp.bfloat16)
    column_sums = jnp.sum(grad_qkv.astype(jnp.float32), axis=0)
    grad_qkv_bias = jnp.concatenate([column_sums[:model_width], column_sums[2 * model_width :]])
    grad_qkv_weight = outer_sum(normed_low, grad_qkv)
    grad_normed_one = back_through(grad_qkv, qkv_weight)
    grad_input_ln, grad_gain_one, grad_bias_one = pull_one(grad_normed_one)
    grad_input = (grad_middle + grad_input_ln).reshape(count_seq, group_len, model_width)
    gradients = (
        lax.psum_scatter(grad_gain_one, ("dp", "ctx"), scatter_dimension=0, tiled=True),
        lax.psum_scatter(grad_bias_one, ("dp", "ctx"), scatter_dimension=0, tiled=True),
        lax.psum_scatter(grad_qkv_weight, ("dp", "ctx"), scatter_dimension=0, tiled=True),
        lax.psum_scatter(grad_qkv_bias, ("dp", "ctx"), scatter_dimension=0, tiled=True),
        lax.psum_scatter(grad_proj_weight, ("dp", "ctx"), scatter_dimension=0, tiled=True),
        lax.psum_scatter(grad_proj_bias, ("dp", "ctx"), scatter_dimension=0, tiled=True),
        lax.psum_scatter(grad_gain_two, ("dp", "ctx"), scatter_dimension=0, tiled=True),
        lax.psum_scatter(grad_bias_two, ("dp", "ctx"), scatter_dimension=0, tiled=True),
        lax.psum_scatter(grad_fc_weight, ("dp", "ctx"), scatter_dimension=0, tiled=True),
        lax.psum_scatter(grad_fc_bias, ("dp", "ctx"), scatter_dimension=0, tiled=True),
        lax.psum_scatter(grad_out_weight, ("dp", "ctx"), scatter_dimension=0, tiled=True),
        lax.psum_scatter(grad_out_bias, ("dp", "ctx"), scatter_dimension=0, tiled=True),
    )
    return (result, grad_input) + tuple(gradients)


def axis_bits(axis):
    size = lax.axis_size(axis)
    return [(axis, 1 << k) for k in reversed(range(size.bit_length() - 1))]


def swap(values, bit):
    axis, mask = bit
    return lax.ppermute(values, axis, [(i, i ^ mask) for i in range(lax.axis_size(axis))])


def bit_value(bit):
    axis, mask = bit
    return (lax.axis_index(axis) // mask) % 2


def in_order(mine, other, bit, dim):
    place = lax.broadcasted_iota(jnp.int32, (2,) + (1,) * (mine.ndim - dim), 0)
    own = place == bit_value(bit)
    return jnp.where(own, jnp.expand_dims(mine, dim), jnp.expand_dims(other, dim))


def gather_bit(values, bit, dim):
    return in_order(values, swap(values, bit), bit, dim)


def take(values, index, dim):
    return lax.dynamic_index_in_dim(values, index, dim, keepdims=False)


def scatter_bit(values, bit, dim):
    here = bit_value(bit)
    sent = swap(take(values, 1 - here, dim), bit)
    kept = take(values, here, dim).astype(jnp.float32)
    return (kept + sent.astype(jnp.float32)).astype(values.dtype)


def trade_bit(values, bit, dim):
    here = bit_value(bit)
    return in_order(take(values, here, dim), swap(take(values, 1 - here, dim), bit), bit, dim)


def gather_bits(values, order, bits, held):
    held = list(held)
    for bit in order:
        held = sorted(held + [bit], key=bits.index)
        values = gather_bit(values, bit, held.index(bit))
    return values


def scatter_bits(values, order, bits):
    left = list(bits)
    for bit in order:
        values = scatter_bit(values, bit, left.index(bit))
        left.remove(bit)
    return values


def stack_rows(vectors, width):
    count = len(vectors)
    rows = [
        lax.pad(
            vector.astype(jnp.float32).reshape(1, -1),
            jnp.float32(0),
            ((k, count - 1 - k, 0), (0, width - vector.shape[0], 0)),
        )
        for k, vector in enumerate(vectors)
    ]
    return functools.reduce(jnp.add, rows)


class Chain:
    def __init__(self, values, order, bits):
        self.values, self.order, self.bits = values, list(order), list(bits)

    def step(self, count=1):
        for _ in range(count):
            bit = self.order.pop(0)
            self.values = scatter_bit(self.values, bit, self.bits.index(bit))
            self.bits.remove(bit)


def together(*chains):
    for chain, values in zip(chains, lax.optimization_barrier([chain.values for chain in chains])):
        chain.values = values


def row_major(values):
    return with_layout_constraint(values, Layout(major_to_minor=tuple(range(values.ndim))))


def after(values, *others):
    return lax.optimization_barrier((values,) + others)[0]


def dot_last(left, right):
    return lax.dot_general(left, right, (((1,), (1,)), ((), ())), preferred_element_type=jnp.float32)


def dot_first(left, right):
    return lax.dot_general(left, right, (((0,), (0,)), ((), ())), preferred_element_type=jnp.float32)


def seen_scores(keys, queries, start):
    scores = dot_last(keys, queries)
    key_pos = lax.broadcasted_iota(jnp.int32, scores.shape, 0)
    query_pos = lax.broadcasted_iota(jnp.int32, scores.shape, 1) + start
    return jnp.where(key_pos <= query_pos, scores, NEG)


def attend_kernel(heads, block, qkv_ref, out_ref):
    wide = heads * HD
    for head in range(heads):
        at = head * HD
        for low in range(0, qkv_ref.shape[0], block):
            high = low + block
            queries = qkv_ref[low:high, at : at + HD] * (1.0 / math.sqrt(HD))
            keys = qkv_ref[:high, wide + at : wide + at + HD]
            values = qkv_ref[:high, 2 * wide + at : 2 * wide + at + HD]
            scores = seen_scores(keys, queries, low)
            weights = jnp.exp(scores - jnp.max(scores, axis=0, keepdims=True))
            total = jnp.sum(weights, axis=0, keepdims=True)
            mixed = dot_first(values, weights.astype(jnp.bfloat16)) / total
            out_ref[low:high, at : at + HD] = mixed.T.astype(jnp.bfloat16)


def attend_grad_kernel(heads, block, qkv_ref, grad_ref, out_ref, keys_acc, values_acc):
    wide = heads * HD
    factor = 1.0 / math.sqrt(HD)
    for head in range(heads):
        at = head * HD
        keys_acc[...] = jnp.zeros_like(keys_acc)
        values_acc[...] = jnp.zeros_like(values_acc)
        for low in range(0, qkv_ref.shape[0], block):
            high = low + block
            queries = qkv_ref[low:high, at : at + HD] * factor
            keys = qkv_ref[:high, wide + at : wide + at + HD]
            values = qkv_ref[:high, 2 * wide + at : 2 * wide + at + HD]
            grads = grad_ref[low:high, at : at + HD]
            scores = seen_scores(keys, queries, low)
            weights = jnp.exp(scores - jnp.max(scores, axis=0, keepdims=True))
            probs = weights / jnp.sum(weights, axis=0, keepdims=True)
            grad_probs = dot_last(values, grads)
            delta = jnp.sum(probs * grad_probs, axis=0, keepdims=True)
            grad_scores = (probs * (grad_probs - delta)).astype(jnp.bfloat16)
            values_acc[:high] += jnp.dot(
                probs.astype(jnp.bfloat16), grads, preferred_element_type=jnp.float32
            )
            keys_acc[:high] += jnp.dot(grad_scores, queries, preferred_element_type=jnp.float32)
            grad_queries = dot_first(keys, grad_scores) * factor
            out_ref[low:high, at : at + HD] = grad_queries.T.astype(jnp.bfloat16)
        out_ref[:, wide + at : wide + at + HD] = keys_acc[...].astype(jnp.bfloat16)
        out_ref[:, 2 * wide + at : 2 * wide + at + HD] = values_acc[...].astype(jnp.bfloat16)


VMEM_LIMIT = 48 * 1024 * 1024


def attend(qkv, heads):
    rows = qkv.shape[0]
    return pl.pallas_call(
        functools.partial(attend_kernel, heads, min(rows, 256)),
        out_shape=jax.ShapeDtypeStruct((rows, heads * HD), jnp.bfloat16),
        compiler_params=pltpu.CompilerParams(vmem_limit_bytes=VMEM_LIMIT),
        name="attend",
    )(qkv)


def attend_back(qkv, grads, heads):
    rows = qkv.shape[0]
    return pl.pallas_call(
        functools.partial(attend_grad_kernel, heads, min(rows, 256)),
        out_shape=jax.ShapeDtypeStruct(qkv.shape, jnp.bfloat16),
        scratch_shapes=[pltpu.VMEM((rows, HD), jnp.float32), pltpu.VMEM((rows, HD), jnp.float32)],
        compiler_params=pltpu.CompilerParams(vmem_limit_bytes=VMEM_LIMIT),
        name="attend_back",
    )(qkv, grads)


def normalize(values):
    average = jnp.mean(values, axis=-1, keepdims=True)
    centered = values - average
    variance = jnp.mean(centered * centered, axis=-1, keepdims=True)
    scale = lax.rsqrt(variance + EPS)
    return centered * scale, scale


def normalize_back(grad_normed, gain, unit, scale):
    inner = grad_normed * gain
    return scale * (
        inner
        - jnp.mean(inner, axis=-1, keepdims=True)
        - unit * jnp.mean(inner * unit, axis=-1, keepdims=True)
    )


def split_body(
    tokens,
    ln1_gain,
    ln1_bias,
    w_qkv,
    b_qv,
    w_proj,
    b_proj,
    ln2_gain,
    ln2_bias,
    w_fc,
    b_fc,
    w_out,
    b_out,
    cotangent,
):
    f32, bf16 = jnp.float32, jnp.bfloat16
    count_seq, group_len, model_width = tokens.shape
    rows_total = count_seq * group_len
    dp_bits, ctx_bits = axis_bits("dp"), axis_bits("ctx")
    bits = dp_bits + ctx_bits
    near, high_bits = dp_bits[-1], dp_bits[:-1]
    far, team_bits = ctx_bits[0], ctx_bits[1:]
    ctx_size, dp_size = lax.axis_size("ctx"), lax.axis_size("dp")
    devices = ctx_size * dp_size
    team = 1 << len(team_bits)
    heads = H // team
    wide = heads * HD
    sequence = bit_value(far)
    member = lax.axis_index("ctx") % team
    core = bit_value(near)
    own_rows = w_qkv.shape[0]
    link_bits = high_bits + ctx_bits
    team_dims, link_dims, all_dims = (2,) * len(team_bits), (2,) * len(link_bits), (2,) * len(bits)

    mine = take(tokens, sequence, 0)
    theirs = swap(take(tokens, 1 - sequence, 0), far)
    pair = in_order(mine, theirs, far, 0)
    sides = [
        gather_bits(part, order, team_bits, [])
        for part, order in ((pair[0], team_bits), (pair[1], team_bits[::-1]))
    ]
    long_tokens = jnp.stack(sides).reshape(ctx_size * group_len, model_width)

    vectors = (ln1_gain, ln1_bias, b_qv, b_proj, ln2_gain, ln2_bias, b_fc, b_out)
    sizes = [vector.shape[0] for vector in vectors]
    riders = stack_rows(vectors, 3 * wide).astype(bf16)
    columns = w_qkv.reshape(own_rows, 3, team, wide).transpose(2, 0, 1, 3)
    columns = columns.reshape(team, own_rows, 3 * wide)
    columns = jnp.concatenate(
        [columns, jnp.broadcast_to(riders, (team,) + riders.shape)], axis=1
    ).reshape(team_dims + (own_rows + len(vectors), 3 * wide))
    columns = row_major(columns)
    for k in reversed(range(len(team_bits))):
        columns = trade_bit(columns, team_bits[k], k)
    columns = gather_bits(columns, [far] + dp_bits[::-1], bits, team_bits)
    columns = row_major(columns.reshape(devices, own_rows + len(vectors), 3 * wide))
    qkv_weight = columns[:, :own_rows].reshape(devices * own_rows, 3 * wide)
    (gain_one, bias_one, qv_bias, proj_bias, gain_two, bias_two, fc_bias, out_bias) = (
        columns[:, own_rows + k, :size].reshape(devices * size).astype(f32)
        for k, size in enumerate(sizes)
    )

    hidden_part = w_fc.shape[1] // dp_size
    hidden = w_fc.shape[1] // 2
    fc_sides = w_fc.reshape(own_rows, dp_size // 2, 2, hidden_part).transpose(2, 0, 1, 3)
    fc_sides = fc_sides.reshape(2, own_rows, hidden)
    proj_both = jnp.broadcast_to(w_proj, (2,) + w_proj.shape)
    cut, proj_cut = hidden // 2, model_width // 2
    first = jnp.concatenate(
        [fc_sides[..., :cut], proj_both[..., :proj_cut], fc_sides[..., cut:], proj_both[..., proj_cut:]],
        axis=2,
    )
    first = trade_bit(first, near, 0)
    whole = cut + proj_cut

    def ordered(turn):
        links = team_bits[::-1] + high_bits
        return links[turn % len(links) :] + links[: turn % len(links)]

    def gather_weight(shard, turn, held):
        order = [far] + ordered(turn)
        early = gather_bits(shard, order[:2], bits, held)
        return gather_bits(after(early, long_tokens), order[2:], bits, held + order[:2])

    left = gather_weight(first[..., :whole], 1, [near]).reshape(devices * own_rows, whole)
    right = gather_weight(first[..., whole:], 2, [near]).reshape(devices * own_rows, whole)
    out_weight = gather_weight(w_out, 0, []).reshape(hidden, model_width)
    fc_weight = jnp.concatenate([left[:, :cut], right[:, :cut]], axis=1)
    proj_weight = jnp.concatenate([left[:, cut:], right[:, cut:]], axis=1)
    fc_bias = take(fc_bias.reshape(dp_size // 2, 2, hidden_part), core, 1).reshape(hidden)

    unit_long, _ = normalize(long_tokens.astype(f32))
    normed_long = (unit_long * gain_one + bias_one).astype(bf16)
    team_bias = take(qv_bias.reshape(2, team, wide), member, 1)
    bias_row = jnp.concatenate([team_bias[0], jnp.zeros((wide,), f32), team_bias[1]])
    qkv = (jnp.dot(normed_long, qkv_weight, preferred_element_type=f32) + bias_row).astype(bf16)
    attended = attend(qkv, heads)

    def to_rows(values):
        parts = lax.all_to_all(
            values.reshape(ctx_size, group_len, wide), "ctx", 0, 0, tiled=True
        )
        parts = parts.reshape(count_seq, team, group_len, wide).transpose(0, 2, 1, 3)
        return parts.reshape(rows_total, model_width)

    def to_heads(values):
        parts = values.reshape(count_seq, group_len, team, wide).transpose(0, 2, 1, 3)
        parts = parts.reshape(ctx_size, group_len, wide)
        return lax.all_to_all(parts, "ctx", 0, 0, tiled=True).reshape(ctx_size * group_len, wide)

    def both_rows(values):
        return gather_bit(values, near, 0).reshape(2 * rows_total, values.shape[1])

    def own_sum(values):
        return scatter_bit(values.reshape(2, rows_total, values.shape[1]), near, 0)

    merged = to_rows(attended)

    grad_top = cotangent.reshape(rows_total, model_width)
    grad_top32 = grad_top.astype(f32)
    grad_both = both_rows(grad_top)
    inputs = tokens.astype(f32).reshape(rows_total, model_width)
    middle_rows = inputs + jnp.dot(merged, proj_weight, preferred_element_type=f32) + proj_bias
    unit_two, scale_two = normalize(middle_rows)
    normed_two = both_rows((unit_two * gain_two + bias_two).astype(bf16))
    pre_act = jnp.dot(normed_two, fc_weight, preferred_element_type=f32) + fc_bias
    activated32, gelu_pull = jax.vjp(gelu_tanh, pre_act)
    activated = activated32.astype(bf16)
    fed = own_sum(jnp.dot(activated, out_weight, preferred_element_type=f32))
    result = (middle_rows + fed + out_bias).astype(bf16).reshape(tokens.shape)

    grad_out_weight = outer_sum(activated, grad_both).astype(bf16)
    grad_out_weight = grad_out_weight.reshape(link_dims + w_out.shape)
    out_chain = Chain(grad_out_weight, ordered(0)[::-1] + [far], link_bits)
    out_chain.step()

    grad_pre = gelu_pull(back_through(grad_both, out_weight))[0].astype(bf16)
    grad_fc_bias = jnp.sum(grad_pre.astype(f32), axis=0)
    grad_fc_weight = outer_sum(normed_two, grad_pre).astype(bf16)
    grad_normed_two = own_sum(back_through(grad_pre, fc_weight))
    grad_gain_two = jnp.sum(grad_normed_two * unit_two, axis=0)
    grad_bias_two = jnp.sum(grad_normed_two, axis=0)
    grad_middle = grad_top32 + normalize_back(grad_normed_two, gain_two, unit_two, scale_two)
    grad_branch = grad_middle.astype(bf16)
    grad_proj_bias = jnp.sum(grad_branch.astype(f32), axis=0)
    grad_proj_weight = outer_sum(merged, grad_branch).astype(bf16)
    halves = [
        jnp.concatenate([grad_fc_weight[:, low : low + cut], grad_proj_weight[:, at : at + proj_cut]], 1)
        for low, at in ((0, 0), (cut, proj_cut))
    ]
    halves = [part.reshape(all_dims + (own_rows, whole)) for part in halves]
    half_chains = [
        Chain(part, ordered(turn)[::-1] + [far], bits) for part, turn in zip(halves, (1, 2))
    ]
    for chain in half_chains:
        chain.step()
    grad_heads = to_heads(back_through(grad_branch, proj_weight).astype(bf16))
    grad_heads, out_chain.values = lax.optimization_barrier((grad_heads, out_chain.values))
    grad_qkv = attend_back(qkv, grad_heads, heads)
    grad_long = back_through(grad_qkv, qkv_weight)
    grad_gain_one = jnp.sum(grad_long * unit_long, axis=0)
    grad_bias_one = jnp.sum(grad_long, axis=0)

    sums = jnp.sum(grad_qkv.astype(f32), axis=0).reshape(3, 1, wide)
    placed = lax.dynamic_update_index_in_dim(
        jnp.zeros((2, team, wide), f32), jnp.concatenate([sums[:1], sums[2:]]), member, 1
    )
    fc_bias_placed = lax.dynamic_update_index_in_dim(
        jnp.zeros((dp_size // 2, 2, hidden_part), f32),
        grad_fc_bias.reshape(dp_size // 2, 1, hidden_part),
        core,
        1,
    )
    totals = (
        grad_gain_one,
        grad_bias_one,
        placed,
        grad_proj_bias,
        grad_gain_two,
        grad_bias_two,
        fc_bias_placed,
        jnp.sum(grad_top32, axis=0),
    )
    spread = jnp.concatenate([total.reshape(devices, -1) for total in totals], axis=1)
    spread = spread.reshape((2,) * len(bits) + (1, -1))

    blocks = grad_long.astype(bf16).reshape((2,) + team_dims + (group_len, model_width))
    side_chains = [
        Chain(blocks[k], order, team_bits) for k, order in enumerate((team_bits, team_bits[::-1]))
    ]
    parts = outer_sum(normed_long, grad_qkv).astype(bf16)
    parts = parts.reshape((2,) * len(bits) + (own_rows, 3 * wide))
    qkv_chain = Chain(parts, [near, far] + high_bits[::-1], bits)
    vector_chain = Chain(spread, [near] + high_bits + ctx_bits, bits)
    for chain in (*side_chains, qkv_chain, out_chain, *half_chains):
        chain.step()
    together(*side_chains, qkv_chain, out_chain, *half_chains, vector_chain)
    for chain in (*side_chains, qkv_chain, out_chain, *half_chains):
        chain.step()
    vector_chain.step(2)
    together(*side_chains, qkv_chain, out_chain, *half_chains, vector_chain)
    for chain in (out_chain, *half_chains, qkv_chain, vector_chain, *side_chains):
        chain.step(len(chain.order))
    grad_out_weight = out_chain.values
    half_ends = [chain.values for chain in half_chains]
    fc_and_proj = jnp.concatenate(half_ends, axis=-1)
    kept, sent = take(fc_and_proj, core, 0), take(fc_and_proj, 1 - core, 0)
    sent = swap(sent, near)
    grad_proj_weight = (kept.astype(f32) + sent.astype(f32)).reshape(own_rows, 2, whole)[..., cut:]
    grad_proj_weight = grad_proj_weight.reshape(w_proj.shape)
    grad_fc_weight = in_order(kept, sent, near, 0).reshape(2, own_rows, 2, whole)[..., :cut]
    grad_fc_weight = grad_fc_weight.reshape(2, own_rows, dp_size // 2, hidden_part)
    grad_fc_weight = grad_fc_weight.transpose(1, 2, 0, 3).reshape(w_fc.shape).astype(f32)

    part = jnp.stack([chain.values for chain in side_chains])
    grad_normed_one = trade_bit(part, far, 0).astype(f32)
    unit_one, scale_one = normalize(tokens.astype(f32))
    grad_input = grad_middle.reshape(tokens.shape) + normalize_back(
        grad_normed_one, gain_one, unit_one, scale_one
    )

    parts = qkv_chain.values
    for k in range(len(team_bits)):
        parts = trade_bit(parts, team_bits[k], k)
    grad_qkv_weight = parts.reshape(team, own_rows, 3, wide).transpose(1, 2, 0, 3)
    grad_qkv_weight = grad_qkv_weight.reshape(w_qkv.shape).astype(f32)
    summed = vector_chain.values[0]
    starts = [sum(sizes[:k]) for k in range(len(sizes))]
    (g_gain_one, g_bias_one, g_qv, g_proj, g_gain_two, g_bias_two, g_fc, g_out) = (
        summed[start : start + size] for start, size in zip(starts, sizes)
    )
    return (
        result,
        grad_input,
        g_gain_one,
        g_bias_one,
        grad_qkv_weight,
        g_qv,
        grad_proj_weight,
        g_proj,
        g_gain_two,
        g_bias_two,
        grad_fc_weight,
        g_fc,
        grad_out_weight.astype(f32),
        g_out,
    )


def body(tokens, *others):
    ctx_size, dp_size = lax.axis_size("ctx"), lax.axis_size("dp")
    powers = ctx_size & (ctx_size - 1) == 0 and dp_size & (dp_size - 1) == 0
    if powers and dp_size > 1 and ctx_size > 2 and tokens.shape[0] == 2 and H % (ctx_size // 2) == 0:
        return split_body(tokens, *others)
    return plain_body(tokens, *others)


def solution(mesh):
    placed = (
        P("dp", "ctx", None),
        P(("dp", "ctx")),
        P(("dp", "ctx")),
        P(("dp", "ctx"), None),
        P(("dp", "ctx")),
        P(("dp", "ctx"), None),
        P(("dp", "ctx")),
        P(("dp", "ctx")),
        P(("dp", "ctx")),
        P(("dp", "ctx"), None),
        P(("dp", "ctx")),
        P(("dp", "ctx"), None),
        P(("dp", "ctx")),
        P("dp", "ctx", None),
    )
    return jax.shard_map(
        body,
        mesh=mesh,
        in_specs=placed,
        out_specs=(
            P("dp", "ctx", None),
            P("dp", "ctx", None),
            P(("dp", "ctx")),
            P(("dp", "ctx")),
            P(("dp", "ctx"), None),
            P(("dp", "ctx")),
            P(("dp", "ctx"), None),
            P(("dp", "ctx")),
            P(("dp", "ctx")),
            P(("dp", "ctx")),
            P(("dp", "ctx"), None),
            P(("dp", "ctx")),
            P(("dp", "ctx"), None),
            P(("dp", "ctx")),
        ),
        check_vma=False,
    )
```

```python
import functools
import math

import jax
import jax.numpy as jnp
from jax import lax
from jax.experimental import pallas as pl
from jax.experimental.layout import Layout, with_layout_constraint
from jax.experimental.pallas import tpu as pltpu
from jax.sharding import PartitionSpec as P

H = 12
HD = 64


EPS = 1e-05
NEG = -1e30


def layer_norm(values, gain_vec, bias_vec):
    average = jnp.mean(values, axis=-1, keepdims=True)
    centered = values - average
    variance = jnp.mean(centered * centered, axis=-1, keepdims=True)
    return centered * lax.rsqrt(variance + EPS) * gain_vec + bias_vec


def gelu_tanh(values):
    return jax.nn.gelu(values, approximate=True)


def outer_sum(left, right):
    return lax.dot_general(
        left, right, (((0,), (0,)), ((), ())), preferred_element_type=jnp.float32
    )


def back_through(grad_rows, weight_mat):
    return lax.dot_general(
        grad_rows, weight_mat, (((1,), (1,)), ((), ())), preferred_element_type=jnp.float32
    )


def split_heads(flat_rows):
    return flat_rows.reshape(flat_rows.shape[0], flat_rows.shape[1], H, HD)


def attend_block(query_rows, key_rows, value_rows, query_pos, key_pos, running):
    factor = 1.0 / math.sqrt(HD)
    scores = (
        jnp.einsum("sqhd,skhd->shqk", query_rows, key_rows, preferred_element_type=jnp.float32)
        * factor
    )
    visible = key_pos[None, :] <= query_pos[:, None]
    scores = jnp.where(visible, scores, NEG)
    run_max, run_sum, run_acc = running
    new_max = jnp.maximum(run_max, jnp.max(scores, axis=-1))
    weights = jnp.where(visible, jnp.exp(scores - new_max[..., None]), 0.0)
    new_sum = jnp.sum(weights, axis=-1)
    added = jnp.einsum(
        "shqk,skhd->shqd",
        weights.astype(jnp.bfloat16),
        value_rows,
        preferred_element_type=jnp.float32,
    )
    return (new_max, new_sum, added)


def attend_grad(
    query_rows, grad_heads, log_total, delta_rows, key_rows, value_rows, query_pos, key_pos
):
    factor = 1.0 / math.sqrt(HD)
    scores = (
        jnp.einsum("sqhd,skhd->shqk", query_rows, key_rows, preferred_element_type=jnp.float32)
        * factor
    )
    visible = key_pos[None, :] <= query_pos[:, None]
    probs = jnp.where(visible, jnp.exp(scores - log_total[..., None]), 0.0)
    grad_values = jnp.einsum(
        "shqk,sqhd->skhd",
        probs.astype(jnp.bfloat16),
        grad_heads,
        preferred_element_type=jnp.float32,
    )
    grad_probs = jnp.einsum(
        "sqhd,skhd->shqk", grad_heads, value_rows, preferred_element_type=jnp.float32
    )
    grad_scores = (probs * (grad_probs - delta_rows[..., None])).astype(jnp.bfloat16)
    grad_query = (
        jnp.einsum("shqk,skhd->sqhd", grad_scores, key_rows, preferred_element_type=jnp.float32)
        * factor
    )
    grad_keys = (
        jnp.einsum("shqk,sqhd->skhd", grad_scores, query_rows, preferred_element_type=jnp.float32)
        * factor
    )
    return (grad_query, grad_keys, grad_values)


def plain_body(
    tokens,
    ln1_gain,
    ln1_bias,
    w_qkv,
    b_qv,
    w_proj,
    b_proj,
    ln2_gain,
    ln2_bias,
    w_fc,
    b_fc,
    w_out,
    b_out,
    cotangent,
):
    gathered = (
        lax.all_gather(ln1_gain, ("dp", "ctx"), axis=0, tiled=True),
        lax.all_gather(ln1_bias, ("dp", "ctx"), axis=0, tiled=True),
        lax.all_gather(w_qkv, ("dp", "ctx"), axis=0, tiled=True),
        lax.all_gather(b_qv, ("dp", "ctx"), axis=0, tiled=True),
        lax.all_gather(w_proj, ("dp", "ctx"), axis=0, tiled=True),
        lax.all_gather(b_proj, ("dp", "ctx"), axis=0, tiled=True),
        lax.all_gather(ln2_gain, ("dp", "ctx"), axis=0, tiled=True),
        lax.all_gather(ln2_bias, ("dp", "ctx"), axis=0, tiled=True),
        lax.all_gather(w_fc, ("dp", "ctx"), axis=0, tiled=True),
        lax.all_gather(b_fc, ("dp", "ctx"), axis=0, tiled=True),
        lax.all_gather(w_out, ("dp", "ctx"), axis=0, tiled=True),
        lax.all_gather(b_out, ("dp", "ctx"), axis=0, tiled=True),
    )
    (
        gain_one,
        bias_one,
        qkv_weight,
        qkv_bias,
        proj_weight,
        proj_bias,
        gain_two,
        bias_two,
        fc_weight,
        fc_bias,
        out_weight,
        out_bias,
    ) = gathered
    count_seq, group_len, model_width = tokens.shape
    rows_total = count_seq * group_len
    query_pos = lax.axis_index("ctx") * group_len + jnp.arange(group_len, dtype=jnp.int32)
    inputs = tokens.astype(jnp.float32).reshape(rows_total, model_width)
    normed_one, pull_one = jax.vjp(
        layer_norm, inputs, gain_one.astype(jnp.float32), bias_one.astype(jnp.float32)
    )
    normed_low = normed_one.astype(jnp.bfloat16)
    qkv_bias32 = qkv_bias.astype(jnp.float32)
    bias_full = jnp.concatenate(
        [qkv_bias32[:model_width], jnp.zeros((model_width,), jnp.float32), qkv_bias32[model_width:]]
    )
    qkv_low = (
        jnp.dot(normed_low, qkv_weight, preferred_element_type=jnp.float32) + bias_full
    ).astype(jnp.bfloat16)
    query_flat = qkv_low[:, :model_width].reshape(count_seq, group_len, model_width)
    query_rows = split_heads(query_flat)
    key_value = qkv_low[:, model_width:].reshape(count_seq, group_len, 2 * model_width)
    initial = (
        jnp.full((count_seq, H, group_len), NEG, jnp.float32),
        jnp.zeros((count_seq, H, group_len), jnp.float32),
        jnp.zeros((count_seq, H, group_len, HD), jnp.float32),
    )
    remote = lax.all_gather(key_value, "ctx", axis=1, tiled=True)
    rows_here = remote.shape[1]
    key_pos = jnp.arange(rows_here, dtype=jnp.int32)
    key_rows = split_heads(remote[:, :, :model_width])
    value_rows = split_heads(remote[:, :, model_width:])
    run_max, run_sum, run_acc = attend_block(
        query_rows, key_rows, value_rows, query_pos, key_pos, initial
    )
    attended = run_acc / run_sum[..., None]
    log_total = run_max + jnp.log(run_sum)
    merged_low = (
        attended.transpose(0, 2, 1, 3).reshape(rows_total, model_width).astype(jnp.bfloat16)
    )
    middle = (
        inputs
        + jnp.dot(merged_low, proj_weight, preferred_element_type=jnp.float32)
        + proj_bias.astype(jnp.float32)
    )
    normed_two, pull_two = jax.vjp(
        layer_norm, middle, gain_two.astype(jnp.float32), bias_two.astype(jnp.float32)
    )
    normed_two_low = normed_two.astype(jnp.bfloat16)
    pre_act = jnp.dot(
        normed_two_low, fc_weight, preferred_element_type=jnp.float32
    ) + fc_bias.astype(jnp.float32)
    activated, gelu_pull = jax.vjp(gelu_tanh, pre_act)
    activated_low = activated.astype(jnp.bfloat16)
    feed_out = jnp.dot(
        activated_low, out_weight, preferred_element_type=jnp.float32
    ) + out_bias.astype(jnp.float32)
    result = (middle + feed_out).astype(jnp.bfloat16).reshape(count_seq, group_len, model_width)
    regathered = (
        lax.all_gather(ln1_gain, ("dp", "ctx"), axis=0, tiled=True),
        lax.all_gather(ln1_bias, ("dp", "ctx"), axis=0, tiled=True),
        lax.all_gather(w_qkv, ("dp", "ctx"), axis=0, tiled=True),
        lax.all_gather(b_qv, ("dp", "ctx"), axis=0, tiled=True),
        lax.all_gather(w_proj, ("dp", "ctx"), axis=0, tiled=True),
        lax.all_gather(b_proj, ("dp", "ctx"), axis=0, tiled=True),
        lax.all_gather(ln2_gain, ("dp", "ctx"), axis=0, tiled=True),
        lax.all_gather(ln2_bias, ("dp", "ctx"), axis=0, tiled=True),
        lax.all_gather(w_fc, ("dp", "ctx"), axis=0, tiled=True),
        lax.all_gather(b_fc, ("dp", "ctx"), axis=0, tiled=True),
        lax.all_gather(w_out, ("dp", "ctx"), axis=0, tiled=True),
        lax.all_gather(b_out, ("dp", "ctx"), axis=0, tiled=True),
    )
    qkv_weight = regathered[2]
    proj_weight = regathered[4]
    fc_weight = regathered[8]
    out_weight = regathered[10]
    grad_top = cotangent.reshape(rows_total, model_width)
    grad_top32 = grad_top.astype(jnp.float32)
    grad_out_bias = jnp.sum(grad_top32, axis=0)
    grad_out_weight = outer_sum(activated_low, grad_top)
    grad_act = back_through(grad_top, out_weight)
    grad_pre = gelu_pull(grad_act)[0].astype(jnp.bfloat16)
    grad_fc_bias = jnp.sum(grad_pre.astype(jnp.float32), axis=0)
    grad_fc_weight = outer_sum(normed_two_low, grad_pre)
    grad_normed_two = back_through(grad_pre, fc_weight)
    grad_middle_ln, grad_gain_two, grad_bias_two = pull_two(grad_normed_two)
    grad_middle = grad_top32 + grad_middle_ln
    grad_branch = grad_middle.astype(jnp.bfloat16)
    grad_proj_bias = jnp.sum(grad_branch.astype(jnp.float32), axis=0)
    grad_proj_weight = outer_sum(merged_low, grad_branch)
    grad_merged = back_through(grad_branch, proj_weight).astype(jnp.bfloat16)
    grad_flat = grad_merged.reshape(count_seq, group_len, model_width)
    grad_heads = split_heads(grad_flat)
    delta_rows = jnp.einsum("sqhd,shqd->shq", grad_heads.astype(jnp.float32), attended)
    remote = lax.all_gather(key_value, "ctx", axis=1, tiled=True)
    rows_here = remote.shape[1]
    key_pos = jnp.arange(rows_here, dtype=jnp.int32)
    part_query, part_keys, part_values = attend_grad(
        query_rows,
        grad_heads,
        log_total,
        delta_rows,
        split_heads(remote[:, :, :model_width]),
        split_heads(remote[:, :, model_width:]),
        query_pos,
        key_pos,
    )
    joined = jnp.concatenate(
        [
            part_keys.reshape(count_seq, rows_here, model_width),
            part_values.reshape(count_seq, rows_here, model_width),
        ],
        axis=2,
    )
    grad_kv_all = joined
    grad_query, grad_kv_all = (part_query, grad_kv_all)
    grad_kv = lax.psum_scatter(
        grad_kv_all.astype(jnp.bfloat16), "ctx", scatter_dimension=1, tiled=True
    ).astype(jnp.float32)
    grad_query_flat = grad_query.reshape(count_seq, group_len, model_width)
    grad_qkv = jnp.concatenate(
        [
            grad_query_flat.reshape(rows_total, model_width),
            grad_kv.reshape(rows_total, 2 * model_width),
        ],
        axis=1,
    ).astype(jnp.bfloat16)
    column_sums = jnp.sum(grad_qkv.astype(jnp.float32), axis=0)
    grad_qkv_bias = jnp.concatenate([column_sums[:model_width], column_sums[2 * model_width :]])
    grad_qkv_weight = outer_sum(normed_low, grad_qkv)
    grad_normed_one = back_through(grad_qkv, qkv_weight)
    grad_input_ln, grad_gain_one, grad_bias_one = pull_one(grad_normed_one)
    grad_input = (grad_middle + grad_input_ln).reshape(count_seq, group_len, model_width)
    gradients = (
        lax.psum_scatter(grad_gain_one, ("dp", "ctx"), scatter_dimension=0, tiled=True),
        lax.psum_scatter(grad_bias_one, ("dp", "ctx"), scatter_dimension=0, tiled=True),
        lax.psum_scatter(grad_qkv_weight, ("dp", "ctx"), scatter_dimension=0, tiled=True),
        lax.psum_scatter(grad_qkv_bias, ("dp", "ctx"), scatter_dimension=0, tiled=True),
        lax.psum_scatter(grad_proj_weight, ("dp", "ctx"), scatter_dimension=0, tiled=True),
        lax.psum_scatter(grad_proj_bias, ("dp", "ctx"), scatter_dimension=0, tiled=True),
        lax.psum_scatter(grad_gain_two, ("dp", "ctx"), scatter_dimension=0, tiled=True),
        lax.psum_scatter(grad_bias_two, ("dp", "ctx"), scatter_dimension=0, tiled=True),
        lax.psum_scatter(grad_fc_weight, ("dp", "ctx"), scatter_dimension=0, tiled=True),
        lax.psum_scatter(grad_fc_bias, ("dp", "ctx"), scatter_dimension=0, tiled=True),
        lax.psum_scatter(grad_out_weight, ("dp", "ctx"), scatter_dimension=0, tiled=True),
        lax.psum_scatter(grad_out_bias, ("dp", "ctx"), scatter_dimension=0, tiled=True),
    )
    return (result, grad_input) + tuple(gradients)


def axis_bits(axis):
    size = lax.axis_size(axis)
    return [(axis, 1 << k) for k in reversed(range(size.bit_length() - 1))]


def swap(values, bit):
    axis, mask = bit
    return lax.ppermute(values, axis, [(i, i ^ mask) for i in range(lax.axis_size(axis))])


def bit_value(bit):
    axis, mask = bit
    return (lax.axis_index(axis) // mask) % 2


def in_order(mine, other, bit, dim):
    place = lax.broadcasted_iota(jnp.int32, (2,) + (1,) * (mine.ndim - dim), 0)
    own = place == bit_value(bit)
    return jnp.where(own, jnp.expand_dims(mine, dim), jnp.expand_dims(other, dim))


def gather_bit(values, bit, dim):
    return in_order(values, swap(values, bit), bit, dim)


def take(values, index, dim):
    return lax.dynamic_index_in_dim(values, index, dim, keepdims=False)


def scatter_bit(values, bit, dim):
    here = bit_value(bit)
    sent = swap(take(values, 1 - here, dim), bit)
    kept = take(values, here, dim).astype(jnp.float32)
    return (kept + sent.astype(jnp.float32)).astype(values.dtype)


def trade_bit(values, bit, dim):
    here = bit_value(bit)
    return in_order(take(values, here, dim), swap(take(values, 1 - here, dim), bit), bit, dim)


def gather_bits(values, order, bits, held):
    held = list(held)
    for bit in order:
        held = sorted(held + [bit], key=bits.index)
        values = gather_bit(values, bit, held.index(bit))
    return values


def scatter_bits(values, order, bits):
    left = list(bits)
    for bit in order:
        values = scatter_bit(values, bit, left.index(bit))
        left.remove(bit)
    return values


def stack_rows(vectors, width):
    count = len(vectors)
    rows = [
        lax.pad(
            vector.astype(jnp.float32).reshape(1, -1),
            jnp.float32(0),
            ((k, count - 1 - k, 0), (0, width - vector.shape[0], 0)),
        )
        for k, vector in enumerate(vectors)
    ]
    return functools.reduce(jnp.add, rows)


class Chain:
    def __init__(self, values, order, bits):
        self.values, self.order, self.bits = values, list(order), list(bits)

    def step(self, count=1):
        for _ in range(count):
            bit = self.order.pop(0)
            self.values = scatter_bit(self.values, bit, self.bits.index(bit))
            self.bits.remove(bit)


def together(*chains):
    for chain, values in zip(chains, lax.optimization_barrier([chain.values for chain in chains])):
        chain.values = values


def row_major(values):
    return with_layout_constraint(values, Layout(major_to_minor=tuple(range(values.ndim))))


def after(values, *others):
    return lax.optimization_barrier((values,) + others)[0]


def dot_last(left, right):
    return lax.dot_general(left, right, (((1,), (1,)), ((), ())), preferred_element_type=jnp.float32)


def dot_first(left, right):
    return lax.dot_general(left, right, (((0,), (0,)), ((), ())), preferred_element_type=jnp.float32)


def seen_scores(keys, queries, start):
    scores = dot_last(keys, queries)
    key_pos = lax.broadcasted_iota(jnp.int32, scores.shape, 0)
    query_pos = lax.broadcasted_iota(jnp.int32, scores.shape, 1) + start
    return jnp.where(key_pos <= query_pos, scores, NEG)


def attend_kernel(heads, block, qkv_ref, out_ref):
    wide = heads * HD
    for head in range(heads):
        at = head * HD
        for low in range(0, qkv_ref.shape[0], block):
            high = low + block
            queries = qkv_ref[low:high, at : at + HD] * (1.0 / math.sqrt(HD))
            keys = qkv_ref[:high, wide + at : wide + at + HD]
            values = qkv_ref[:high, 2 * wide + at : 2 * wide + at + HD]
            scores = seen_scores(keys, queries, low)
            weights = jnp.exp(scores - jnp.max(scores, axis=0, keepdims=True))
            total = jnp.sum(weights, axis=0, keepdims=True)
            mixed = dot_first(values, weights.astype(jnp.bfloat16)) / total
            out_ref[low:high, at : at + HD] = mixed.T.astype(jnp.bfloat16)


def attend_grad_kernel(heads, block, qkv_ref, grad_ref, out_ref, keys_acc, values_acc):
    wide = heads * HD
    factor = 1.0 / math.sqrt(HD)
    for head in range(heads):
        at = head * HD
        keys_acc[...] = jnp.zeros_like(keys_acc)
        values_acc[...] = jnp.zeros_like(values_acc)
        for low in range(0, qkv_ref.shape[0], block):
            high = low + block
            queries = qkv_ref[low:high, at : at + HD] * factor
            keys = qkv_ref[:high, wide + at : wide + at + HD]
            values = qkv_ref[:high, 2 * wide + at : 2 * wide + at + HD]
            grads = grad_ref[low:high, at : at + HD]
            scores = seen_scores(keys, queries, low)
            weights = jnp.exp(scores - jnp.max(scores, axis=0, keepdims=True))
            probs = weights / jnp.sum(weights, axis=0, keepdims=True)
            grad_probs = dot_last(values, grads)
            delta = jnp.sum(probs * grad_probs, axis=0, keepdims=True)
            grad_scores = (probs * (grad_probs - delta)).astype(jnp.bfloat16)
            values_acc[:high] += jnp.dot(
                probs.astype(jnp.bfloat16), grads, preferred_element_type=jnp.float32
            )
            keys_acc[:high] += jnp.dot(grad_scores, queries, preferred_element_type=jnp.float32)
            grad_queries = dot_first(keys, grad_scores) * factor
            out_ref[low:high, at : at + HD] = grad_queries.T.astype(jnp.bfloat16)
        out_ref[:, wide + at : wide + at + HD] = keys_acc[...].astype(jnp.bfloat16)
        out_ref[:, 2 * wide + at : 2 * wide + at + HD] = values_acc[...].astype(jnp.bfloat16)


VMEM_LIMIT = 48 * 1024 * 1024


def attend(qkv, heads):
    rows = qkv.shape[0]
    return pl.pallas_call(
        functools.partial(attend_kernel, heads, min(rows, 256)),
        out_shape=jax.ShapeDtypeStruct((rows, heads * HD), jnp.bfloat16),
        compiler_params=pltpu.CompilerParams(vmem_limit_bytes=VMEM_LIMIT),
        name="attend",
    )(qkv)


def attend_back(qkv, grads, heads):
    rows = qkv.shape[0]
    return pl.pallas_call(
        functools.partial(attend_grad_kernel, heads, min(rows, 256)),
        out_shape=jax.ShapeDtypeStruct(qkv.shape, jnp.bfloat16),
        scratch_shapes=[pltpu.VMEM((rows, HD), jnp.float32), pltpu.VMEM((rows, HD), jnp.float32)],
        compiler_params=pltpu.CompilerParams(vmem_limit_bytes=VMEM_LIMIT),
        name="attend_back",
    )(qkv, grads)


def normalize(values):
    average = jnp.mean(values, axis=-1, keepdims=True)
    centered = values - average
    variance = jnp.mean(centered * centered, axis=-1, keepdims=True)
    scale = lax.rsqrt(variance + EPS)
    return centered * scale, scale


def normalize_back(grad_normed, gain, unit, scale):
    inner = grad_normed * gain
    return scale * (
        inner
        - jnp.mean(inner, axis=-1, keepdims=True)
        - unit * jnp.mean(inner * unit, axis=-1, keepdims=True)
    )


def split_body(
    tokens,
    ln1_gain,
    ln1_bias,
    w_qkv,
    b_qv,
    w_proj,
    b_proj,
    ln2_gain,
    ln2_bias,
    w_fc,
    b_fc,
    w_out,
    b_out,
    cotangent,
):
    f32, bf16 = jnp.float32, jnp.bfloat16
    count_seq, group_len, model_width = tokens.shape
    rows_total = count_seq * group_len
    dp_bits, ctx_bits = axis_bits("dp"), axis_bits("ctx")
    bits = dp_bits + ctx_bits
    near, high_bits = dp_bits[-1], dp_bits[:-1]
    far, team_bits = ctx_bits[0], ctx_bits[1:]
    ctx_size, dp_size = lax.axis_size("ctx"), lax.axis_size("dp")
    devices = ctx_size * dp_size
    team = 1 << len(team_bits)
    heads = H // team
    wide = heads * HD
    sequence = bit_value(far)
    member = lax.axis_index("ctx") % team
    core = bit_value(near)
    own_rows = w_qkv.shape[0]
    link_bits = high_bits + ctx_bits
    team_dims, link_dims, all_dims = (2,) * len(team_bits), (2,) * len(link_bits), (2,) * len(bits)

    mine = take(tokens, sequence, 0)
    theirs = swap(take(tokens, 1 - sequence, 0), far)
    pair = in_order(mine, theirs, far, 0)
    sides = [
        gather_bits(part, order, team_bits, [])
        for part, order in ((pair[0], team_bits), (pair[1], team_bits[::-1]))
    ]
    long_tokens = jnp.stack(sides).reshape(ctx_size * group_len, model_width)

    vectors = (ln1_gain, ln1_bias, b_qv, b_proj, ln2_gain, ln2_bias, b_fc, b_out)
    sizes = [vector.shape[0] for vector in vectors]
    riders = stack_rows(vectors, 3 * wide).astype(bf16)
    columns = w_qkv.reshape(own_rows, 3, team, wide).transpose(2, 0, 1, 3)
    columns = columns.reshape(team, own_rows, 3 * wide)
    columns = jnp.concatenate(
        [columns, jnp.broadcast_to(riders, (team,) + riders.shape)], axis=1
    ).reshape(team_dims + (own_rows + len(vectors), 3 * wide))
    columns = row_major(columns)
    for k in reversed(range(len(team_bits))):
        columns = trade_bit(columns, team_bits[k], k)
    columns = gather_bits(columns, [far] + dp_bits[::-1], bits, team_bits)
    columns = row_major(columns.reshape(devices, own_rows + len(vectors), 3 * wide))
    qkv_weight = columns[:, :own_rows].reshape(devices * own_rows, 3 * wide)
    (gain_one, bias_one, qv_bias, proj_bias, gain_two, bias_two, fc_bias, out_bias) = (
        columns[:, own_rows + k, :size].reshape(devices * size).astype(f32)
        for k, size in enumerate(sizes)
    )

    hidden_part = w_fc.shape[1] // dp_size
    hidden = w_fc.shape[1] // 2
    fc_sides = w_fc.reshape(own_rows, dp_size // 2, 2, hidden_part).transpose(2, 0, 1, 3)
    fc_sides = fc_sides.reshape(2, own_rows, hidden)
    proj_both = jnp.broadcast_to(w_proj, (2,) + w_proj.shape)
    cut, proj_cut = hidden // 2, model_width // 2
    first = jnp.concatenate(
        [fc_sides[..., :cut], proj_both[..., :proj_cut], fc_sides[..., cut:], proj_both[..., proj_cut:]],
        axis=2,
    )
    first = trade_bit(first, near, 0)
    whole = cut + proj_cut

    def ordered(turn):
        links = team_bits[::-1] + high_bits
        return links[turn % len(links) :] + links[: turn % len(links)]

    def gather_weight(shard, turn, held):
        order = [far] + ordered(turn)
        early = gather_bits(shard, order[:2], bits, held)
        return gather_bits(after(early, long_tokens), order[2:], bits, held + order[:2])

    left = gather_weight(first[..., :whole], 1, [near]).reshape(devices * own_rows, whole)
    right = gather_weight(first[..., whole:], 2, [near]).reshape(devices * own_rows, whole)
    order = [far] + ordered(0)
    out_weight = gather_bits(w_out, order[:-1], bits, [])
    long_tokens, out_weight = lax.optimization_barrier((long_tokens, out_weight))
    out_last, out_place = order[-1], sorted(order, key=bits.index).index(order[-1])
    out_other = swap(out_weight, out_last)
    fc_weight = jnp.concatenate([left[:, :cut], right[:, :cut]], axis=1)
    proj_weight = jnp.concatenate([left[:, cut:], right[:, cut:]], axis=1)
    fc_bias = take(fc_bias.reshape(dp_size // 2, 2, hidden_part), core, 1).reshape(hidden)

    unit_long, _ = normalize(long_tokens.astype(f32))
    normed_long = (unit_long * gain_one + bias_one).astype(bf16)
    team_bias = take(qv_bias.reshape(2, team, wide), member, 1)
    bias_row = jnp.concatenate([team_bias[0], jnp.zeros((wide,), f32), team_bias[1]])
    qkv = (jnp.dot(normed_long, qkv_weight, preferred_element_type=f32) + bias_row).astype(bf16)
    attended = attend(qkv, heads)

    def to_rows(values):
        parts = lax.all_to_all(
            values.reshape(ctx_size, group_len, wide), "ctx", 0, 0, tiled=True
        )
        parts = parts.reshape(count_seq, team, group_len, wide).transpose(0, 2, 1, 3)
        return parts.reshape(rows_total, model_width)

    def to_heads(values):
        parts = values.reshape(count_seq, group_len, team, wide).transpose(0, 2, 1, 3)
        parts = parts.reshape(ctx_size, group_len, wide)
        return lax.all_to_all(parts, "ctx", 0, 0, tiled=True).reshape(ctx_size * group_len, wide)

    def both_rows(values):
        return gather_bit(values, near, 0).reshape(2 * rows_total, values.shape[1])

    def own_sum(values):
        return scatter_bit(values.reshape(2, rows_total, values.shape[1]), near, 0)

    merged = to_rows(attended)
    merged, out_other = lax.optimization_barrier((merged, out_other))
    out_weight = in_order(out_weight, out_other, out_last, out_place).reshape(hidden, model_width)

    grad_top = cotangent.reshape(rows_total, model_width)
    grad_top32 = grad_top.astype(f32)
    grad_both = both_rows(grad_top)
    inputs = tokens.astype(f32).reshape(rows_total, model_width)
    middle_rows = inputs + jnp.dot(merged, proj_weight, preferred_element_type=f32) + proj_bias
    unit_two, scale_two = normalize(middle_rows)
    normed_two = both_rows((unit_two * gain_two + bias_two).astype(bf16))
    pre_act = jnp.dot(normed_two, fc_weight, preferred_element_type=f32) + fc_bias
    activated32, gelu_pull = jax.vjp(gelu_tanh, pre_act)
    activated = activated32.astype(bf16)
    fed = own_sum(jnp.dot(activated, out_weight, preferred_element_type=f32))
    result = (middle_rows + fed + out_bias).astype(bf16).reshape(tokens.shape)

    grad_out_weight = outer_sum(activated, grad_both).astype(bf16)
    grad_out_weight = grad_out_weight.reshape(link_dims + w_out.shape)
    out_chain = Chain(grad_out_weight, ordered(0)[::-1] + [far], link_bits)
    out_chain.step()

    grad_pre = gelu_pull(back_through(grad_both, out_weight))[0].astype(bf16)
    grad_fc_bias = jnp.sum(grad_pre.astype(f32), axis=0)
    grad_fc_weight = outer_sum(normed_two, grad_pre).astype(bf16)
    grad_normed_two = own_sum(back_through(grad_pre, fc_weight))
    grad_gain_two = jnp.sum(grad_normed_two * unit_two, axis=0)
    grad_bias_two = jnp.sum(grad_normed_two, axis=0)
    grad_middle = grad_top32 + normalize_back(grad_normed_two, gain_two, unit_two, scale_two)
    grad_branch = grad_middle.astype(bf16)
    grad_proj_bias = jnp.sum(grad_branch.astype(f32), axis=0)
    grad_proj_weight = outer_sum(merged, grad_branch).astype(bf16)
    halves = [
        jnp.concatenate([grad_fc_weight[:, low : low + cut], grad_proj_weight[:, at : at + proj_cut]], 1)
        for low, at in ((0, 0), (cut, proj_cut))
    ]
    halves = [part.reshape(all_dims + (own_rows, whole)) for part in halves]
    half_chains = [
        Chain(part, ordered(turn)[::-1] + [far], bits) for part, turn in zip(halves, (1, 2))
    ]
    for chain in half_chains:
        chain.step()
    grad_heads = to_heads(back_through(grad_branch, proj_weight).astype(bf16))
    grad_heads, out_chain.values = lax.optimization_barrier((grad_heads, out_chain.values))
    grad_qkv = attend_back(qkv, grad_heads, heads)
    grad_long = back_through(grad_qkv, qkv_weight)
    grad_gain_one = jnp.sum(grad_long * unit_long, axis=0)
    grad_bias_one = jnp.sum(grad_long, axis=0)

    sums = jnp.sum(grad_qkv.astype(f32), axis=0).reshape(3, 1, wide)
    placed = lax.dynamic_update_index_in_dim(
        jnp.zeros((2, team, wide), f32), jnp.concatenate([sums[:1], sums[2:]]), member, 1
    )
    fc_bias_placed = lax.dynamic_update_index_in_dim(
        jnp.zeros((dp_size // 2, 2, hidden_part), f32),
        grad_fc_bias.reshape(dp_size // 2, 1, hidden_part),
        core,
        1,
    )
    totals = (
        grad_gain_one,
        grad_bias_one,
        placed,
        grad_proj_bias,
        grad_gain_two,
        grad_bias_two,
        fc_bias_placed,
        jnp.sum(grad_top32, axis=0),
    )
    spread = jnp.concatenate([total.reshape(devices, -1) for total in totals], axis=1)
    spread = jnp.pad(spread, ((0, 0), (0, 3 * wide - spread.shape[1]))).astype(bf16)
    spread = jnp.pad(spread[:, None], ((0, 0), (0, 7), (0, 0)))

    blocks = grad_long.astype(bf16).reshape((2,) + team_dims + (group_len, model_width))
    side_chains = [
        Chain(blocks[k], order, team_bits) for k, order in enumerate((team_bits, team_bits[::-1]))
    ]
    parts = outer_sum(normed_long, grad_qkv).astype(bf16).reshape(devices, own_rows, 3 * wide)
    parts = jnp.concatenate([parts, spread], axis=1)
    parts = parts.reshape((2,) * len(bits) + parts.shape[1:])
    qkv_chain = Chain(parts, [near, far] + high_bits[::-1], bits)
    for chain in (*side_chains, qkv_chain, out_chain, *half_chains):
        chain.step()
    together(*side_chains, qkv_chain, out_chain, *half_chains)
    for chain in (*side_chains, qkv_chain, out_chain, *half_chains):
        chain.step()
    together(*side_chains, qkv_chain, out_chain, *half_chains)
    for chain in (out_chain, *half_chains, qkv_chain, *side_chains):
        chain.step(len(chain.order))
    grad_out_weight = out_chain.values
    half_ends = [chain.values for chain in half_chains]
    fc_and_proj = jnp.concatenate(half_ends, axis=-1)
    kept, sent = take(fc_and_proj, core, 0), take(fc_and_proj, 1 - core, 0)
    sent = swap(sent, near)
    grad_proj_weight = (kept.astype(f32) + sent.astype(f32)).reshape(own_rows, 2, whole)[..., cut:]
    grad_proj_weight = grad_proj_weight.reshape(w_proj.shape)
    grad_fc_weight = in_order(kept, sent, near, 0).reshape(2, own_rows, 2, whole)[..., :cut]
    grad_fc_weight = grad_fc_weight.reshape(2, own_rows, dp_size // 2, hidden_part)
    grad_fc_weight = grad_fc_weight.transpose(1, 2, 0, 3).reshape(w_fc.shape).astype(f32)

    part = jnp.stack([chain.values for chain in side_chains])
    grad_normed_one = trade_bit(part, far, 0).astype(f32)
    unit_one, scale_one = normalize(tokens.astype(f32))
    grad_input = grad_middle.reshape(tokens.shape) + normalize_back(
        grad_normed_one, gain_one, unit_one, scale_one
    )

    parts = qkv_chain.values
    for k in range(len(team_bits)):
        parts = trade_bit(parts, team_bits[k], k)
    parts = parts.reshape((team,) + parts.shape[-2:]).astype(f32)
    grad_qkv_weight = parts[:, :own_rows].reshape(team, own_rows, 3, wide).transpose(1, 2, 0, 3)
    grad_qkv_weight = grad_qkv_weight.reshape(w_qkv.shape)
    summed = jnp.sum(parts[:, own_rows], axis=0)
    starts = [sum(sizes[:k]) for k in range(len(sizes))]
    (g_gain_one, g_bias_one, g_qv, g_proj, g_gain_two, g_bias_two, g_fc, g_out) = (
        summed[start : start + size] for start, size in zip(starts, sizes)
    )
    return (
        result,
        grad_input,
        g_gain_one,
        g_bias_one,
        grad_qkv_weight,
        g_qv,
        grad_proj_weight,
        g_proj,
        g_gain_two,
        g_bias_two,
        grad_fc_weight,
        g_fc,
        grad_out_weight.astype(f32),
        g_out,
    )


def body(tokens, *others):
    ctx_size, dp_size = lax.axis_size("ctx"), lax.axis_size("dp")
    powers = ctx_size & (ctx_size - 1) == 0 and dp_size & (dp_size - 1) == 0
    if powers and dp_size > 1 and ctx_size > 2 and tokens.shape[0] == 2 and H % (ctx_size // 2) == 0:
        return split_body(tokens, *others)
    return plain_body(tokens, *others)


def solution(mesh):
    placed = (
        P("dp", "ctx", None),
        P(("dp", "ctx")),
        P(("dp", "ctx")),
        P(("dp", "ctx"), None),
        P(("dp", "ctx")),
        P(("dp", "ctx"), None),
        P(("dp", "ctx")),
        P(("dp", "ctx")),
        P(("dp", "ctx")),
        P(("dp", "ctx"), None),
        P(("dp", "ctx")),
        P(("dp", "ctx"), None),
        P(("dp", "ctx")),
        P("dp", "ctx", None),
    )
    return jax.shard_map(
        body,
        mesh=mesh,
        in_specs=placed,
        out_specs=(
            P("dp", "ctx", None),
            P("dp", "ctx", None),
            P(("dp", "ctx")),
            P(("dp", "ctx")),
            P(("dp", "ctx"), None),
            P(("dp", "ctx")),
            P(("dp", "ctx"), None),
            P(("dp", "ctx")),
            P(("dp", "ctx")),
            P(("dp", "ctx")),
            P(("dp", "ctx"), None),
            P(("dp", "ctx")),
            P(("dp", "ctx"), None),
            P(("dp", "ctx")),
        ),
        check_vma=False,
    )
```

```python
import functools
import math

import jax
import jax.numpy as jnp
from jax import lax
from jax.experimental import pallas as pl
from jax.experimental.layout import Layout, with_layout_constraint
from jax.experimental.pallas import tpu as pltpu
from jax.sharding import PartitionSpec as P

H = 12
HD = 64


EPS = 1e-05
NEG = -1e30


def layer_norm(values, gain_vec, bias_vec):
    average = jnp.mean(values, axis=-1, keepdims=True)
    centered = values - average
    variance = jnp.mean(centered * centered, axis=-1, keepdims=True)
    return centered * lax.rsqrt(variance + EPS) * gain_vec + bias_vec


def gelu_tanh(values):
    return jax.nn.gelu(values, approximate=True)


def outer_sum(left, right):
    return lax.dot_general(
        left, right, (((0,), (0,)), ((), ())), preferred_element_type=jnp.float32
    )


def back_through(grad_rows, weight_mat):
    return lax.dot_general(
        grad_rows, weight_mat, (((1,), (1,)), ((), ())), preferred_element_type=jnp.float32
    )


def split_heads(flat_rows):
    return flat_rows.reshape(flat_rows.shape[0], flat_rows.shape[1], H, HD)


def attend_block(query_rows, key_rows, value_rows, query_pos, key_pos, running):
    factor = 1.0 / math.sqrt(HD)
    scores = (
        jnp.einsum("sqhd,skhd->shqk", query_rows, key_rows, preferred_element_type=jnp.float32)
        * factor
    )
    visible = key_pos[None, :] <= query_pos[:, None]
    scores = jnp.where(visible, scores, NEG)
    run_max, run_sum, run_acc = running
    new_max = jnp.maximum(run_max, jnp.max(scores, axis=-1))
    weights = jnp.where(visible, jnp.exp(scores - new_max[..., None]), 0.0)
    new_sum = jnp.sum(weights, axis=-1)
    added = jnp.einsum(
        "shqk,skhd->shqd",
        weights.astype(jnp.bfloat16),
        value_rows,
        preferred_element_type=jnp.float32,
    )
    return (new_max, new_sum, added)


def attend_grad(
    query_rows, grad_heads, log_total, delta_rows, key_rows, value_rows, query_pos, key_pos
):
    factor = 1.0 / math.sqrt(HD)
    scores = (
        jnp.einsum("sqhd,skhd->shqk", query_rows, key_rows, preferred_element_type=jnp.float32)
        * factor
    )
    visible = key_pos[None, :] <= query_pos[:, None]
    probs = jnp.where(visible, jnp.exp(scores - log_total[..., None]), 0.0)
    grad_values = jnp.einsum(
        "shqk,sqhd->skhd",
        probs.astype(jnp.bfloat16),
        grad_heads,
        preferred_element_type=jnp.float32,
    )
    grad_probs = jnp.einsum(
        "sqhd,skhd->shqk", grad_heads, value_rows, preferred_element_type=jnp.float32
    )
    grad_scores = (probs * (grad_probs - delta_rows[..., None])).astype(jnp.bfloat16)
    grad_query = (
        jnp.einsum("shqk,skhd->sqhd", grad_scores, key_rows, preferred_element_type=jnp.float32)
        * factor
    )
    grad_keys = (
        jnp.einsum("shqk,sqhd->skhd", grad_scores, query_rows, preferred_element_type=jnp.float32)
        * factor
    )
    return (grad_query, grad_keys, grad_values)


def plain_body(
    tokens,
    ln1_gain,
    ln1_bias,
    w_qkv,
    b_qv,
    w_proj,
    b_proj,
    ln2_gain,
    ln2_bias,
    w_fc,
    b_fc,
    w_out,
    b_out,
    cotangent,
):
    gathered = (
        lax.all_gather(ln1_gain, ("dp", "ctx"), axis=0, tiled=True),
        lax.all_gather(ln1_bias, ("dp", "ctx"), axis=0, tiled=True),
        lax.all_gather(w_qkv, ("dp", "ctx"), axis=0, tiled=True),
        lax.all_gather(b_qv, ("dp", "ctx"), axis=0, tiled=True),
        lax.all_gather(w_proj, ("dp", "ctx"), axis=0, tiled=True),
        lax.all_gather(b_proj, ("dp", "ctx"), axis=0, tiled=True),
        lax.all_gather(ln2_gain, ("dp", "ctx"), axis=0, tiled=True),
        lax.all_gather(ln2_bias, ("dp", "ctx"), axis=0, tiled=True),
        lax.all_gather(w_fc, ("dp", "ctx"), axis=0, tiled=True),
        lax.all_gather(b_fc, ("dp", "ctx"), axis=0, tiled=True),
        lax.all_gather(w_out, ("dp", "ctx"), axis=0, tiled=True),
        lax.all_gather(b_out, ("dp", "ctx"), axis=0, tiled=True),
    )
    (
        gain_one,
        bias_one,
        qkv_weight,
        qkv_bias,
        proj_weight,
        proj_bias,
        gain_two,
        bias_two,
        fc_weight,
        fc_bias,
        out_weight,
        out_bias,
    ) = gathered
    count_seq, group_len, model_width = tokens.shape
    rows_total = count_seq * group_len
    query_pos = lax.axis_index("ctx") * group_len + jnp.arange(group_len, dtype=jnp.int32)
    inputs = tokens.astype(jnp.float32).reshape(rows_total, model_width)
    normed_one, pull_one = jax.vjp(
        layer_norm, inputs, gain_one.astype(jnp.float32), bias_one.astype(jnp.float32)
    )
    normed_low = normed_one.astype(jnp.bfloat16)
    qkv_bias32 = qkv_bias.astype(jnp.float32)
    bias_full = jnp.concatenate(
        [qkv_bias32[:model_width], jnp.zeros((model_width,), jnp.float32), qkv_bias32[model_width:]]
    )
    qkv_low = (
        jnp.dot(normed_low, qkv_weight, preferred_element_type=jnp.float32) + bias_full
    ).astype(jnp.bfloat16)
    query_flat = qkv_low[:, :model_width].reshape(count_seq, group_len, model_width)
    query_rows = split_heads(query_flat)
    key_value = qkv_low[:, model_width:].reshape(count_seq, group_len, 2 * model_width)
    initial = (
        jnp.full((count_seq, H, group_len), NEG, jnp.float32),
        jnp.zeros((count_seq, H, group_len), jnp.float32),
        jnp.zeros((count_seq, H, group_len, HD), jnp.float32),
    )
    remote = lax.all_gather(key_value, "ctx", axis=1, tiled=True)
    rows_here = remote.shape[1]
    key_pos = jnp.arange(rows_here, dtype=jnp.int32)
    key_rows = split_heads(remote[:, :, :model_width])
    value_rows = split_heads(remote[:, :, model_width:])
    run_max, run_sum, run_acc = attend_block(
        query_rows, key_rows, value_rows, query_pos, key_pos, initial
    )
    attended = run_acc / run_sum[..., None]
    log_total = run_max + jnp.log(run_sum)
    merged_low = (
        attended.transpose(0, 2, 1, 3).reshape(rows_total, model_width).astype(jnp.bfloat16)
    )
    middle = (
        inputs
        + jnp.dot(merged_low, proj_weight, preferred_element_type=jnp.float32)
        + proj_bias.astype(jnp.float32)
    )
    normed_two, pull_two = jax.vjp(
        layer_norm, middle, gain_two.astype(jnp.float32), bias_two.astype(jnp.float32)
    )
    normed_two_low = normed_two.astype(jnp.bfloat16)
    pre_act = jnp.dot(
        normed_two_low, fc_weight, preferred_element_type=jnp.float32
    ) + fc_bias.astype(jnp.float32)
    activated, gelu_pull = jax.vjp(gelu_tanh, pre_act)
    activated_low = activated.astype(jnp.bfloat16)
    feed_out = jnp.dot(
        activated_low, out_weight, preferred_element_type=jnp.float32
    ) + out_bias.astype(jnp.float32)
    result = (middle + feed_out).astype(jnp.bfloat16).reshape(count_seq, group_len, model_width)
    regathered = (
        lax.all_gather(ln1_gain, ("dp", "ctx"), axis=0, tiled=True),
        lax.all_gather(ln1_bias, ("dp", "ctx"), axis=0, tiled=True),
        lax.all_gather(w_qkv, ("dp", "ctx"), axis=0, tiled=True),
        lax.all_gather(b_qv, ("dp", "ctx"), axis=0, tiled=True),
        lax.all_gather(w_proj, ("dp", "ctx"), axis=0, tiled=True),
        lax.all_gather(b_proj, ("dp", "ctx"), axis=0, tiled=True),
        lax.all_gather(ln2_gain, ("dp", "ctx"), axis=0, tiled=True),
        lax.all_gather(ln2_bias, ("dp", "ctx"), axis=0, tiled=True),
        lax.all_gather(w_fc, ("dp", "ctx"), axis=0, tiled=True),
        lax.all_gather(b_fc, ("dp", "ctx"), axis=0, tiled=True),
        lax.all_gather(w_out, ("dp", "ctx"), axis=0, tiled=True),
        lax.all_gather(b_out, ("dp", "ctx"), axis=0, tiled=True),
    )
    qkv_weight = regathered[2]
    proj_weight = regathered[4]
    fc_weight = regathered[8]
    out_weight = regathered[10]
    grad_top = cotangent.reshape(rows_total, model_width)
    grad_top32 = grad_top.astype(jnp.float32)
    grad_out_bias = jnp.sum(grad_top32, axis=0)
    grad_out_weight = outer_sum(activated_low, grad_top)
    grad_act = back_through(grad_top, out_weight)
    grad_pre = gelu_pull(grad_act)[0].astype(jnp.bfloat16)
    grad_fc_bias = jnp.sum(grad_pre.astype(jnp.float32), axis=0)
    grad_fc_weight = outer_sum(normed_two_low, grad_pre)
    grad_normed_two = back_through(grad_pre, fc_weight)
    grad_middle_ln, grad_gain_two, grad_bias_two = pull_two(grad_normed_two)
    grad_middle = grad_top32 + grad_middle_ln
    grad_branch = grad_middle.astype(jnp.bfloat16)
    grad_proj_bias = jnp.sum(grad_branch.astype(jnp.float32), axis=0)
    grad_proj_weight = outer_sum(merged_low, grad_branch)
    grad_merged = back_through(grad_branch, proj_weight).astype(jnp.bfloat16)
    grad_flat = grad_merged.reshape(count_seq, group_len, model_width)
    grad_heads = split_heads(grad_flat)
    delta_rows = jnp.einsum("sqhd,shqd->shq", grad_heads.astype(jnp.float32), attended)
    remote = lax.all_gather(key_value, "ctx", axis=1, tiled=True)
    rows_here = remote.shape[1]
    key_pos = jnp.arange(rows_here, dtype=jnp.int32)
    part_query, part_keys, part_values = attend_grad(
        query_rows,
        grad_heads,
        log_total,
        delta_rows,
        split_heads(remote[:, :, :model_width]),
        split_heads(remote[:, :, model_width:]),
        query_pos,
        key_pos,
    )
    joined = jnp.concatenate(
        [
            part_keys.reshape(count_seq, rows_here, model_width),
            part_values.reshape(count_seq, rows_here, model_width),
        ],
        axis=2,
    )
    grad_kv_all = joined
    grad_query, grad_kv_all = (part_query, grad_kv_all)
    grad_kv = lax.psum_scatter(
        grad_kv_all.astype(jnp.bfloat16), "ctx", scatter_dimension=1, tiled=True
    ).astype(jnp.float32)
    grad_query_flat = grad_query.reshape(count_seq, group_len, model_width)
    grad_qkv = jnp.concatenate(
        [
            grad_query_flat.reshape(rows_total, model_width),
            grad_kv.reshape(rows_total, 2 * model_width),
        ],
        axis=1,
    ).astype(jnp.bfloat16)
    column_sums = jnp.sum(grad_qkv.astype(jnp.float32), axis=0)
    grad_qkv_bias = jnp.concatenate([column_sums[:model_width], column_sums[2 * model_width :]])
    grad_qkv_weight = outer_sum(normed_low, grad_qkv)
    grad_normed_one = back_through(grad_qkv, qkv_weight)
    grad_input_ln, grad_gain_one, grad_bias_one = pull_one(grad_normed_one)
    grad_input = (grad_middle + grad_input_ln).reshape(count_seq, group_len, model_width)
    gradients = (
        lax.psum_scatter(grad_gain_one, ("dp", "ctx"), scatter_dimension=0, tiled=True),
        lax.psum_scatter(grad_bias_one, ("dp", "ctx"), scatter_dimension=0, tiled=True),
        lax.psum_scatter(grad_qkv_weight, ("dp", "ctx"), scatter_dimension=0, tiled=True),
        lax.psum_scatter(grad_qkv_bias, ("dp", "ctx"), scatter_dimension=0, tiled=True),
        lax.psum_scatter(grad_proj_weight, ("dp", "ctx"), scatter_dimension=0, tiled=True),
        lax.psum_scatter(grad_proj_bias, ("dp", "ctx"), scatter_dimension=0, tiled=True),
        lax.psum_scatter(grad_gain_two, ("dp", "ctx"), scatter_dimension=0, tiled=True),
        lax.psum_scatter(grad_bias_two, ("dp", "ctx"), scatter_dimension=0, tiled=True),
        lax.psum_scatter(grad_fc_weight, ("dp", "ctx"), scatter_dimension=0, tiled=True),
        lax.psum_scatter(grad_fc_bias, ("dp", "ctx"), scatter_dimension=0, tiled=True),
        lax.psum_scatter(grad_out_weight, ("dp", "ctx"), scatter_dimension=0, tiled=True),
        lax.psum_scatter(grad_out_bias, ("dp", "ctx"), scatter_dimension=0, tiled=True),
    )
    return (result, grad_input) + tuple(gradients)


def axis_bits(axis):
    size = lax.axis_size(axis)
    return [(axis, 1 << k) for k in reversed(range(size.bit_length() - 1))]


def swap(values, bit):
    axis, mask = bit
    return lax.ppermute(values, axis, [(i, i ^ mask) for i in range(lax.axis_size(axis))])


def bit_value(bit):
    axis, mask = bit
    return (lax.axis_index(axis) // mask) % 2


def in_order(mine, other, bit, dim):
    place = lax.broadcasted_iota(jnp.int32, (2,) + (1,) * (mine.ndim - dim), 0)
    own = place == bit_value(bit)
    return jnp.where(own, jnp.expand_dims(mine, dim), jnp.expand_dims(other, dim))


def gather_bit(values, bit, dim):
    return in_order(values, swap(values, bit), bit, dim)


def take(values, index, dim):
    return lax.dynamic_index_in_dim(values, index, dim, keepdims=False)


def scatter_bit(values, bit, dim):
    here = bit_value(bit)
    sent = swap(take(values, 1 - here, dim), bit)
    kept = take(values, here, dim).astype(jnp.float32)
    return (kept + sent.astype(jnp.float32)).astype(values.dtype)


def trade_bit(values, bit, dim):
    here = bit_value(bit)
    return in_order(take(values, here, dim), swap(take(values, 1 - here, dim), bit), bit, dim)


def gather_bits(values, order, bits, held):
    held = list(held)
    for bit in order:
        held = sorted(held + [bit], key=bits.index)
        values = gather_bit(values, bit, held.index(bit))
    return values


def scatter_bits(values, order, bits):
    left = list(bits)
    for bit in order:
        values = scatter_bit(values, bit, left.index(bit))
        left.remove(bit)
    return values


def stack_rows(vectors, width):
    count = len(vectors)
    rows = [
        lax.pad(
            vector.astype(jnp.float32).reshape(1, -1),
            jnp.float32(0),
            ((k, count - 1 - k, 0), (0, width - vector.shape[0], 0)),
        )
        for k, vector in enumerate(vectors)
    ]
    return functools.reduce(jnp.add, rows)


class Chain:
    def __init__(self, values, order, bits):
        self.values, self.order, self.bits = values, list(order), list(bits)

    def step(self, count=1):
        for _ in range(count):
            bit = self.order.pop(0)
            self.values = scatter_bit(self.values, bit, self.bits.index(bit))
            self.bits.remove(bit)


def together(*chains):
    for chain, values in zip(chains, lax.optimization_barrier([chain.values for chain in chains])):
        chain.values = values


def row_major(values):
    return with_layout_constraint(values, Layout(major_to_minor=tuple(range(values.ndim))))


def after(values, *others):
    return lax.optimization_barrier((values,) + others)[0]


def dot_last(left, right):
    return lax.dot_general(left, right, (((1,), (1,)), ((), ())), preferred_element_type=jnp.float32)


def dot_first(left, right):
    return lax.dot_general(left, right, (((0,), (0,)), ((), ())), preferred_element_type=jnp.float32)


def seen_scores(keys, queries, start):
    scores = dot_last(keys, queries)
    key_pos = lax.broadcasted_iota(jnp.int32, scores.shape, 0)
    query_pos = lax.broadcasted_iota(jnp.int32, scores.shape, 1) + start
    return jnp.where(key_pos <= query_pos, scores, NEG)


def attend_kernel(heads, block, qkv_ref, out_ref):
    wide = heads * HD
    for head in range(heads):
        at = head * HD
        for low in range(0, qkv_ref.shape[0], block):
            high = low + block
            queries = qkv_ref[low:high, at : at + HD] * (1.0 / math.sqrt(HD))
            keys = qkv_ref[:high, wide + at : wide + at + HD]
            values = qkv_ref[:high, 2 * wide + at : 2 * wide + at + HD]
            scores = seen_scores(keys, queries, low)
            weights = jnp.exp(scores - jnp.max(scores, axis=0, keepdims=True))
            total = jnp.sum(weights, axis=0, keepdims=True)
            mixed = dot_first(values, weights.astype(jnp.bfloat16)) / total
            out_ref[low:high, at : at + HD] = mixed.T.astype(jnp.bfloat16)


def attend_grad_kernel(heads, block, qkv_ref, grad_ref, out_ref, keys_acc, values_acc):
    wide = heads * HD
    factor = 1.0 / math.sqrt(HD)
    for head in range(heads):
        at = head * HD
        keys_acc[...] = jnp.zeros_like(keys_acc)
        values_acc[...] = jnp.zeros_like(values_acc)
        for low in range(0, qkv_ref.shape[0], block):
            high = low + block
            queries = qkv_ref[low:high, at : at + HD] * factor
            keys = qkv_ref[:high, wide + at : wide + at + HD]
            values = qkv_ref[:high, 2 * wide + at : 2 * wide + at + HD]
            grads = grad_ref[low:high, at : at + HD]
            scores = seen_scores(keys, queries, low)
            weights = jnp.exp(scores - jnp.max(scores, axis=0, keepdims=True))
            probs = weights / jnp.sum(weights, axis=0, keepdims=True)
            grad_probs = dot_last(values, grads)
            delta = jnp.sum(probs * grad_probs, axis=0, keepdims=True)
            grad_scores = (probs * (grad_probs - delta)).astype(jnp.bfloat16)
            values_acc[:high] += jnp.dot(
                probs.astype(jnp.bfloat16), grads, preferred_element_type=jnp.float32
            )
            keys_acc[:high] += jnp.dot(grad_scores, queries, preferred_element_type=jnp.float32)
            grad_queries = dot_first(keys, grad_scores) * factor
            out_ref[low:high, at : at + HD] = grad_queries.T.astype(jnp.bfloat16)
        out_ref[:, wide + at : wide + at + HD] = keys_acc[...].astype(jnp.bfloat16)
        out_ref[:, 2 * wide + at : 2 * wide + at + HD] = values_acc[...].astype(jnp.bfloat16)


VMEM_LIMIT = 48 * 1024 * 1024


def attend(qkv, heads):
    rows = qkv.shape[0]
    return pl.pallas_call(
        functools.partial(attend_kernel, heads, min(rows, 256)),
        out_shape=jax.ShapeDtypeStruct((rows, heads * HD), jnp.bfloat16),
        compiler_params=pltpu.CompilerParams(vmem_limit_bytes=VMEM_LIMIT),
        name="attend",
    )(qkv)


def attend_back(qkv, grads, heads):
    rows = qkv.shape[0]
    return pl.pallas_call(
        functools.partial(attend_grad_kernel, heads, min(rows, 256)),
        out_shape=jax.ShapeDtypeStruct(qkv.shape, jnp.bfloat16),
        scratch_shapes=[pltpu.VMEM((rows, HD), jnp.float32), pltpu.VMEM((rows, HD), jnp.float32)],
        compiler_params=pltpu.CompilerParams(vmem_limit_bytes=VMEM_LIMIT),
        name="attend_back",
    )(qkv, grads)


def normalize(values):
    average = jnp.mean(values, axis=-1, keepdims=True)
    centered = values - average
    variance = jnp.mean(centered * centered, axis=-1, keepdims=True)
    scale = lax.rsqrt(variance + EPS)
    return centered * scale, scale


def normalize_back(grad_normed, gain, unit, scale):
    inner = grad_normed * gain
    return scale * (
        inner
        - jnp.mean(inner, axis=-1, keepdims=True)
        - unit * jnp.mean(inner * unit, axis=-1, keepdims=True)
    )


def split_body(
    tokens,
    ln1_gain,
    ln1_bias,
    w_qkv,
    b_qv,
    w_proj,
    b_proj,
    ln2_gain,
    ln2_bias,
    w_fc,
    b_fc,
    w_out,
    b_out,
    cotangent,
):
    f32, bf16 = jnp.float32, jnp.bfloat16
    count_seq, group_len, model_width = tokens.shape
    rows_total = count_seq * group_len
    dp_bits, ctx_bits = axis_bits("dp"), axis_bits("ctx")
    bits = dp_bits + ctx_bits
    near, high_bits = dp_bits[-1], dp_bits[:-1]
    far, team_bits = ctx_bits[0], ctx_bits[1:]
    ctx_size, dp_size = lax.axis_size("ctx"), lax.axis_size("dp")
    devices = ctx_size * dp_size
    team = 1 << len(team_bits)
    heads = H // team
    wide = heads * HD
    sequence = bit_value(far)
    member = lax.axis_index("ctx") % team
    core = bit_value(near)
    own_rows = w_qkv.shape[0]
    link_bits = high_bits + ctx_bits
    team_dims, link_dims, all_dims = (2,) * len(team_bits), (2,) * len(link_bits), (2,) * len(bits)

    mine = take(tokens, sequence, 0)
    theirs = swap(take(tokens, 1 - sequence, 0), far)
    pair = in_order(mine, theirs, far, 0)
    sides = [
        gather_bits(part, order, team_bits, [])
        for part, order in ((pair[0], team_bits), (pair[1], team_bits[::-1]))
    ]
    long_tokens = jnp.stack(sides).reshape(ctx_size * group_len, model_width)

    vectors = (ln1_gain, ln1_bias, b_qv, b_proj, ln2_gain, ln2_bias, b_fc, b_out)
    sizes = [vector.shape[0] for vector in vectors]
    riders = stack_rows(vectors, 3 * wide).astype(bf16)
    columns = w_qkv.reshape(own_rows, 3, team, wide).transpose(2, 0, 1, 3)
    columns = columns.reshape(team, own_rows, 3 * wide)
    columns = jnp.concatenate(
        [columns, jnp.broadcast_to(riders, (team,) + riders.shape)], axis=1
    ).reshape(team_dims + (own_rows + len(vectors), 3 * wide))
    columns = row_major(columns)
    for k in reversed(range(len(team_bits))):
        columns = trade_bit(columns, team_bits[k], k)
    columns = gather_bits(columns, [far] + dp_bits[::-1], bits, team_bits)
    columns = row_major(columns.reshape(devices, own_rows + len(vectors), 3 * wide))
    qkv_weight = columns[:, :own_rows].reshape(devices * own_rows, 3 * wide)
    (gain_one, bias_one, qv_bias, proj_bias, gain_two, bias_two, fc_bias, out_bias) = (
        columns[:, own_rows + k, :size].reshape(devices * size).astype(f32)
        for k, size in enumerate(sizes)
    )

    hidden_part = w_fc.shape[1] // dp_size
    hidden = w_fc.shape[1] // 2
    fc_sides = w_fc.reshape(own_rows, dp_size // 2, 2, hidden_part).transpose(2, 0, 1, 3)
    fc_sides = fc_sides.reshape(2, own_rows, hidden)
    proj_both = jnp.broadcast_to(w_proj, (2,) + w_proj.shape)
    cut, proj_cut = hidden // 2, model_width // 2
    first = jnp.concatenate(
        [fc_sides[..., :cut], proj_both[..., :proj_cut], fc_sides[..., cut:], proj_both[..., proj_cut:]],
        axis=2,
    )
    first = trade_bit(first, near, 0)
    whole = cut + proj_cut

    def ordered(turn):
        links = team_bits[::-1] + high_bits
        return links[turn % len(links) :] + links[: turn % len(links)]

    def gather_weight(shard, turn, held):
        order = [far] + ordered(turn)
        early = gather_bits(shard, order[:2], bits, held)
        return gather_bits(after(early, long_tokens), order[2:], bits, held + order[:2])

    left = gather_weight(first[..., :whole], 1, [near]).reshape(devices * own_rows, whole)
    right = gather_weight(first[..., whole:], 2, [near]).reshape(devices * own_rows, whole)
    order = [far] + ordered(0)
    out_weight = gather_bits(w_out, order[:-1], bits, [])
    long_tokens, out_weight = lax.optimization_barrier((long_tokens, out_weight))
    out_last, out_place = order[-1], sorted(order, key=bits.index).index(order[-1])
    out_other = swap(out_weight, out_last)
    fc_weight = jnp.concatenate([left[:, :cut], right[:, :cut]], axis=1)
    proj_weight = jnp.concatenate([left[:, cut:], right[:, cut:]], axis=1)
    fc_bias = take(fc_bias.reshape(dp_size // 2, 2, hidden_part), core, 1).reshape(hidden)

    unit_long, _ = normalize(long_tokens.astype(f32))
    normed_long = (unit_long * gain_one + bias_one).astype(bf16)
    team_bias = take(qv_bias.reshape(2, team, wide), member, 1)
    bias_row = jnp.concatenate([team_bias[0], jnp.zeros((wide,), f32), team_bias[1]])
    qkv = (jnp.dot(normed_long, qkv_weight, preferred_element_type=f32) + bias_row).astype(bf16)
    attended = attend(qkv, heads)

    def to_rows(values):
        parts = lax.all_to_all(
            values.reshape(ctx_size, group_len, wide), "ctx", 0, 0, tiled=True
        )
        parts = parts.reshape(count_seq, team, group_len, wide).transpose(0, 2, 1, 3)
        return parts.reshape(rows_total, model_width)

    def to_heads(values):
        parts = values.reshape(count_seq, group_len, team, wide).transpose(0, 2, 1, 3)
        parts = parts.reshape(ctx_size, group_len, wide)
        return lax.all_to_all(parts, "ctx", 0, 0, tiled=True).reshape(ctx_size * group_len, wide)

    def both_rows(values):
        return gather_bit(values, near, 0).reshape(2 * rows_total, values.shape[1])

    def own_sum(values):
        return scatter_bit(values.reshape(2, rows_total, values.shape[1]), near, 0)

    merged = to_rows(attended)
    merged, out_other = lax.optimization_barrier((merged, out_other))
    out_weight = in_order(out_weight, out_other, out_last, out_place).reshape(hidden, model_width)

    grad_top = cotangent.reshape(rows_total, model_width)
    grad_top32 = grad_top.astype(f32)
    grad_both = both_rows(grad_top)
    inputs = tokens.astype(f32).reshape(rows_total, model_width)
    middle_rows = inputs + jnp.dot(merged, proj_weight, preferred_element_type=f32) + proj_bias
    unit_two, scale_two = normalize(middle_rows)
    normed_two = both_rows((unit_two * gain_two + bias_two).astype(bf16))
    pre_act = jnp.dot(normed_two, fc_weight, preferred_element_type=f32) + fc_bias
    activated32, gelu_pull = jax.vjp(gelu_tanh, pre_act)
    activated = activated32.astype(bf16)
    fed = own_sum(jnp.dot(activated, out_weight, preferred_element_type=f32))
    result = (middle_rows + fed + out_bias).astype(bf16).reshape(tokens.shape)

    grad_out_weight = outer_sum(activated, grad_both).astype(bf16)
    grad_out_weight = grad_out_weight.reshape(link_dims + w_out.shape)
    out_chain = Chain(grad_out_weight, ordered(0)[::-1] + [far], link_bits)
    out_chain.step()

    grad_pre = gelu_pull(back_through(grad_both, out_weight))[0].astype(bf16)
    grad_fc_bias = jnp.sum(grad_pre.astype(f32), axis=0)
    grad_fc_weight = outer_sum(normed_two, grad_pre).astype(bf16)
    grad_normed_two = own_sum(back_through(grad_pre, fc_weight))
    grad_gain_two = jnp.sum(grad_normed_two * unit_two, axis=0)
    grad_bias_two = jnp.sum(grad_normed_two, axis=0)
    grad_middle = grad_top32 + normalize_back(grad_normed_two, gain_two, unit_two, scale_two)
    grad_branch = grad_middle.astype(bf16)
    grad_proj_bias = jnp.sum(grad_branch.astype(f32), axis=0)
    grad_proj_weight = outer_sum(merged, grad_branch).astype(bf16)
    halves = [
        jnp.concatenate([grad_fc_weight[:, low : low + cut], grad_proj_weight[:, at : at + proj_cut]], 1)
        for low, at in ((0, 0), (cut, proj_cut))
    ]
    halves = [part.reshape(all_dims + (own_rows, whole)) for part in halves]
    half_chains = [
        Chain(part, ordered(turn)[::-1] + [far], bits) for part, turn in zip(halves, (1, 2))
    ]
    for chain in half_chains:
        chain.step()
    grad_heads = to_heads(back_through(grad_branch, proj_weight).astype(bf16))
    grad_heads, out_chain.values = lax.optimization_barrier((grad_heads, out_chain.values))
    grad_qkv = attend_back(qkv, grad_heads, heads)
    grad_long = back_through(grad_qkv, qkv_weight)
    grad_gain_one = jnp.sum(grad_long * unit_long, axis=0)
    grad_bias_one = jnp.sum(grad_long, axis=0)

    sums = jnp.sum(grad_qkv.astype(f32), axis=0).reshape(3, 1, wide)
    placed = lax.dynamic_update_index_in_dim(
        jnp.zeros((2, team, wide), f32), jnp.concatenate([sums[:1], sums[2:]]), member, 1
    )
    fc_bias_placed = lax.dynamic_update_index_in_dim(
        jnp.zeros((dp_size // 2, 2, hidden_part), f32),
        grad_fc_bias.reshape(dp_size // 2, 1, hidden_part),
        core,
        1,
    )
    totals = (
        grad_gain_one,
        grad_bias_one,
        placed,
        grad_proj_bias,
        grad_gain_two,
        grad_bias_two,
        fc_bias_placed,
        jnp.sum(grad_top32, axis=0),
    )
    spread = jnp.concatenate([total.reshape(devices, -1) for total in totals], axis=1)
    spread = jnp.pad(spread, ((0, 0), (0, 3 * wide - spread.shape[1]))).astype(bf16)
    spread = jnp.pad(spread[:, None], ((0, 0), (0, 7), (0, 0)))

    blocks = grad_long.astype(bf16).reshape((2,) + team_dims + (group_len, model_width))
    side_chains = [
        Chain(blocks[k], order, team_bits) for k, order in enumerate((team_bits, team_bits[::-1]))
    ]
    parts = outer_sum(normed_long, grad_qkv).astype(bf16).reshape(devices, own_rows, 3 * wide)
    parts = jnp.concatenate([parts, spread], axis=1)
    parts = parts.reshape((2,) * len(bits) + parts.shape[1:])
    qkv_chain = Chain(parts, dp_bits[::-1] + [far], bits)
    for chain in (*side_chains, qkv_chain):
        chain.step()
    together(*side_chains, qkv_chain)
    every = (*side_chains, qkv_chain, out_chain, *half_chains)
    for chain in every:
        chain.step()
    together(*every)
    part_chain = Chain(jnp.stack([chain.values for chain in side_chains]), [], [])
    part_chain.values = trade_bit(part_chain.values, far, 0)
    for chain in (qkv_chain, out_chain, *half_chains):
        chain.step()
    together(part_chain, qkv_chain, out_chain, *half_chains)
    for chain in (out_chain, *half_chains, qkv_chain):
        chain.step(len(chain.order))
    grad_out_weight = out_chain.values
    half_ends = [chain.values for chain in half_chains]
    fc_and_proj = jnp.concatenate(half_ends, axis=-1)
    kept, sent = take(fc_and_proj, core, 0), take(fc_and_proj, 1 - core, 0)
    sent = swap(sent, near)
    grad_proj_weight = (kept.astype(f32) + sent.astype(f32)).reshape(own_rows, 2, whole)[..., cut:]
    grad_proj_weight = grad_proj_weight.reshape(w_proj.shape)
    grad_fc_weight = in_order(kept, sent, near, 0).reshape(2, own_rows, 2, whole)[..., :cut]
    grad_fc_weight = grad_fc_weight.reshape(2, own_rows, dp_size // 2, hidden_part)
    grad_fc_weight = grad_fc_weight.transpose(1, 2, 0, 3).reshape(w_fc.shape).astype(f32)

    grad_normed_one = part_chain.values.astype(f32)
    unit_one, scale_one = normalize(tokens.astype(f32))
    grad_input = grad_middle.reshape(tokens.shape) + normalize_back(
        grad_normed_one, gain_one, unit_one, scale_one
    )

    parts = qkv_chain.values
    for k in range(len(team_bits)):
        parts = trade_bit(parts, team_bits[k], k)
    parts = parts.reshape((team,) + parts.shape[-2:]).astype(f32)
    grad_qkv_weight = parts[:, :own_rows].reshape(team, own_rows, 3, wide).transpose(1, 2, 0, 3)
    grad_qkv_weight = grad_qkv_weight.reshape(w_qkv.shape)
    summed = jnp.sum(parts[:, own_rows], axis=0)
    starts = [sum(sizes[:k]) for k in range(len(sizes))]
    (g_gain_one, g_bias_one, g_qv, g_proj, g_gain_two, g_bias_two, g_fc, g_out) = (
        summed[start : start + size] for start, size in zip(starts, sizes)
    )
    return (
        result,
        grad_input,
        g_gain_one,
        g_bias_one,
        grad_qkv_weight,
        g_qv,
        grad_proj_weight,
        g_proj,
        g_gain_two,
        g_bias_two,
        grad_fc_weight,
        g_fc,
        grad_out_weight.astype(f32),
        g_out,
    )


def body(tokens, *others):
    ctx_size, dp_size = lax.axis_size("ctx"), lax.axis_size("dp")
    powers = ctx_size & (ctx_size - 1) == 0 and dp_size & (dp_size - 1) == 0
    if powers and dp_size > 1 and ctx_size > 2 and tokens.shape[0] == 2 and H % (ctx_size // 2) == 0:
        return split_body(tokens, *others)
    return plain_body(tokens, *others)


def solution(mesh):
    placed = (
        P("dp", "ctx", None),
        P(("dp", "ctx")),
        P(("dp", "ctx")),
        P(("dp", "ctx"), None),
        P(("dp", "ctx")),
        P(("dp", "ctx"), None),
        P(("dp", "ctx")),
        P(("dp", "ctx")),
        P(("dp", "ctx")),
        P(("dp", "ctx"), None),
        P(("dp", "ctx")),
        P(("dp", "ctx"), None),
        P(("dp", "ctx")),
        P("dp", "ctx", None),
    )
    return jax.shard_map(
        body,
        mesh=mesh,
        in_specs=placed,
        out_specs=(
            P("dp", "ctx", None),
            P("dp", "ctx", None),
            P(("dp", "ctx")),
            P(("dp", "ctx")),
            P(("dp", "ctx"), None),
            P(("dp", "ctx")),
            P(("dp", "ctx"), None),
            P(("dp", "ctx")),
            P(("dp", "ctx")),
            P(("dp", "ctx")),
            P(("dp", "ctx"), None),
            P(("dp", "ctx")),
            P(("dp", "ctx"), None),
            P(("dp", "ctx")),
        ),
        check_vma=False,
    )
```

```python
import functools
import math

import jax
import jax.numpy as jnp
from jax import lax
from jax.experimental import pallas as pl
from jax.experimental.layout import Layout, with_layout_constraint
from jax.experimental.pallas import tpu as pltpu
from jax.sharding import PartitionSpec as P

H = 12
HD = 64


EPS = 1e-05
NEG = -1e30


def layer_norm(values, gain_vec, bias_vec):
    average = jnp.mean(values, axis=-1, keepdims=True)
    centered = values - average
    variance = jnp.mean(centered * centered, axis=-1, keepdims=True)
    return centered * lax.rsqrt(variance + EPS) * gain_vec + bias_vec


def gelu_tanh(values):
    return jax.nn.gelu(values, approximate=True)


def outer_sum(left, right):
    return lax.dot_general(
        left, right, (((0,), (0,)), ((), ())), preferred_element_type=jnp.float32
    )


def back_through(grad_rows, weight_mat):
    return lax.dot_general(
        grad_rows, weight_mat, (((1,), (1,)), ((), ())), preferred_element_type=jnp.float32
    )


def split_heads(flat_rows):
    return flat_rows.reshape(flat_rows.shape[0], flat_rows.shape[1], H, HD)


def attend_block(query_rows, key_rows, value_rows, query_pos, key_pos, running):
    factor = 1.0 / math.sqrt(HD)
    scores = (
        jnp.einsum("sqhd,skhd->shqk", query_rows, key_rows, preferred_element_type=jnp.float32)
        * factor
    )
    visible = key_pos[None, :] <= query_pos[:, None]
    scores = jnp.where(visible, scores, NEG)
    run_max, run_sum, run_acc = running
    new_max = jnp.maximum(run_max, jnp.max(scores, axis=-1))
    weights = jnp.where(visible, jnp.exp(scores - new_max[..., None]), 0.0)
    new_sum = jnp.sum(weights, axis=-1)
    added = jnp.einsum(
        "shqk,skhd->shqd",
        weights.astype(jnp.bfloat16),
        value_rows,
        preferred_element_type=jnp.float32,
    )
    return (new_max, new_sum, added)


def attend_grad(
    query_rows, grad_heads, log_total, delta_rows, key_rows, value_rows, query_pos, key_pos
):
    factor = 1.0 / math.sqrt(HD)
    scores = (
        jnp.einsum("sqhd,skhd->shqk", query_rows, key_rows, preferred_element_type=jnp.float32)
        * factor
    )
    visible = key_pos[None, :] <= query_pos[:, None]
    probs = jnp.where(visible, jnp.exp(scores - log_total[..., None]), 0.0)
    grad_values = jnp.einsum(
        "shqk,sqhd->skhd",
        probs.astype(jnp.bfloat16),
        grad_heads,
        preferred_element_type=jnp.float32,
    )
    grad_probs = jnp.einsum(
        "sqhd,skhd->shqk", grad_heads, value_rows, preferred_element_type=jnp.float32
    )
    grad_scores = (probs * (grad_probs - delta_rows[..., None])).astype(jnp.bfloat16)
    grad_query = (
        jnp.einsum("shqk,skhd->sqhd", grad_scores, key_rows, preferred_element_type=jnp.float32)
        * factor
    )
    grad_keys = (
        jnp.einsum("shqk,sqhd->skhd", grad_scores, query_rows, preferred_element_type=jnp.float32)
        * factor
    )
    return (grad_query, grad_keys, grad_values)


def plain_body(
    tokens,
    ln1_gain,
    ln1_bias,
    w_qkv,
    b_qv,
    w_proj,
    b_proj,
    ln2_gain,
    ln2_bias,
    w_fc,
    b_fc,
    w_out,
    b_out,
    cotangent,
):
    gathered = (
        lax.all_gather(ln1_gain, ("dp", "ctx"), axis=0, tiled=True),
        lax.all_gather(ln1_bias, ("dp", "ctx"), axis=0, tiled=True),
        lax.all_gather(w_qkv, ("dp", "ctx"), axis=0, tiled=True),
        lax.all_gather(b_qv, ("dp", "ctx"), axis=0, tiled=True),
        lax.all_gather(w_proj, ("dp", "ctx"), axis=0, tiled=True),
        lax.all_gather(b_proj, ("dp", "ctx"), axis=0, tiled=True),
        lax.all_gather(ln2_gain, ("dp", "ctx"), axis=0, tiled=True),
        lax.all_gather(ln2_bias, ("dp", "ctx"), axis=0, tiled=True),
        lax.all_gather(w_fc, ("dp", "ctx"), axis=0, tiled=True),
        lax.all_gather(b_fc, ("dp", "ctx"), axis=0, tiled=True),
        lax.all_gather(w_out, ("dp", "ctx"), axis=0, tiled=True),
        lax.all_gather(b_out, ("dp", "ctx"), axis=0, tiled=True),
    )
    (
        gain_one,
        bias_one,
        qkv_weight,
        qkv_bias,
        proj_weight,
        proj_bias,
        gain_two,
        bias_two,
        fc_weight,
        fc_bias,
        out_weight,
        out_bias,
    ) = gathered
    count_seq, group_len, model_width = tokens.shape
    rows_total = count_seq * group_len
    query_pos = lax.axis_index("ctx") * group_len + jnp.arange(group_len, dtype=jnp.int32)
    inputs = tokens.astype(jnp.float32).reshape(rows_total, model_width)
    normed_one, pull_one = jax.vjp(
        layer_norm, inputs, gain_one.astype(jnp.float32), bias_one.astype(jnp.float32)
    )
    normed_low = normed_one.astype(jnp.bfloat16)
    qkv_bias32 = qkv_bias.astype(jnp.float32)
    bias_full = jnp.concatenate(
        [qkv_bias32[:model_width], jnp.zeros((model_width,), jnp.float32), qkv_bias32[model_width:]]
    )
    qkv_low = (
        jnp.dot(normed_low, qkv_weight, preferred_element_type=jnp.float32) + bias_full
    ).astype(jnp.bfloat16)
    query_flat = qkv_low[:, :model_width].reshape(count_seq, group_len, model_width)
    query_rows = split_heads(query_flat)
    key_value = qkv_low[:, model_width:].reshape(count_seq, group_len, 2 * model_width)
    initial = (
        jnp.full((count_seq, H, group_len), NEG, jnp.float32),
        jnp.zeros((count_seq, H, group_len), jnp.float32),
        jnp.zeros((count_seq, H, group_len, HD), jnp.float32),
    )
    remote = lax.all_gather(key_value, "ctx", axis=1, tiled=True)
    rows_here = remote.shape[1]
    key_pos = jnp.arange(rows_here, dtype=jnp.int32)
    key_rows = split_heads(remote[:, :, :model_width])
    value_rows = split_heads(remote[:, :, model_width:])
    run_max, run_sum, run_acc = attend_block(
        query_rows, key_rows, value_rows, query_pos, key_pos, initial
    )
    attended = run_acc / run_sum[..., None]
    log_total = run_max + jnp.log(run_sum)
    merged_low = (
        attended.transpose(0, 2, 1, 3).reshape(rows_total, model_width).astype(jnp.bfloat16)
    )
    middle = (
        inputs
        + jnp.dot(merged_low, proj_weight, preferred_element_type=jnp.float32)
        + proj_bias.astype(jnp.float32)
    )
    normed_two, pull_two = jax.vjp(
        layer_norm, middle, gain_two.astype(jnp.float32), bias_two.astype(jnp.float32)
    )
    normed_two_low = normed_two.astype(jnp.bfloat16)
    pre_act = jnp.dot(
        normed_two_low, fc_weight, preferred_element_type=jnp.float32
    ) + fc_bias.astype(jnp.float32)
    activated, gelu_pull = jax.vjp(gelu_tanh, pre_act)
    activated_low = activated.astype(jnp.bfloat16)
    feed_out = jnp.dot(
        activated_low, out_weight, preferred_element_type=jnp.float32
    ) + out_bias.astype(jnp.float32)
    result = (middle + feed_out).astype(jnp.bfloat16).reshape(count_seq, group_len, model_width)
    regathered = (
        lax.all_gather(ln1_gain, ("dp", "ctx"), axis=0, tiled=True),
        lax.all_gather(ln1_bias, ("dp", "ctx"), axis=0, tiled=True),
        lax.all_gather(w_qkv, ("dp", "ctx"), axis=0, tiled=True),
        lax.all_gather(b_qv, ("dp", "ctx"), axis=0, tiled=True),
        lax.all_gather(w_proj, ("dp", "ctx"), axis=0, tiled=True),
        lax.all_gather(b_proj, ("dp", "ctx"), axis=0, tiled=True),
        lax.all_gather(ln2_gain, ("dp", "ctx"), axis=0, tiled=True),
        lax.all_gather(ln2_bias, ("dp", "ctx"), axis=0, tiled=True),
        lax.all_gather(w_fc, ("dp", "ctx"), axis=0, tiled=True),
        lax.all_gather(b_fc, ("dp", "ctx"), axis=0, tiled=True),
        lax.all_gather(w_out, ("dp", "ctx"), axis=0, tiled=True),
        lax.all_gather(b_out, ("dp", "ctx"), axis=0, tiled=True),
    )
    qkv_weight = regathered[2]
    proj_weight = regathered[4]
    fc_weight = regathered[8]
    out_weight = regathered[10]
    grad_top = cotangent.reshape(rows_total, model_width)
    grad_top32 = grad_top.astype(jnp.float32)
    grad_out_bias = jnp.sum(grad_top32, axis=0)
    grad_out_weight = outer_sum(activated_low, grad_top)
    grad_act = back_through(grad_top, out_weight)
    grad_pre = gelu_pull(grad_act)[0].astype(jnp.bfloat16)
    grad_fc_bias = jnp.sum(grad_pre.astype(jnp.float32), axis=0)
    grad_fc_weight = outer_sum(normed_two_low, grad_pre)
    grad_normed_two = back_through(grad_pre, fc_weight)
    grad_middle_ln, grad_gain_two, grad_bias_two = pull_two(grad_normed_two)
    grad_middle = grad_top32 + grad_middle_ln
    grad_branch = grad_middle.astype(jnp.bfloat16)
    grad_proj_bias = jnp.sum(grad_branch.astype(jnp.float32), axis=0)
    grad_proj_weight = outer_sum(merged_low, grad_branch)
    grad_merged = back_through(grad_branch, proj_weight).astype(jnp.bfloat16)
    grad_flat = grad_merged.reshape(count_seq, group_len, model_width)
    grad_heads = split_heads(grad_flat)
    delta_rows = jnp.einsum("sqhd,shqd->shq", grad_heads.astype(jnp.float32), attended)
    remote = lax.all_gather(key_value, "ctx", axis=1, tiled=True)
    rows_here = remote.shape[1]
    key_pos = jnp.arange(rows_here, dtype=jnp.int32)
    part_query, part_keys, part_values = attend_grad(
        query_rows,
        grad_heads,
        log_total,
        delta_rows,
        split_heads(remote[:, :, :model_width]),
        split_heads(remote[:, :, model_width:]),
        query_pos,
        key_pos,
    )
    joined = jnp.concatenate(
        [
            part_keys.reshape(count_seq, rows_here, model_width),
            part_values.reshape(count_seq, rows_here, model_width),
        ],
        axis=2,
    )
    grad_kv_all = joined
    grad_query, grad_kv_all = (part_query, grad_kv_all)
    grad_kv = lax.psum_scatter(
        grad_kv_all.astype(jnp.bfloat16), "ctx", scatter_dimension=1, tiled=True
    ).astype(jnp.float32)
    grad_query_flat = grad_query.reshape(count_seq, group_len, model_width)
    grad_qkv = jnp.concatenate(
        [
            grad_query_flat.reshape(rows_total, model_width),
            grad_kv.reshape(rows_total, 2 * model_width),
        ],
        axis=1,
    ).astype(jnp.bfloat16)
    column_sums = jnp.sum(grad_qkv.astype(jnp.float32), axis=0)
    grad_qkv_bias = jnp.concatenate([column_sums[:model_width], column_sums[2 * model_width :]])
    grad_qkv_weight = outer_sum(normed_low, grad_qkv)
    grad_normed_one = back_through(grad_qkv, qkv_weight)
    grad_input_ln, grad_gain_one, grad_bias_one = pull_one(grad_normed_one)
    grad_input = (grad_middle + grad_input_ln).reshape(count_seq, group_len, model_width)
    gradients = (
        lax.psum_scatter(grad_gain_one, ("dp", "ctx"), scatter_dimension=0, tiled=True),
        lax.psum_scatter(grad_bias_one, ("dp", "ctx"), scatter_dimension=0, tiled=True),
        lax.psum_scatter(grad_qkv_weight, ("dp", "ctx"), scatter_dimension=0, tiled=True),
        lax.psum_scatter(grad_qkv_bias, ("dp", "ctx"), scatter_dimension=0, tiled=True),
        lax.psum_scatter(grad_proj_weight, ("dp", "ctx"), scatter_dimension=0, tiled=True),
        lax.psum_scatter(grad_proj_bias, ("dp", "ctx"), scatter_dimension=0, tiled=True),
        lax.psum_scatter(grad_gain_two, ("dp", "ctx"), scatter_dimension=0, tiled=True),
        lax.psum_scatter(grad_bias_two, ("dp", "ctx"), scatter_dimension=0, tiled=True),
        lax.psum_scatter(grad_fc_weight, ("dp", "ctx"), scatter_dimension=0, tiled=True),
        lax.psum_scatter(grad_fc_bias, ("dp", "ctx"), scatter_dimension=0, tiled=True),
        lax.psum_scatter(grad_out_weight, ("dp", "ctx"), scatter_dimension=0, tiled=True),
        lax.psum_scatter(grad_out_bias, ("dp", "ctx"), scatter_dimension=0, tiled=True),
    )
    return (result, grad_input) + tuple(gradients)


def axis_bits(axis):
    size = lax.axis_size(axis)
    return [(axis, 1 << k) for k in reversed(range(size.bit_length() - 1))]


def swap(values, bit):
    axis, mask = bit
    return lax.ppermute(values, axis, [(i, i ^ mask) for i in range(lax.axis_size(axis))])


def bit_value(bit):
    axis, mask = bit
    return (lax.axis_index(axis) // mask) % 2


def in_order(mine, other, bit, dim):
    place = lax.broadcasted_iota(jnp.int32, (2,) + (1,) * (mine.ndim - dim), 0)
    own = place == bit_value(bit)
    return jnp.where(own, jnp.expand_dims(mine, dim), jnp.expand_dims(other, dim))


def gather_bit(values, bit, dim):
    return in_order(values, swap(values, bit), bit, dim)


def take(values, index, dim):
    return lax.dynamic_index_in_dim(values, index, dim, keepdims=False)


def scatter_bit(values, bit, dim):
    here = bit_value(bit)
    sent = swap(take(values, 1 - here, dim), bit)
    kept = take(values, here, dim).astype(jnp.float32)
    return (kept + sent.astype(jnp.float32)).astype(values.dtype)


def trade_bit(values, bit, dim):
    here = bit_value(bit)
    return in_order(take(values, here, dim), swap(take(values, 1 - here, dim), bit), bit, dim)


def gather_bits(values, order, bits, held):
    held = list(held)
    for bit in order:
        held = sorted(held + [bit], key=bits.index)
        values = gather_bit(values, bit, held.index(bit))
    return values


def scatter_bits(values, order, bits):
    left = list(bits)
    for bit in order:
        values = scatter_bit(values, bit, left.index(bit))
        left.remove(bit)
    return values


def stack_rows(vectors, width):
    count = len(vectors)
    rows = [
        lax.pad(
            vector.astype(jnp.float32).reshape(1, -1),
            jnp.float32(0),
            ((k, count - 1 - k, 0), (0, width - vector.shape[0], 0)),
        )
        for k, vector in enumerate(vectors)
    ]
    return functools.reduce(jnp.add, rows)


class Chain:
    def __init__(self, values, order, bits):
        self.values, self.order, self.bits = values, list(order), list(bits)

    def step(self, count=1):
        for _ in range(count):
            bit = self.order.pop(0)
            self.values = scatter_bit(self.values, bit, self.bits.index(bit))
            self.bits.remove(bit)


def together(*chains):
    for chain, values in zip(chains, lax.optimization_barrier([chain.values for chain in chains])):
        chain.values = values


def row_major(values):
    return with_layout_constraint(values, Layout(major_to_minor=tuple(range(values.ndim))))


def after(values, *others):
    return lax.optimization_barrier((values,) + others)[0]


def dot_last(left, right):
    return lax.dot_general(left, right, (((1,), (1,)), ((), ())), preferred_element_type=jnp.float32)


def dot_first(left, right):
    return lax.dot_general(left, right, (((0,), (0,)), ((), ())), preferred_element_type=jnp.float32)


def seen_scores(keys, queries, start):
    scores = dot_last(keys[start:], queries)
    key_pos = lax.broadcasted_iota(jnp.int32, scores.shape, 0)
    query_pos = lax.broadcasted_iota(jnp.int32, scores.shape, 1)
    scores = jnp.where(key_pos <= query_pos, scores, NEG)
    if start:
        scores = jnp.concatenate([dot_last(keys[:start], queries), scores], axis=0)
    return scores


def attend_kernel(heads, block, qkv_ref, out_ref):
    wide = heads * HD
    for head in range(heads):
        at = head * HD
        for low in range(0, qkv_ref.shape[0], block):
            high = low + block
            queries = qkv_ref[low:high, at : at + HD] * (1.0 / math.sqrt(HD))
            keys = qkv_ref[:high, wide + at : wide + at + HD]
            values = qkv_ref[:high, 2 * wide + at : 2 * wide + at + HD]
            scores = seen_scores(keys, queries, low)
            weights = jnp.exp(scores - jnp.max(scores, axis=0, keepdims=True))
            total = jnp.sum(weights, axis=0, keepdims=True)
            mixed = dot_first(values, weights.astype(jnp.bfloat16)) / total
            out_ref[low:high, at : at + HD] = mixed.T.astype(jnp.bfloat16)


def attend_grad_kernel(heads, block, qkv_ref, grad_ref, out_ref, keys_acc, values_acc):
    wide = heads * HD
    factor = 1.0 / math.sqrt(HD)
    for head in range(heads):
        at = head * HD
        keys_acc[...] = jnp.zeros_like(keys_acc)
        values_acc[...] = jnp.zeros_like(values_acc)
        for low in range(0, qkv_ref.shape[0], block):
            high = low + block
            queries = qkv_ref[low:high, at : at + HD] * factor
            keys = qkv_ref[:high, wide + at : wide + at + HD]
            values = qkv_ref[:high, 2 * wide + at : 2 * wide + at + HD]
            grads = grad_ref[low:high, at : at + HD]
            scores = seen_scores(keys, queries, low)
            weights = jnp.exp(scores - jnp.max(scores, axis=0, keepdims=True))
            probs = weights * (1.0 / jnp.sum(weights, axis=0, keepdims=True))
            grad_probs = dot_last(values, grads)
            delta = jnp.sum(probs * grad_probs, axis=0, keepdims=True)
            grad_scores = (probs * (grad_probs - delta)).astype(jnp.bfloat16)
            values_acc[:high] += jnp.dot(
                probs.astype(jnp.bfloat16), grads, preferred_element_type=jnp.float32
            )
            keys_acc[:high] += jnp.dot(grad_scores, queries, preferred_element_type=jnp.float32)
            grad_queries = dot_first(keys, grad_scores) * factor
            out_ref[low:high, at : at + HD] = grad_queries.T.astype(jnp.bfloat16)
        out_ref[:, wide + at : wide + at + HD] = keys_acc[...].astype(jnp.bfloat16)
        out_ref[:, 2 * wide + at : 2 * wide + at + HD] = values_acc[...].astype(jnp.bfloat16)


VMEM_LIMIT = 48 * 1024 * 1024


def attend(qkv, heads):
    rows = qkv.shape[0]
    return pl.pallas_call(
        functools.partial(attend_kernel, heads, min(rows, 256)),
        out_shape=jax.ShapeDtypeStruct((rows, heads * HD), jnp.bfloat16),
        compiler_params=pltpu.CompilerParams(vmem_limit_bytes=VMEM_LIMIT),
        name="attend",
    )(qkv)


def attend_back(qkv, grads, heads):
    rows = qkv.shape[0]
    return pl.pallas_call(
        functools.partial(attend_grad_kernel, heads, min(rows, 256)),
        out_shape=jax.ShapeDtypeStruct(qkv.shape, jnp.bfloat16),
        scratch_shapes=[pltpu.VMEM((rows, HD), jnp.float32), pltpu.VMEM((rows, HD), jnp.float32)],
        compiler_params=pltpu.CompilerParams(vmem_limit_bytes=VMEM_LIMIT),
        name="attend_back",
    )(qkv, grads)


def normalize(values):
    average = jnp.mean(values, axis=-1, keepdims=True)
    centered = values - average
    variance = jnp.mean(centered * centered, axis=-1, keepdims=True)
    scale = lax.rsqrt(variance + EPS)
    return centered * scale, scale


def normalize_back(grad_normed, gain, unit, scale):
    inner = grad_normed * gain
    return scale * (
        inner
        - jnp.mean(inner, axis=-1, keepdims=True)
        - unit * jnp.mean(inner * unit, axis=-1, keepdims=True)
    )


def split_body(
    tokens,
    ln1_gain,
    ln1_bias,
    w_qkv,
    b_qv,
    w_proj,
    b_proj,
    ln2_gain,
    ln2_bias,
    w_fc,
    b_fc,
    w_out,
    b_out,
    cotangent,
):
    f32, bf16 = jnp.float32, jnp.bfloat16
    count_seq, group_len, model_width = tokens.shape
    rows_total = count_seq * group_len
    dp_bits, ctx_bits = axis_bits("dp"), axis_bits("ctx")
    bits = dp_bits + ctx_bits
    near, high_bits = dp_bits[-1], dp_bits[:-1]
    far, team_bits = ctx_bits[0], ctx_bits[1:]
    ctx_size, dp_size = lax.axis_size("ctx"), lax.axis_size("dp")
    devices = ctx_size * dp_size
    team = 1 << len(team_bits)
    heads = H // team
    wide = heads * HD
    sequence = bit_value(far)
    member = lax.axis_index("ctx") % team
    core = bit_value(near)
    own_rows = w_qkv.shape[0]
    link_bits = high_bits + ctx_bits
    team_dims, link_dims, all_dims = (2,) * len(team_bits), (2,) * len(link_bits), (2,) * len(bits)

    mine = take(tokens, sequence, 0)
    theirs = swap(take(tokens, 1 - sequence, 0), far)
    pair = in_order(mine, theirs, far, 0)
    sides = [
        gather_bits(part, order, team_bits, [])
        for part, order in ((pair[0], team_bits), (pair[1], team_bits[::-1]))
    ]
    long_tokens = jnp.stack(sides).reshape(ctx_size * group_len, model_width)

    vectors = (ln1_gain, ln1_bias, b_qv, b_proj, ln2_gain, ln2_bias, b_fc, b_out)
    sizes = [vector.shape[0] for vector in vectors]
    riders = stack_rows(vectors, 3 * wide).astype(bf16)
    columns = w_qkv.reshape(own_rows, 3, team, wide).transpose(2, 0, 1, 3)
    columns = columns.reshape(team, own_rows, 3 * wide)
    columns = jnp.concatenate(
        [columns, jnp.broadcast_to(riders, (team,) + riders.shape)], axis=1
    ).reshape(team_dims + (own_rows + len(vectors), 3 * wide))
    columns = row_major(columns)
    for k in reversed(range(len(team_bits))):
        columns = trade_bit(columns, team_bits[k], k)
    columns = gather_bits(columns, [far] + dp_bits[::-1], bits, team_bits)
    columns = row_major(columns.reshape(devices, own_rows + len(vectors), 3 * wide))
    qkv_weight = columns[:, :own_rows].reshape(devices * own_rows, 3 * wide)
    (gain_one, bias_one, qv_bias, proj_bias, gain_two, bias_two, fc_bias, out_bias) = (
        columns[:, own_rows + k, :size].reshape(devices * size).astype(f32)
        for k, size in enumerate(sizes)
    )

    hidden_part = w_fc.shape[1] // dp_size
    hidden = w_fc.shape[1] // 2
    fc_sides = w_fc.reshape(own_rows, dp_size // 2, 2, hidden_part).transpose(2, 0, 1, 3)
    fc_sides = fc_sides.reshape(2, own_rows, hidden)
    proj_both = jnp.broadcast_to(w_proj, (2,) + w_proj.shape)
    cut, proj_cut = hidden // 2, model_width // 2
    first = jnp.concatenate(
        [fc_sides[..., :cut], proj_both[..., :proj_cut], fc_sides[..., cut:], proj_both[..., proj_cut:]],
        axis=2,
    )
    first = trade_bit(first, near, 0)
    whole = cut + proj_cut

    def ordered(turn):
        links = team_bits[::-1] + high_bits
        return links[turn % len(links) :] + links[: turn % len(links)]

    def gather_weight(shard, turn, held):
        order = [far] + ordered(turn)
        early = gather_bits(shard, order[:2], bits, held)
        return gather_bits(after(early, long_tokens), order[2:], bits, held + order[:2])

    left = gather_weight(first[..., :whole], 1, [near]).reshape(devices * own_rows, whole)
    right = gather_weight(first[..., whole:], 2, [near]).reshape(devices * own_rows, whole)
    order = [far] + ordered(0)
    out_weight = gather_bits(w_out, order[:-1], bits, [])
    long_tokens, out_weight = lax.optimization_barrier((long_tokens, out_weight))
    out_last, out_place = order[-1], sorted(order, key=bits.index).index(order[-1])
    out_other = swap(out_weight, out_last)
    fc_weight = jnp.concatenate([left[:, :cut], right[:, :cut]], axis=1)
    proj_weight = jnp.concatenate([left[:, cut:], right[:, cut:]], axis=1)
    fc_bias = take(fc_bias.reshape(dp_size // 2, 2, hidden_part), core, 1).reshape(hidden)

    unit_long, _ = normalize(long_tokens.astype(f32))
    normed_long = (unit_long * gain_one + bias_one).astype(bf16)
    team_bias = take(qv_bias.reshape(2, team, wide), member, 1)
    bias_row = jnp.concatenate([team_bias[0], jnp.zeros((wide,), f32), team_bias[1]])
    qkv = (jnp.dot(normed_long, qkv_weight, preferred_element_type=f32) + bias_row).astype(bf16)
    attended = attend(qkv, heads)

    def to_rows(values):
        parts = lax.all_to_all(
            values.reshape(ctx_size, group_len, wide), "ctx", 0, 0, tiled=True
        )
        parts = parts.reshape(count_seq, team, group_len, wide).transpose(0, 2, 1, 3)
        return parts.reshape(rows_total, model_width)

    def to_heads(values):
        parts = values.reshape(count_seq, group_len, team, wide).transpose(0, 2, 1, 3)
        parts = parts.reshape(ctx_size, group_len, wide)
        return lax.all_to_all(parts, "ctx", 0, 0, tiled=True).reshape(ctx_size * group_len, wide)

    def both_rows(values):
        return gather_bit(values, near, 0).reshape(2 * rows_total, values.shape[1])

    def own_sum(values):
        return scatter_bit(values.reshape(2, rows_total, values.shape[1]), near, 0)

    merged = to_rows(attended)
    merged, out_other = lax.optimization_barrier((merged, out_other))
    out_weight = in_order(out_weight, out_other, out_last, out_place).reshape(hidden, model_width)

    grad_top = cotangent.reshape(rows_total, model_width)
    grad_top32 = grad_top.astype(f32)
    grad_both = both_rows(grad_top)
    inputs = tokens.astype(f32).reshape(rows_total, model_width)
    middle_rows = inputs + jnp.dot(merged, proj_weight, preferred_element_type=f32) + proj_bias
    unit_two, scale_two = normalize(middle_rows)
    normed_two = both_rows((unit_two * gain_two + bias_two).astype(bf16))
    pre_act = jnp.dot(normed_two, fc_weight, preferred_element_type=f32) + fc_bias
    activated32, gelu_pull = jax.vjp(gelu_tanh, pre_act)
    activated = activated32.astype(bf16)
    fed = own_sum(jnp.dot(activated, out_weight, preferred_element_type=f32))
    result = (middle_rows + fed + out_bias).astype(bf16).reshape(tokens.shape)

    grad_out_weight = outer_sum(activated, grad_both).astype(bf16)
    grad_out_weight = grad_out_weight.reshape(link_dims + w_out.shape)
    out_chain = Chain(grad_out_weight, ordered(0)[::-1] + [far], link_bits)
    out_chain.step()

    grad_pre = gelu_pull(back_through(grad_both, out_weight))[0].astype(bf16)
    grad_fc_bias = jnp.sum(grad_pre.astype(f32), axis=0)
    grad_fc_weight = outer_sum(normed_two, grad_pre).astype(bf16)
    grad_normed_two = own_sum(back_through(grad_pre, fc_weight))
    grad_gain_two = jnp.sum(grad_normed_two * unit_two, axis=0)
    grad_bias_two = jnp.sum(grad_normed_two, axis=0)
    grad_middle = grad_top32 + normalize_back(grad_normed_two, gain_two, unit_two, scale_two)
    grad_branch = grad_middle.astype(bf16)
    grad_proj_bias = jnp.sum(grad_branch.astype(f32), axis=0)
    grad_proj_weight = outer_sum(merged, grad_branch).astype(bf16)
    halves = [
        jnp.concatenate([grad_fc_weight[:, low : low + cut], grad_proj_weight[:, at : at + proj_cut]], 1)
        for low, at in ((0, 0), (cut, proj_cut))
    ]
    halves = [part.reshape(all_dims + (own_rows, whole)) for part in halves]
    half_chains = [
        Chain(part, ordered(turn)[::-1] + [far], bits) for part, turn in zip(halves, (1, 2))
    ]
    for chain in half_chains:
        chain.step()
    grad_heads = to_heads(back_through(grad_branch, proj_weight).astype(bf16))
    grad_heads, out_chain.values = lax.optimization_barrier((grad_heads, out_chain.values))
    grad_qkv = attend_back(qkv, grad_heads, heads)
    grad_long = back_through(grad_qkv, qkv_weight)
    grad_gain_one = jnp.sum(grad_long * unit_long, axis=0)
    grad_bias_one = jnp.sum(grad_long, axis=0)

    sums = jnp.sum(grad_qkv.astype(f32), axis=0).reshape(3, 1, wide)
    placed = lax.dynamic_update_index_in_dim(
        jnp.zeros((2, team, wide), f32), jnp.concatenate([sums[:1], sums[2:]]), member, 1
    )
    fc_bias_placed = lax.dynamic_update_index_in_dim(
        jnp.zeros((dp_size // 2, 2, hidden_part), f32),
        grad_fc_bias.reshape(dp_size // 2, 1, hidden_part),
        core,
        1,
    )
    totals = (
        grad_gain_one,
        grad_bias_one,
        placed,
        grad_proj_bias,
        grad_gain_two,
        grad_bias_two,
        fc_bias_placed,
        jnp.sum(grad_top32, axis=0),
    )
    spread = jnp.concatenate([total.reshape(devices, -1) for total in totals], axis=1)
    spread = jnp.pad(spread, ((0, 0), (0, 3 * wide - spread.shape[1]))).astype(bf16)
    spread = jnp.pad(spread[:, None], ((0, 0), (0, 7), (0, 0)))

    blocks = grad_long.astype(bf16).reshape((2,) + team_dims + (group_len, model_width))
    side_chains = [
        Chain(blocks[k], order, team_bits) for k, order in enumerate((team_bits, team_bits[::-1]))
    ]
    parts = outer_sum(normed_long, grad_qkv).astype(bf16).reshape(devices, own_rows, 3 * wide)
    parts = jnp.concatenate([parts, spread], axis=1)
    parts = parts.reshape((2,) * len(bits) + parts.shape[1:])
    qkv_chain = Chain(parts, dp_bits[::-1] + [far], bits)
    for chain in (*side_chains, qkv_chain):
        chain.step()
    together(*side_chains, qkv_chain)
    every = (*side_chains, qkv_chain, out_chain, *half_chains)
    for chain in every:
        chain.step()
    together(*every)
    part_chain = Chain(jnp.stack([chain.values for chain in side_chains]), [], [])
    part_chain.values = trade_bit(part_chain.values, far, 0)
    for chain in (qkv_chain, out_chain, *half_chains):
        chain.step()
    together(part_chain, qkv_chain, out_chain, *half_chains)
    for chain in (out_chain, *half_chains, qkv_chain):
        chain.step(len(chain.order))
    grad_out_weight = out_chain.values
    half_ends = [chain.values for chain in half_chains]
    fc_and_proj = jnp.concatenate(half_ends, axis=-1)
    kept, sent = take(fc_and_proj, core, 0), take(fc_and_proj, 1 - core, 0)
    sent = swap(sent, near)
    grad_proj_weight = (kept.astype(f32) + sent.astype(f32)).reshape(own_rows, 2, whole)[..., cut:]
    grad_proj_weight = grad_proj_weight.reshape(w_proj.shape)
    grad_fc_weight = in_order(kept, sent, near, 0).reshape(2, own_rows, 2, whole)[..., :cut]
    grad_fc_weight = grad_fc_weight.reshape(2, own_rows, dp_size // 2, hidden_part)
    grad_fc_weight = grad_fc_weight.transpose(1, 2, 0, 3).reshape(w_fc.shape).astype(f32)

    grad_normed_one = part_chain.values.astype(f32)
    unit_one, scale_one = normalize(tokens.astype(f32))
    grad_input = grad_middle.reshape(tokens.shape) + normalize_back(
        grad_normed_one, gain_one, unit_one, scale_one
    )

    parts = qkv_chain.values
    for k in range(len(team_bits)):
        parts = trade_bit(parts, team_bits[k], k)
    parts = parts.reshape((team,) + parts.shape[-2:]).astype(f32)
    grad_qkv_weight = parts[:, :own_rows].reshape(team, own_rows, 3, wide).transpose(1, 2, 0, 3)
    grad_qkv_weight = grad_qkv_weight.reshape(w_qkv.shape)
    summed = jnp.sum(parts[:, own_rows], axis=0)
    starts = [sum(sizes[:k]) for k in range(len(sizes))]
    (g_gain_one, g_bias_one, g_qv, g_proj, g_gain_two, g_bias_two, g_fc, g_out) = (
        summed[start : start + size] for start, size in zip(starts, sizes)
    )
    return (
        result,
        grad_input,
        g_gain_one,
        g_bias_one,
        grad_qkv_weight,
        g_qv,
        grad_proj_weight,
        g_proj,
        g_gain_two,
        g_bias_two,
        grad_fc_weight,
        g_fc,
        grad_out_weight.astype(f32),
        g_out,
    )


def body(tokens, *others):
    ctx_size, dp_size = lax.axis_size("ctx"), lax.axis_size("dp")
    powers = ctx_size & (ctx_size - 1) == 0 and dp_size & (dp_size - 1) == 0
    if powers and dp_size > 1 and ctx_size > 2 and tokens.shape[0] == 2 and H % (ctx_size // 2) == 0:
        return split_body(tokens, *others)
    return plain_body(tokens, *others)


def solution(mesh):
    placed = (
        P("dp", "ctx", None),
        P(("dp", "ctx")),
        P(("dp", "ctx")),
        P(("dp", "ctx"), None),
        P(("dp", "ctx")),
        P(("dp", "ctx"), None),
        P(("dp", "ctx")),
        P(("dp", "ctx")),
        P(("dp", "ctx")),
        P(("dp", "ctx"), None),
        P(("dp", "ctx")),
        P(("dp", "ctx"), None),
        P(("dp", "ctx")),
        P("dp", "ctx", None),
    )
    return jax.shard_map(
        body,
        mesh=mesh,
        in_specs=placed,
        out_specs=(
            P("dp", "ctx", None),
            P("dp", "ctx", None),
            P(("dp", "ctx")),
            P(("dp", "ctx")),
            P(("dp", "ctx"), None),
            P(("dp", "ctx")),
            P(("dp", "ctx"), None),
            P(("dp", "ctx")),
            P(("dp", "ctx")),
            P(("dp", "ctx")),
            P(("dp", "ctx"), None),
            P(("dp", "ctx")),
            P(("dp", "ctx"), None),
            P(("dp", "ctx")),
        ),
        check_vma=False,
    )
```
